128 devices in a mesh: gx: 8 (over y, core), gy: 16 (over z, x).
Axes of the slice: x: 4, y: 4, z: 4, core: 2. Of those that a mesh axis runs over, the one named last changes fastest.
Arguments:
- ensemble: float32 [80, 4, 256, 4096], P(None, None, 'gx', 'gy'), may hold values from -6 to 6
- obs_value: float32 [4, 2048], replicated, may hold values from -6 to 6
- obs_variance: float32 [4, 2048], replicated, may hold values from 0.25 to 2
- obs_owner: int32 [4, 2048], replicated, may hold values from 0 to 127, as said below
- obs_cell: int32 [4, 2048], replicated, may hold values from 0 to 8191
- obs_reach: int32 [4, 2048, 8], replicated, may hold values 0 or 1
- batch_order: int32 [4], replicated, may hold values from 0 to 3, each once
Outputs:
- posterior: float32 [80, 4, 256, 4096], P(None, None, 'gx', 'gy')
- innovation: float32 [4, 2048], replicated
The draws below stay inside these ranges and needn't reach their ends.
Inputs may be any that keep to these rules, and one draw needn't show every extreme that they name: `obs_owner`: tile numbers as in the reference program. In every batch no tile owns more than 64 observations, and some tile owns exactly 64.
All inputs are finite; a program needn't handle non-finite values.
Results may differ from the reference program's by a relative error of at most 0.00017.
Values sent between devices are 32-bit elements; how exact they have to be, the bound alone decides.
No kernel may reach another device: no remote copies, remote signals or barrier semaphores. Data moves between devices by JAX's collectives and lax.ppermute only.
A program may use at most 128 MiB of HBM per device.

```python
import math
import jax
import jax.numpy as jnp
from jax import lax

M = 80
LEV = 4
NB = 4
TX = 32
TY = 256
OWN_CAP = 64
OBS = 2048
NX = 256
NY = 4096
N_GX = 8
N_GY = 16
DEVICES = 128


def draw_obs_owner(key, part):
    key = jax.random.fold_in(key, 11)
    rows_list = []
    for batch in range(NB):
        batch_key = jax.random.fold_in(key, batch)
        first_key, second_key, third_key = jax.random.split(batch_key, 3)
        dense = jax.random.randint(first_key, (), 0, DEVICES).astype(jnp.int32)
        slots = jnp.arange(DEVICES * OWN_CAP, dtype=jnp.int32) // OWN_CAP
        ranking = jax.random.permutation(second_key, DEVICES * OWN_CAP).astype(jnp.int32)
        priority = jnp.where(slots == dense, ranking - DEVICES * OWN_CAP, ranking)
        picked = jnp.argsort(priority)[:OBS]
        chosen = slots[picked]
        shuffle = jax.random.permutation(third_key, OBS)
        rows_list.append(chosen[shuffle])
    return jnp.stack(rows_list).astype(jnp.int32)


def touch_ends(result, key, least, largest):
    extent = result.shape
    index_at = [jax.random.randint(jax.random.fold_in(key, axis), (), 0, extent[axis]) for axis in range(len(extent))]
    result = result.at[tuple(index_at)].set(least)
    longest = extent.index(max(extent))
    index_at[longest] = (index_at[longest] + 1) % extent[longest]
    return result.at[tuple(index_at)].set(largest)


def block_levels(stream_key, extent, cuts, low, top_value):
    level = 1.0
    for position, parts in cuts:
        steps = jax.random.uniform(jax.random.fold_in(jax.random.fold_in(stream_key, 6), position), (parts,), jnp.float32, low / len(cuts), top_value / len(cuts))
        level = level * jnp.repeat(jnp.exp(steps), extent[position] // parts).reshape((-1,) + (1,) * (len(extent) - 1 - position))
    return level


def noise(rng, dims, scale, bound, cuts=(), kind=jnp.bfloat16):
    drawn = jax.random.normal(rng, dims, jnp.float32) * scale
    if len(cuts) > 0:
        drawn = block_levels(rng, dims, cuts, -0.22, 0.18) * drawn
    return jnp.clip(drawn, min=-bound, max=bound).astype(kind)


def setup_inputs(seed: int = 0) -> dict:
    keys = jax.random.split(jax.random.key(seed), 8)
    ensemble = noise(keys[0], (M, LEV, NX, NY), 1.0, 6.0, ((2, 8), (3, 16)), jnp.float32)
    obs_value = noise(keys[1], (NB, OBS), 1.0, 6.0, (), jnp.float32)
    obs_variance = jnp.clip(jnp.exp(jax.random.uniform(keys[2], (NB, OBS), jnp.float32, math.log(0.25), math.log(2.0))), 0.25, 2.0)
    obs_owner = draw_obs_owner(jax.random.fold_in(keys[7], 71), 0)
    obs_cell = touch_ends(jax.random.randint(keys[4], (NB, OBS), 0, TX * TY), jax.random.fold_in(keys[4], 1), 0, (TX * TY) - 1).astype(jnp.int32)
    obs_reach = touch_ends((jax.random.randint(keys[5], (NB, OBS, 8), 0, 3) < 2).astype(jnp.int32), jax.random.fold_in(keys[5], 1), 0, 1)
    batch_order = jax.random.permutation(keys[6], NB).astype(jnp.int32)
    return dict(ensemble=ensemble, obs_value=obs_value, obs_variance=obs_variance, obs_owner=obs_owner, obs_cell=obs_cell, obs_reach=obs_reach, batch_order=batch_order)


EPS = 1e-05
TAPER = (0.25, 0.5, 0.25, 0.5, 1.0, 0.5, 0.25, 0.5, 0.25)

def increments(prior, value, variance):
    members = prior.shape[0]
    center = lax.optimization_barrier(jnp.mean(prior, axis=0))
    deviation = prior - center[None, :]
    spread = lax.optimization_barrier(jnp.sum(deviation * deviation, axis=0)) / (members - 1)
    total = spread + variance
    normed = (value - center) / jnp.sqrt(total)
    shift = (spread / total * (value - center))[None, :] + (jnp.sqrt(variance / total) - 1.0)[None, :] * deviation
    scaled = deviation / ((members - 1) * (spread + EPS))[None, :]
    return (scaled, shift, normed)

def reference(ensemble, obs_value, obs_variance, obs_owner, obs_cell, obs_reach, batch_order):
    state = ensemble
    innovation = jnp.zeros((NB, OBS), jnp.float32)
    tiles = jnp.arange(DEVICES, dtype=jnp.int32)
    for step in range(NB):
        batch = batch_order[step]
        value = obs_value[batch]
        variance = obs_variance[batch]
        owner = obs_owner[batch]
        cell = obs_cell[batch]
        reach = obs_reach[batch].astype(jnp.float32)
        tile_x = owner // N_GY
        tile_y = owner % N_GY
        cell_x = tile_x * TX + cell // TY
        cell_y = tile_y * TY + cell % TY
        prior = state[:, 0, cell_x, cell_y]
        scaled, shift, normed = increments(prior, value, variance)
        innovation = innovation.at[batch].set(normed)
        table = jnp.zeros((OBS, DEVICES), jnp.float32)
        for offset in range(9):
            step_x = offset // 3 - 1
            step_y = offset % 3 - 1
            if offset == 4:
                reached = jnp.ones((OBS,), jnp.float32)
            elif offset < 4:
                reached = reach[:, offset]
            else:
                reached = reach[:, offset - 1]
            target_x = tile_x + step_x
            target_y = tile_y + step_y
            inside = (target_x >= 0) & (target_x < N_GX) & (target_y >= 0) & (target_y < N_GY)
            target = target_x * N_GY + target_y
            weight = jnp.where(inside, TAPER[offset] * reached, 0.0)
            table = table + weight[:, None] * (target[:, None] == tiles[None, :]).astype(jnp.float32)
        gain = jnp.einsum('mj,jt,nj->tmn', scaled, table, shift, precision=lax.Precision.HIGHEST)
        gain = gain.reshape(N_GX, N_GY, M, M)
        center = lax.optimization_barrier(jnp.mean(state, axis=0))
        anomaly = (state - center[None]).reshape(M, LEV, N_GX, TX, N_GY, TY)
        update = jnp.einsum('mlaxby,abmn->nlaxby', anomaly, gain, precision=lax.Precision.HIGHEST)
        state = state + update.reshape(M, LEV, NX, NY)
    return (state, innovation)
```

```python
import functools

import jax
import jax.numpy as jnp
from jax import lax
from jax.experimental import pallas as pl
from jax.experimental.pallas import tpu as pltpu
from jax.sharding import PartitionSpec as P

M = 80
LEV = 4
NB = 4
TX = 32
TY = 256
CAP = 64
OBS = 2048
TILES = 128
EPS = 1e-05
F32 = jnp.float32
BF16 = jnp.bfloat16
HIGH = lax.Precision.HIGHEST

ROW_A = M
ROW_C = M + 1
ROW_W = M + 2
ROWS = 96
TAPER = (0.25, 0.5, 0.25, 0.5, 1.0, 0.5, 0.25, 0.5, 0.25)


def split2(x):
    high = x.astype(BF16)
    return high, (x - high.astype(F32)).astype(BF16)


def split3(x):
    high = x.astype(BF16)
    rest = x - high.astype(F32)
    mid = rest.astype(BF16)
    return high, mid, (rest - mid.astype(F32)).astype(BF16)


def iota(shape, dim):
    return lax.broadcasted_iota(jnp.int32, shape, dim)


def dot(a, b, **kw):
    return jnp.dot(a, b, preferred_element_type=F32, **kw)


def dot_t(a, b, **kw):
    return lax.dot_general(a, b, (((1,), (1,)), ((), ())), preferred_element_type=F32, **kw)


def pack(rows):
    return jnp.concatenate([rows[: ROWS // 2], rows[ROWS // 2 :]], axis=1)


def unpack(packed):
    return jnp.concatenate([packed[:, :CAP], packed[:, CAP:]], axis=0)


def make_payload(prior, meta):
    valid = meta[0:1] > 0.5
    value = meta[1:2]
    variance = jnp.where(valid, meta[2:3], 1.0)
    center = jnp.sum(prior, axis=0, keepdims=True) / M
    deviation = prior - center
    spread = jnp.sum(deviation * deviation, axis=0, keepdims=True) / (M - 1)
    total = spread + variance
    miss = value - center
    normed = jnp.where(valid, miss / jnp.sqrt(total), 0.0)
    a = spread / total * miss
    c = jnp.sqrt(variance / total) - 1.0
    d = jnp.where(valid, 1.0 / ((M - 1) * (spread + EPS)), 0.0)
    rows = [deviation, a, c]
    for i in range(9):
        if i == 4:
            rows.append(d)
        else:
            at = 3 + (i if i < 4 else i - 1)
            rows.append(d * (meta[at : at + 1] * TAPER[i]))
    rows.append(jnp.zeros((ROWS - M - 11, CAP), F32))
    return pack(jnp.concatenate(rows, axis=0)), normed


def init_kernel(order, value, variance, owner, cell, reach, x_hbm, z_out, meta_out, pay_out, nv_out, surface, sem):
    load = pltpu.make_async_copy(x_hbm.at[:, 0], surface, sem)
    load.start()
    my_x = lax.axis_index("gx")
    me = my_x * lax.axis_size("gy") + lax.axis_index("gy")
    flip = lax.rem(my_x, 2) == 1
    owned = jnp.concatenate([owner[pl.ds(order[k], 1), :] for k in range(NB)], axis=0) == me
    ownf = jnp.where(owned, 1.0, 0.0)
    chunks = OBS // 128
    own64 = jnp.concatenate([ownf[:, 128 * c : 128 * c + 128] for c in range(chunks)], axis=0).astype(BF16)
    upper = jnp.where(iota((128, 128), 0) < iota((128, 128), 1), 1.0, 0.0).astype(BF16)
    rows = NB * chunks
    r0, r1 = iota((rows, rows), 0), iota((rows, rows), 1)
    before = jnp.where((r1 < r0) & (((r0 - r1) & (NB - 1)) == 0), 1.0, 0.0).astype(BF16)
    base = dot(dot(before, own64).astype(BF16), jnp.ones((128, 128), BF16))
    rank64 = dot(own64, upper) + base
    rank = jnp.concatenate([rank64[NB * c : NB * c + NB] for c in range(chunks)], axis=1)
    rank = jnp.where(owned, rank, -1.0)
    slots = iota((CAP, OBS), 0).astype(F32)
    metas = []
    for k in range(NB):
        b = order[k]
        hot = jnp.where(rank[k : k + 1] == slots, 1.0, 0.0).astype(BF16)
        where = cell[pl.ds(b, 1), :]
        vh, vm, vl = split3(value[pl.ds(b, 1), :])
        rh, rm, rl = split3(variance[pl.ds(b, 1), :])
        parts = [
            reach[b].astype(F32),
            lax.shift_right_logical(where, 8).astype(F32),
            (where & 255).astype(F32),
            vh.astype(F32), vm.astype(F32), vl.astype(F32),
            rh.astype(F32), rm.astype(F32), rl.astype(F32),
            jnp.ones((1, OBS), F32),
            jnp.zeros((15, OBS), F32),
        ]
        metas.append(dot_t(jnp.concatenate(parts, axis=0).astype(BF16), hot))
    for k in range(NB):
        got = metas[k]
        rows = [got[16:17], got[10:11] + got[11:12] + got[12:13], got[13:14] + got[14:15] + got[15:16]]
        for i in range(8):
            rows.append(jnp.where(flip, got[7 - i : 8 - i], got[i : i + 1]))
        rows.append(jnp.zeros((5, CAP), F32))
        meta_out[k] = jnp.concatenate(rows, axis=0)
    cell_x = jnp.concatenate([g[8:9] for g in metas], axis=1)
    cell_y = jnp.concatenate([g[9:10] for g in metas], axis=1)
    hot_y = jnp.where(cell_y == iota((TY, NB * CAP), 0).astype(F32), 1.0, 0.0).astype(BF16)
    hot_x = jnp.where(cell_x == iota((TX, NB * CAP), 0).astype(F32), 1.0, 0.0)
    load.wait()
    group = 16
    for g in range(M // group):
        h, m, l = split3(surface[group * g : group * g + group].reshape(group * TX, TY))
        picked = dot(h, hot_y) + dot(m, hot_y) + dot(l, hot_y)
        z_out[group * g : group * g + group, : NB * CAP] = jnp.sum(
            picked.reshape(group, TX, NB * CAP) * hot_x[None], axis=1
        )
    z_out[:, NB * CAP :] = jnp.where(iota((M, 128), 0) == iota((M, 128), 1), 1.0, 0.0)
    pay, normed = make_payload(z_out[:, :CAP], meta_out[0])
    pay_out[...] = pay
    nv_out[...] = normed


def right_side(rows):
    return rows[ROW_A : ROW_A + 1] + rows[ROW_C : ROW_C + 1] * rows[:M]


def left_side(rows, direction, side):
    at = ROW_W + 3 * direction + side
    return rows[:M] * rows[at : at + 1]


def gain_of(terms):
    left = jnp.concatenate([left_side(rows, d, s) for rows, _, d, s in terms], axis=1)
    right = jnp.concatenate([r for _, r, _, _ in terms], axis=1)
    return dot_t(right, left, precision=HIGH)


def send_kernel(own, outer, sib, sib_outer, out):
    own, outer, sib, sib_outer = (unpack(r[...]) for r in (own, outer, sib, sib_outer))
    r_own, r_outer, r_sib, r_so = (right_side(r) for r in (own, outer, sib, sib_outer))
    out[0] = gain_of([(own, r_own, 1, 0), (outer, r_outer, 0, 2), (sib, r_sib, 2, 2)])
    out[1] = gain_of([(sib, r_sib, 1, 2), (own, r_own, 2, 0), (sib_outer, r_so, 0, 0)])


def same_kernel(own, outer, sib, out):
    own, outer, sib = (unpack(r[...]) for r in (own, outer, sib))
    r_own, r_outer, r_sib = (right_side(r) for r in (own, outer, sib))
    out[...] = gain_of([(own, r_own, 1, 1), (outer, r_outer, 0, 1), (sib, r_sib, 2, 1)])


def advance(z, gain):
    anomaly = z - jnp.sum(z, axis=0, keepdims=True) / M
    return z + dot(gain, anomaly, precision=HIGH)


def step_kernel(k, q0, h, g, z, meta, z_out, pay_out, nv_out):
    gain = q0[...] + h[1] + g[...]
    new = advance(z[...], gain)
    z_out[...] = new
    pay, normed = make_payload(new[:, CAP * k : CAP * k + CAP], meta[k])
    pay_out[...] = pay
    nv_out[...] = normed


def final_kernel(q0, h, g, z, x, out, mix):
    @pl.when(pl.program_id(0) == 0)
    def _():
        gain = q0[...] + h[1] + g[...]
        t = z[:, NB * CAP :]
        t = advance(t, gain)[:, :M]
        d = t - jnp.where(iota((M, M), 0) == iota((M, M), 1), 1.0, 0.0)
        dh, dl = split2(d)
        mix[...] = jnp.concatenate([dh, dh, dl], axis=1)

    w = mix[...]
    for t in range(TX // 8):
        block = x[:, 0, 8 * t : 8 * t + 8, :]
        turned = jnp.swapaxes(block, 0, 1)
        updates = []
        for i in range(8):
            h_, l_ = split2(turned[i])
            updates.append(dot(w, jnp.concatenate([h_, l_, h_], axis=0))[None])
        out[:, 0, 8 * t : 8 * t + 8, :] = block + jnp.swapaxes(jnp.concatenate(updates, axis=0), 0, 1)


def rank_kernel(owner, out):
    chunks = OBS // 128
    upper = jnp.where(iota((128, 128), 0) < iota((128, 128), 1), 1.0, 0.0).astype(BF16)
    tiles = iota((TILES, 128), 0)
    for b in range(NB):
        base = jnp.zeros((TILES, 1), F32)
        for c in range(chunks):
            at = slice(128 * c, 128 * c + 128)
            hot = jnp.where(owner[b : b + 1, at] == tiles, 1.0, 0.0)
            rank = dot(hot.astype(BF16), upper) + base
            out[b : b + 1, at] = jnp.sum(hot * rank, axis=0, keepdims=True)
            base = base + jnp.sum(hot, axis=1, keepdims=True)


def place_kernel(order, owner, rank, nv, out):
    turned = nv[...].T
    tiles = iota((TILES, OBS), 0)
    slots = iota((CAP, OBS), 0).astype(F32)
    for k in range(NB):
        b = order[k]
        hot = jnp.where(owner[pl.ds(b, 1), :] == tiles, 1.0, 0.0).astype(BF16)
        h, m, l = split3(turned[CAP * k : CAP * k + CAP])
        got = dot(h, hot) + dot(m, hot) + dot(l, hot)
        mine = rank[pl.ds(b, 1), :] == slots
        out[pl.ds(b, 1), :] = jnp.sum(jnp.where(mine, got, 0.0), axis=0, keepdims=True)


VMEM = pl.BlockSpec(memory_space=pltpu.VMEM)
SMEM = pl.BlockSpec(memory_space=pltpu.SMEM)
ANY = pl.BlockSpec(memory_space=pl.ANY)


def shape(*dims):
    return jax.ShapeDtypeStruct(dims, F32)


def swap(count, first):
    pairs = []
    for i in range(first, count - 1, 2):
        pairs += [(i, i + 1), (i + 1, i)]
    return pairs


def diagonal(width, height):
    pairs = []
    for x in range(0, width, 2):
        for k in range(1, height):
            low, high = x * height + k, (x + 1) * height + k - 1
            pairs += [(low, high), (high, low)]
    return pairs


def local(ensemble, obs_value, obs_variance, obs_owner, obs_cell, obs_reach, batch_order):
    params = pltpu.CompilerParams(vmem_limit_bytes=48 * 2**20)
    call = functools.partial(pl.pallas_call, compiler_params=params)
    width, height = lax.axis_size("gx"), lax.axis_size("gy")
    core, outward, diag = swap(width, 0), swap(width, 1), diagonal(width, height)
    z, meta, pay, nv = call(
        init_kernel,
        out_shape=(shape(M, NB * CAP + 128), shape(NB, 16, CAP), shape(ROWS // 2, 128), shape(1, CAP)),
        in_specs=[SMEM, VMEM, VMEM, VMEM, VMEM, VMEM, ANY],
        out_specs=(VMEM,) * 4,
        scratch_shapes=[pltpu.VMEM((M, TX, TY), F32), pltpu.SemaphoreType.DMA],
        name="init",
    )(batch_order, obs_value, obs_variance, obs_owner, obs_cell, jnp.swapaxes(obs_reach, 1, 2), ensemble)
    rank = call(rank_kernel, out_shape=shape(NB, OBS), in_specs=[VMEM], out_specs=VMEM, name="rank")(obs_owner)
    normed = [nv]
    for k in range(NB):
        outer = lax.ppermute(pay, "gx", outward)
        sib = lax.ppermute(pay, "gx", core)
        sib_outer = lax.ppermute(outer, "gx", core)
        send = call(send_kernel, out_shape=shape(2, M, M), in_specs=[VMEM] * 4, out_specs=VMEM, name="send")(
            pay, outer, sib, sib_outer
        )
        h = lax.ppermute(send, ("gx", "gy"), diag)
        q0 = call(same_kernel, out_shape=shape(M, M), in_specs=[VMEM] * 3, out_specs=VMEM, name="same")(pay, outer, sib)
        g = lax.ppermute(h[0], "gx", core)
        if k + 1 < NB:
            z, pay, nv = call(
                functools.partial(step_kernel, k + 1),
                out_shape=(shape(M, NB * CAP + 128), shape(ROWS // 2, 128), shape(1, CAP)),
                in_specs=[VMEM] * 5,
                out_specs=(VMEM,) * 3,
                name="step",
            )(q0, h, g, z, meta)
            normed.append(nv)
    small = lambda *dims: pl.BlockSpec(dims, lambda i: (0,) * len(dims))
    slab = pl.BlockSpec((M, 1, TX, TY), lambda i: (0, i, 0, 0))
    state = call(
        final_kernel,
        out_shape=shape(M, LEV, TX, TY),
        grid=(LEV,),
        in_specs=[small(M, M), small(2, M, M), small(M, M), small(M, NB * CAP + 128), slab],
        out_specs=slab,
        scratch_shapes=[pltpu.VMEM((M, 3 * M), BF16)],
        name="final",
    )(q0, h, g, z, ensemble)
    mine = jnp.concatenate(normed, axis=1)
    everyone = lax.all_to_all(jnp.broadcast_to(mine, (TILES, NB * CAP)), ("gx", "gy"), 0, 0, tiled=True)
    innovation = call(
        place_kernel,
        out_shape=shape(NB, OBS),
        in_specs=[SMEM, VMEM, VMEM, VMEM],
        out_specs=VMEM,
        name="place",
    )(batch_order, obs_owner, rank, everyone)
    return state, innovation


def solution(mesh):
    placed = (P(None, None, "gx", "gy"), P(), P(), P(), P(), P(), P())
    return jax.shard_map(
        local,
        mesh=mesh,
        in_specs=placed,
        out_specs=(P(None, None, "gx", "gy"), P()),
        check_vma=False,
    )
```

```python
import functools

import jax
import jax.numpy as jnp
from jax import lax
from jax.experimental import pallas as pl
from jax.experimental.pallas import tpu as pltpu
from jax.sharding import PartitionSpec as P

M = 80
LEV = 4
NB = 4
TX = 32
TY = 256
CAP = 64
OBS = 2048
TILES = 128
EPS = 1e-05
F32 = jnp.float32
BF16 = jnp.bfloat16
HIGH = lax.Precision.HIGHEST

ROW_A = M
ROW_C = M + 1
ROW_W = M + 2
ROWS = 96
TAPER = (0.25, 0.5, 0.25, 0.5, 1.0, 0.5, 0.25, 0.5, 0.25)


def split2(x):
    high = x.astype(BF16)
    return high, (x - high.astype(F32)).astype(BF16)


def split3(x):
    high = x.astype(BF16)
    rest = x - high.astype(F32)
    mid = rest.astype(BF16)
    return high, mid, (rest - mid.astype(F32)).astype(BF16)


def iota(shape, dim):
    return lax.broadcasted_iota(jnp.int32, shape, dim)


def dot(a, b, **kw):
    return jnp.dot(a, b, preferred_element_type=F32, **kw)


def dot_t(a, b, **kw):
    return lax.dot_general(a, b, (((1,), (1,)), ((), ())), preferred_element_type=F32, **kw)


def pack(rows):
    return jnp.concatenate([rows[: ROWS // 2], rows[ROWS // 2 :]], axis=1)


def unpack(packed):
    return jnp.concatenate([packed[:, :CAP], packed[:, CAP:]], axis=0)


def make_payload(prior, meta):
    valid = meta[0:1] > 0.5
    value = meta[1:2]
    variance = jnp.where(valid, meta[2:3], 1.0)
    center = jnp.sum(prior, axis=0, keepdims=True) / M
    deviation = prior - center
    spread = jnp.sum(deviation * deviation, axis=0, keepdims=True) / (M - 1)
    total = spread + variance
    miss = value - center
    normed = jnp.where(valid, miss / jnp.sqrt(total), 0.0)
    a = spread / total * miss
    c = jnp.sqrt(variance / total) - 1.0
    d = jnp.where(valid, 1.0 / ((M - 1) * (spread + EPS)), 0.0)
    rows = [deviation, a, c]
    for i in range(9):
        if i == 4:
            rows.append(d)
        else:
            at = 3 + (i if i < 4 else i - 1)
            rows.append(d * (meta[at : at + 1] * TAPER[i]))
    rows.append(jnp.zeros((ROWS - M - 11, CAP), F32))
    return pack(jnp.concatenate(rows, axis=0)), normed


def init_kernel(order_hbm, value_hbm, variance_hbm, owner_hbm, cell_hbm, reach_hbm, x_hbm, out,
                order, value, variance, owner, cell, reach, surface, sems):
    small = [
        pltpu.make_async_copy(source, target, sems.at[i])
        for i, (source, target) in enumerate([
            (order_hbm, order), (owner_hbm, owner), (cell_hbm, cell),
            (value_hbm, value), (variance_hbm, variance), (reach_hbm, reach),
        ])
    ]
    load = pltpu.make_async_copy(x_hbm.at[:, 0], surface, sems.at[6])
    for copy in small:
        copy.start()
    load.start()
    me = lax.axis_index("gx") * lax.axis_size("gy") + lax.axis_index("gy")
    small[0].wait()
    small[1].wait()
    owned = jnp.concatenate([owner[pl.ds(order[k], 1), :] for k in range(NB)], axis=0) == me
    ownf = jnp.where(owned, 1.0, 0.0)
    chunks = OBS // 128
    own64 = jnp.concatenate([ownf[:, 128 * c : 128 * c + 128] for c in range(chunks)], axis=0).astype(BF16)
    upper = jnp.where(iota((128, 128), 0) < iota((128, 128), 1), 1.0, 0.0).astype(BF16)
    rows = NB * chunks
    r0, r1 = iota((rows, rows), 0), iota((rows, rows), 1)
    before = jnp.where((r1 < r0) & (((r0 - r1) & (NB - 1)) == 0), 1.0, 0.0).astype(BF16)
    base = dot(dot(before, own64).astype(BF16), jnp.ones((128, 128), BF16))
    rank64 = dot(own64, upper) + base
    rank = jnp.concatenate([rank64[NB * c : NB * c + NB] for c in range(chunks)], axis=1)
    rank = jnp.where(owned, rank, -1.0)
    slots = iota((CAP, OBS), 0).astype(F32)
    for copy in small[2:]:
        copy.wait()
    metas = []
    for k in range(NB):
        b = order[k]
        hot = jnp.where(rank[k : k + 1] == slots, 1.0, 0.0).astype(BF16)
        where = cell[pl.ds(b, 1), :]
        vh, vm, vl = split3(value[pl.ds(b, 1), :])
        rh, rm, rl = split3(variance[pl.ds(b, 1), :])
        parts = [
            reach[b].astype(F32),
            lax.shift_right_logical(where, 8).astype(F32),
            (where & 255).astype(F32),
            vh.astype(F32), vm.astype(F32), vl.astype(F32),
            rh.astype(F32), rm.astype(F32), rl.astype(F32),
            jnp.ones((1, OBS), F32),
            jnp.zeros((15, OBS), F32),
        ]
        metas.append(dot_t(jnp.concatenate(parts, axis=0).astype(BF16), hot))
    got = jnp.concatenate(metas, axis=1)
    out[M:] = jnp.concatenate(
        [
            got[16:17],
            got[10:11] + got[11:12] + got[12:13],
            got[13:14] + got[14:15] + got[15:16],
            got[:8],
            jnp.zeros((5, NB * CAP), F32),
        ],
        axis=0,
    )
    hot_y = jnp.where(got[9:10] == iota((TY, NB * CAP), 0).astype(F32), 1.0, 0.0).astype(BF16)
    hot_x = jnp.where(got[8:9] == iota((TX, NB * CAP), 0).astype(F32), 1.0, 0.0)
    load.wait()
    group = 16
    for g in range(M // group):
        h, m, l = split3(surface[group * g : group * g + group].reshape(group * TX, TY))
        picked = dot(h, hot_y) + dot(m, hot_y) + dot(l, hot_y)
        out[group * g : group * g + group] = jnp.sum(
            picked.reshape(group, TX, NB * CAP) * hot_x[None], axis=1
        )


def core_of():
    return lax.rem(lax.axis_index("gx"), 2)


def upward(index):
    return lax.rem(index + core_of(), 2) == 0


def emit(k, z, pay_out, edge_out, nv_out):
    pays, news = [], []
    for t in range(2):
        at = slice(CAP * k, CAP * k + CAP)
        pay, normed = make_payload(z[t][:M, at], z[t][M:, at])
        pay_out[t] = pay
        pays.append(pay)
        news.append(normed)
    edge_out[...] = jnp.where(upward(lax.axis_index("gx") // 2), pays[1], pays[0])
    nv_out[...] = jnp.where(core_of() == 0, news[0], news[1])


def start_kernel(own, sib, z_out, pay_out, edge_out, nv_out):
    first = core_of() == 0
    mine, other = own[...], sib[...]
    z = [jnp.where(first, mine, other), jnp.where(first, other, mine)]
    unit = jnp.where(iota((ROWS, 128), 0) == iota((ROWS, 128), 1), 1.0, 0.0)
    unit = jnp.where(iota((ROWS, 128), 0) < M, unit, 0.0)
    for t in range(2):
        z_out[t, :, : NB * CAP] = z[t]
        z_out[t, :, NB * CAP :] = unit
    emit(0, z, pay_out, edge_out, nv_out)


def right_side(rows):
    return rows[ROW_A : ROW_A + 1] + rows[ROW_C : ROW_C + 1] * rows[:M]


def gains(pay, far, sib_far, weight):
    up = upward(lax.axis_index("gx") // 2)
    far, sib_far = far[...], sib_far[...]
    blocks = [jnp.where(up, sib_far, far), pay[0], pay[1], jnp.where(up, far, sib_far)]
    blocks = [unpack(b) for b in blocks]
    rights = [right_side(b) for b in blocks]
    results = []
    for t in range(2):
        left = jnp.concatenate([blocks[t + i][:M] * weight(blocks[t + i], 1 - i) for i in range(3)], axis=1)
        right = jnp.concatenate(rights[t : t + 3], axis=1)
        results.append(dot_t(right, left, precision=HIGH))
    return results


def factor(rows, dx, dy):
    at = ROW_W + 3 * (dx + 1) + dy + 1
    return rows[at : at + 1]


def send_kernel(pay, far, sib_far, out):
    up = upward(lax.axis_index("gy"))
    both = gains(pay, far, sib_far, lambda rows, dx: jnp.where(up, factor(rows, dx, 1), factor(rows, dx, -1)))
    for t in range(2):
        out[t] = both[t]


def same_kernel(k, order, owner, pay, far, sib_far, out, rank_out):
    both = gains(pay, far, sib_far, lambda rows, dx: factor(rows, dx, 0))
    for t in range(2):
        out[t] = both[t]
    row = owner[pl.ds(order[k], 1), :]
    upper = jnp.where(iota((128, 128), 0) < iota((128, 128), 1), 1.0, 0.0).astype(BF16)
    tiles = iota((TILES, 128), 0)
    base = jnp.zeros((TILES, 1), F32)
    for c in range(OBS // 128):
        at = slice(128 * c, 128 * c + 128)
        hot = jnp.where(row[:, at] == tiles, 1.0, 0.0)
        rank = dot(hot.astype(BF16), upper) + base
        rank_out[:, at] = jnp.sum(hot * rank, axis=0, keepdims=True)
        base = base + jnp.sum(hot, axis=1, keepdims=True)


def advance(z, gain):
    anomaly = z - jnp.sum(z, axis=0, keepdims=True) / M
    return z + dot(gain, anomaly, precision=HIGH)


def step_kernel(k, q0, h, g, z, z_out, pay_out, edge_out, nv_out):
    new = []
    for t in range(2):
        moved = advance(z[t, :M], q0[t] + h[t] + g[t])
        z_out[t, :M] = moved
        z_out[t, M:] = z[t, M:]
        new.append(jnp.concatenate([moved, z[t, M:]], axis=0))
    emit(k, new, pay_out, edge_out, nv_out)


def final_kernel(q0, h, g, z, x, out, mix):
    @pl.when(pl.program_id(0) == 0)
    def _():
        c = core_of()
        t = advance(z[c, :M, NB * CAP :], q0[c] + h[c] + g[c])[:, :M]
        d = t - jnp.where(iota((M, M), 0) == iota((M, M), 1), 1.0, 0.0)
        dh, dl = split2(d)
        mix[...] = jnp.concatenate([dh, dh, dl], axis=1)

    w = mix[...]
    for t in range(TX // 8):
        block = x[:, 0, 8 * t : 8 * t + 8, :]
        turned = jnp.swapaxes(block, 0, 1)
        updates = []
        for i in range(8):
            h_, l_ = split2(turned[i])
            updates.append(dot(w, jnp.concatenate([h_, l_, h_], axis=0))[None])
        out[:, 0, 8 * t : 8 * t + 8, :] = block + jnp.swapaxes(jnp.concatenate(updates, axis=0), 0, 1)


def place_kernel(order, owner, nv, r0, r1, r2, r3, out):
    turned = nv[...].T
    slots = iota((CAP, 128), 0).astype(F32)
    for k, rank in enumerate((r0, r1, r2, r3)):
        b = order[k]
        table = turned[CAP * k : CAP * k + CAP]
        row = owner[pl.ds(b, 1), :]
        pieces = []
        for c in range(OBS // 128):
            at = slice(128 * c, 128 * c + 128)
            got = jnp.take_along_axis(table, jnp.broadcast_to(row[:, at], (CAP, 128)), axis=1)
            got = jnp.where(rank[:, at] == slots, got, 0.0)
            pieces.append(jnp.sum(got, axis=0, keepdims=True))
        out[pl.ds(b, 1), :] = jnp.concatenate(pieces, axis=1)


VMEM = pl.BlockSpec(memory_space=pltpu.VMEM)
SMEM = pl.BlockSpec(memory_space=pltpu.SMEM)
HBM = pl.BlockSpec(memory_space=pltpu.HBM)


def shape(*dims):
    return jax.ShapeDtypeStruct(dims, F32)


def swaps(pairs):
    return pairs + [(high, low) for low, high in pairs]


def local(ensemble, obs_value, obs_variance, obs_owner, obs_cell, obs_reach, batch_order):
    params = pltpu.CompilerParams(vmem_limit_bytes=48 * 2**20)
    call = functools.partial(pl.pallas_call, compiler_params=params)
    width, height = lax.axis_size("gx"), lax.axis_size("gy")
    both = ("gx", "gy")
    core = swaps([(x, x + 1) for x in range(0, width, 2)])
    side_x = swaps([(2 * y + c, 2 * y + 2 + c) for c in range(2) for y in range(c, width // 2 - 1, 2)])
    side_y = swaps([
        (x * height + k, x * height + k + 1) for x in range(width) for k in range(x % 2, height - 1, 2)
    ])
    pay_shapes = (shape(2, ROWS // 2, 128), shape(ROWS // 2, 128), shape(1, CAP))
    z_shape = shape(2, ROWS, NB * CAP + 128)
    row = pltpu.VMEM((NB, OBS), F32)
    row_i = pltpu.VMEM((NB, OBS), jnp.int32)
    own = call(
        init_kernel,
        out_shape=shape(ROWS, NB * CAP),
        in_specs=[HBM] * 7,
        out_specs=VMEM,
        scratch_shapes=[
            pltpu.SMEM((NB,), jnp.int32), row, row, row_i, row_i,
            pltpu.VMEM((NB, 8, OBS), jnp.int32), pltpu.VMEM((M, TX, TY), F32), pltpu.SemaphoreType.DMA((7,)),
        ],
        name="init",
    )(batch_order, obs_value, obs_variance, obs_owner, obs_cell, jnp.swapaxes(obs_reach, 1, 2), ensemble)
    z, pay, edge, nv = call(
        start_kernel,
        out_shape=(z_shape,) + pay_shapes,
        in_specs=[VMEM] * 2,
        out_specs=(VMEM,) * 4,
        name="start",
    )(own, lax.ppermute(own, "gx", core))
    normed, ranks = [nv], []
    for k in range(NB):
        far = lax.ppermute(edge, "gx", side_x)
        sib_far = lax.ppermute(far, "gx", core)
        send = call(send_kernel, out_shape=shape(2, M, M), in_specs=[VMEM] * 3, out_specs=VMEM, name="send")(
            pay, far, sib_far
        )
        h = lax.ppermute(send, both, side_y)
        q0, rank = call(
            functools.partial(same_kernel, k),
            out_shape=(shape(2, M, M), shape(1, OBS)),
            in_specs=[SMEM] + [VMEM] * 4,
            out_specs=(VMEM, VMEM),
            name="same",
        )(batch_order, obs_owner, pay, far, sib_far)
        ranks.append(rank)
        g = lax.ppermute(h, "gx", core)
        if k + 1 < NB:
            z, pay, edge, nv = call(
                functools.partial(step_kernel, k + 1),
                out_shape=(z_shape,) + pay_shapes,
                in_specs=[VMEM] * 4,
                out_specs=(VMEM,) * 4,
                name="step",
            )(q0, h, g, z)
            normed.append(nv)
    small = lambda *dims: pl.BlockSpec(dims, lambda i: (0,) * len(dims))
    slab = pl.BlockSpec((M, 1, TX, TY), lambda i: (0, i, 0, 0))
    state = call(
        final_kernel,
        out_shape=shape(M, LEV, TX, TY),
        grid=(LEV,),
        in_specs=[small(2, M, M)] * 3 + [small(2, ROWS, NB * CAP + 128), slab],
        out_specs=slab,
        scratch_shapes=[pltpu.VMEM((M, 3 * M), BF16)],
        name="final",
    )(q0, h, g, z, ensemble)
    mine = jnp.concatenate(normed, axis=1)
    everyone = lax.all_to_all(jnp.broadcast_to(mine, (TILES, NB * CAP)), both, 0, 0, tiled=True)
    innovation = call(
        place_kernel,
        out_shape=shape(NB, OBS),
        in_specs=[SMEM] + [VMEM] * 6,
        out_specs=VMEM,
        name="place",
    )(batch_order, obs_owner, everyone, *ranks)
    return state, innovation


def solution(mesh):
    placed = (P(None, None, "gx", "gy"), P(), P(), P(), P(), P(), P())
    return jax.shard_map(
        local,
        mesh=mesh,
        in_specs=placed,
        out_specs=(P(None, None, "gx", "gy"), P()),
        check_vma=False,
    )
```

```python
import functools

import jax
import jax.numpy as jnp
from jax import lax
from jax.experimental import pallas as pl
from jax.experimental.pallas import tpu as pltpu
from jax.sharding import PartitionSpec as P

M = 80
LEV = 4
NB = 4
TX = 32
TY = 256
CAP = 64
OBS = 2048
TILES = 128
EPS = 1e-05
F32 = jnp.float32
BF16 = jnp.bfloat16
HIGH = lax.Precision.HIGHEST

ROW_A = M
ROW_C = M + 1
ROW_W = M + 2
ROWS = 96
TAPER = (0.25, 0.5, 0.25, 0.5, 1.0, 0.5, 0.25, 0.5, 0.25)


def split2(x):
    high = x.astype(BF16)
    return high, (x - high.astype(F32)).astype(BF16)


def split3(x):
    high = x.astype(BF16)
    rest = x - high.astype(F32)
    mid = rest.astype(BF16)
    return high, mid, (rest - mid.astype(F32)).astype(BF16)


def iota(shape, dim):
    return lax.broadcasted_iota(jnp.int32, shape, dim)


def dot(a, b, **kw):
    return jnp.dot(a, b, preferred_element_type=F32, **kw)


def dot_t(a, b, **kw):
    return lax.dot_general(a, b, (((1,), (1,)), ((), ())), preferred_element_type=F32, **kw)


def pack(rows):
    return jnp.concatenate([rows[: ROWS // 2], rows[ROWS // 2 :]], axis=1)


def unpack(packed):
    return jnp.concatenate([packed[:, :CAP], packed[:, CAP:]], axis=0)


def make_payload(prior, meta):
    valid = meta[0:1] > 0.5
    value = meta[1:2]
    variance = jnp.where(valid, meta[2:3], 1.0)
    center = jnp.sum(prior, axis=0, keepdims=True) / M
    deviation = prior - center
    spread = jnp.sum(deviation * deviation, axis=0, keepdims=True) / (M - 1)
    total = spread + variance
    miss = value - center
    normed = jnp.where(valid, miss / jnp.sqrt(total), 0.0)
    a = spread / total * miss
    c = jnp.sqrt(variance / total) - 1.0
    d = jnp.where(valid, 1.0 / ((M - 1) * (spread + EPS)), 0.0)
    rows = [deviation, a, c]
    for i in range(9):
        if i == 4:
            rows.append(d)
        else:
            at = 3 + (i if i < 4 else i - 1)
            rows.append(d * (meta[at : at + 1] * TAPER[i]))
    rows.append(jnp.zeros((ROWS - M - 11, CAP), F32))
    return pack(jnp.concatenate(rows, axis=0)), normed


def init_kernel(order_hbm, value_hbm, variance_hbm, owner_hbm, cell_hbm, reach_hbm, x_hbm, out,
                order, value, variance, owner, cell, reach, surface, sems):
    small = [
        pltpu.make_async_copy(source, target, sems.at[i])
        for i, (source, target) in enumerate([
            (order_hbm, order), (owner_hbm, owner), (cell_hbm, cell),
            (value_hbm, value), (variance_hbm, variance), (reach_hbm, reach),
        ])
    ]
    load = pltpu.make_async_copy(x_hbm.at[:, 0], surface, sems.at[6])
    for copy in small:
        copy.start()
    load.start()
    me = lax.axis_index("gx") * lax.axis_size("gy") + lax.axis_index("gy")
    small[0].wait()
    small[1].wait()
    owned = jnp.concatenate([owner[pl.ds(order[k], 1), :] for k in range(NB)], axis=0) == me
    ownf = jnp.where(owned, 1.0, 0.0)
    chunks = OBS // 128
    own64 = jnp.concatenate([ownf[:, 128 * c : 128 * c + 128] for c in range(chunks)], axis=0).astype(BF16)
    upper = jnp.where(iota((128, 128), 0) < iota((128, 128), 1), 1.0, 0.0).astype(BF16)
    rows = NB * chunks
    r0, r1 = iota((rows, rows), 0), iota((rows, rows), 1)
    before = jnp.where((r1 < r0) & (((r0 - r1) & (NB - 1)) == 0), 1.0, 0.0).astype(BF16)
    base = dot(dot(before, own64).astype(BF16), jnp.ones((128, 128), BF16))
    rank64 = dot(own64, upper) + base
    rank = jnp.concatenate([rank64[NB * c : NB * c + NB] for c in range(chunks)], axis=1)
    rank = jnp.where(owned, rank, -1.0)
    slots = iota((CAP, OBS), 0).astype(F32)
    for copy in small[2:]:
        copy.wait()
    metas = []
    for k in range(NB):
        b = order[k]
        hot = jnp.where(rank[k : k + 1] == slots, 1.0, 0.0).astype(BF16)
        where = cell[pl.ds(b, 1), :]
        vh, vm, vl = split3(value[pl.ds(b, 1), :])
        rh, rm, rl = split3(variance[pl.ds(b, 1), :])
        parts = [
            reach[b].astype(F32),
            lax.shift_right_logical(where, 8).astype(F32),
            (where & 255).astype(F32),
            vh.astype(F32), vm.astype(F32), vl.astype(F32),
            rh.astype(F32), rm.astype(F32), rl.astype(F32),
            jnp.ones((1, OBS), F32),
            jnp.zeros((15, OBS), F32),
        ]
        metas.append(dot_t(jnp.concatenate(parts, axis=0).astype(BF16), hot))
    got = jnp.concatenate(metas, axis=1)
    out[M:] = jnp.concatenate(
        [
            got[16:17],
            got[10:11] + got[11:12] + got[12:13],
            got[13:14] + got[14:15] + got[15:16],
            got[:8],
            jnp.zeros((5, NB * CAP), F32),
        ],
        axis=0,
    )
    hot_y = jnp.where(got[9:10] == iota((TY, NB * CAP), 0).astype(F32), 1.0, 0.0).astype(BF16)
    hot_x = jnp.where(got[8:9] == iota((TX, NB * CAP), 0).astype(F32), 1.0, 0.0)
    load.wait()
    group = 16
    for g in range(M // group):
        h, m, l = split3(surface[group * g : group * g + group].reshape(group * TX, TY))
        picked = dot(h, hot_y) + dot(m, hot_y) + dot(l, hot_y)
        out[group * g : group * g + group] = jnp.sum(
            picked.reshape(group, TX, NB * CAP) * hot_x[None], axis=1
        )


def core_of():
    return lax.rem(lax.axis_index("gx"), 2)


def edge(index, count):
    return (index == 0) | (index == count - 1)


def upward(index):
    return lax.rem(index + core_of(), 2) == 0


def emit(k, z, pay_out, edge_out, nv_out):
    pays, news = [], []
    for t in range(2):
        at = slice(CAP * k, CAP * k + CAP)
        pay, normed = make_payload(z[t][:M, at], z[t][M:, at])
        pay_out[t] = pay
        pays.append(pay)
        news.append(normed)
    edge_out[...] = jnp.where(upward(lax.axis_index("gx") // 2), pays[1], pays[0])
    nv_out[...] = jnp.where(core_of() == 0, news[0], news[1])


def start_kernel(own, sib, z_out, pay_out, edge_out, nv_out):
    first = core_of() == 0
    mine, other = own[...], sib[...]
    z = [jnp.where(first, mine, other), jnp.where(first, other, mine)]
    unit = jnp.where(iota((ROWS, 128), 0) == iota((ROWS, 128), 1), 1.0, 0.0)
    unit = jnp.where(iota((ROWS, 128), 0) < M, unit, 0.0)
    for t in range(2):
        z_out[t, :, : NB * CAP] = z[t]
        z_out[t, :, NB * CAP :] = unit
    emit(0, z, pay_out, edge_out, nv_out)


def right_side(rows):
    return rows[ROW_A : ROW_A + 1] + rows[ROW_C : ROW_C + 1] * rows[:M]


def gains(pay, far, sib_far, weight):
    y, chips = lax.axis_index("gx") // 2, lax.axis_size("gx") // 2
    up = upward(y)
    first = core_of() == 0
    ends = edge(y, chips)
    far = jnp.where(ends & jnp.logical_not(first), 0.0, far[...])
    sib_far = jnp.where(ends & first, 0.0, sib_far[...])
    blocks = [jnp.where(up, sib_far, far), pay[0], pay[1], jnp.where(up, far, sib_far)]
    blocks = [unpack(b) for b in blocks]
    rights = [right_side(b) for b in blocks]
    results = []
    for t in range(2):
        left = jnp.concatenate([blocks[t + i][:M] * weight(blocks[t + i], 1 - i) for i in range(3)], axis=1)
        right = jnp.concatenate(rights[t : t + 3], axis=1)
        results.append(dot_t(right, left, precision=HIGH))
    return results


def factor(rows, dx, dy):
    at = ROW_W + 3 * (dx + 1) + dy + 1
    return rows[at : at + 1]


def send_kernel(pay, far, sib_far, out):
    up = upward(lax.axis_index("gy"))
    both = gains(pay, far, sib_far, lambda rows, dx: jnp.where(up, factor(rows, dx, 1), factor(rows, dx, -1)))
    for t in range(2):
        out[t] = both[t]


def same_kernel(k, order, owner, pay, far, sib_far, out, rank_out):
    both = gains(pay, far, sib_far, lambda rows, dx: factor(rows, dx, 0))
    for t in range(2):
        out[t] = both[t]
    row = owner[pl.ds(order[k], 1), :]
    upper = jnp.where(iota((128, 128), 0) < iota((128, 128), 1), 1.0, 0.0).astype(BF16)
    tiles = iota((TILES, 128), 0)
    base = jnp.zeros((TILES, 1), F32)
    for c in range(OBS // 128):
        at = slice(128 * c, 128 * c + 128)
        hot = jnp.where(row[:, at] == tiles, 1.0, 0.0)
        rank = dot(hot.astype(BF16), upper) + base
        rank_out[:, at] = jnp.sum(hot * rank, axis=0, keepdims=True)
        base = base + jnp.sum(hot, axis=1, keepdims=True)


def advance(z, gain):
    anomaly = z - jnp.sum(z, axis=0, keepdims=True) / M
    return z + dot(gain, anomaly, precision=HIGH)


def whole_gain(t, q0, h, g):
    first = core_of() == 0
    ends = edge(lax.axis_index("gy"), lax.axis_size("gy"))
    return q0[t] + jnp.where(ends & jnp.logical_not(first), 0.0, h[t]) + jnp.where(ends & first, 0.0, g[t])


def step_kernel(k, q0, h, g, z, z_out, pay_out, edge_out, nv_out):
    new = []
    for t in range(2):
        moved = advance(z[t, :M], whole_gain(t, q0, h, g))
        z_out[t, :M] = moved
        z_out[t, M:] = z[t, M:]
        new.append(jnp.concatenate([moved, z[t, M:]], axis=0))
    emit(k, new, pay_out, edge_out, nv_out)


def final_kernel(q0, h, g, z, x, out, mix):
    @pl.when(pl.program_id(0) == 0)
    def _():
        c = core_of()
        t = advance(z[c, :M, NB * CAP :], whole_gain(c, q0, h, g))[:, :M]
        d = t - jnp.where(iota((M, M), 0) == iota((M, M), 1), 1.0, 0.0)
        dh, dl = split2(d)
        mix[...] = jnp.concatenate([dh, dh, dl], axis=1)

    w = mix[...]
    for t in range(TX // 8):
        block = x[:, 0, 8 * t : 8 * t + 8, :]
        turned = jnp.swapaxes(block, 0, 1)
        updates = []
        for i in range(8):
            h_, l_ = split2(turned[i])
            updates.append(dot(w, jnp.concatenate([h_, l_, h_], axis=0))[None])
        out[:, 0, 8 * t : 8 * t + 8, :] = block + jnp.swapaxes(jnp.concatenate(updates, axis=0), 0, 1)


def place_kernel(order, owner, nv, r0, r1, r2, r3, out):
    turned = nv[...].T
    slots = iota((CAP, 128), 0).astype(F32)
    for k, rank in enumerate((r0, r1, r2, r3)):
        b = order[k]
        table = turned[CAP * k : CAP * k + CAP]
        row = owner[pl.ds(b, 1), :]
        pieces = []
        for c in range(OBS // 128):
            at = slice(128 * c, 128 * c + 128)
            got = jnp.take_along_axis(table, jnp.broadcast_to(row[:, at], (CAP, 128)), axis=1)
            got = jnp.where(rank[:, at] == slots, got, 0.0)
            pieces.append(jnp.sum(got, axis=0, keepdims=True))
        out[pl.ds(b, 1), :] = jnp.concatenate(pieces, axis=1)


VMEM = pl.BlockSpec(memory_space=pltpu.VMEM)
SMEM = pl.BlockSpec(memory_space=pltpu.SMEM)
HBM = pl.BlockSpec(memory_space=pltpu.HBM)


def shape(*dims):
    return jax.ShapeDtypeStruct(dims, F32)


def swaps(pairs):
    return pairs + [(high, low) for low, high in pairs]


def local(ensemble, obs_value, obs_variance, obs_owner, obs_cell, obs_reach, batch_order):
    params = pltpu.CompilerParams(vmem_limit_bytes=48 * 2**20)
    call = functools.partial(pl.pallas_call, compiler_params=params)
    width, height = lax.axis_size("gx"), lax.axis_size("gy")
    both = ("gx", "gy")
    core = swaps([(x, x + 1) for x in range(0, width, 2)])
    chips = width // 2
    side_x = swaps([(2 * y + c, 2 * ((y + 1) % chips) + c) for c in range(2) for y in range(c, chips, 2)])
    side_y = swaps([
        (x * height + k, x * height + (k + 1) % height) for x in range(width) for k in range(x % 2, height, 2)
    ])
    pay_shapes = (shape(2, ROWS // 2, 128), shape(ROWS // 2, 128), shape(1, CAP))
    z_shape = shape(2, ROWS, NB * CAP + 128)
    row = pltpu.VMEM((NB, OBS), F32)
    row_i = pltpu.VMEM((NB, OBS), jnp.int32)
    own = call(
        init_kernel,
        out_shape=shape(ROWS, NB * CAP),
        in_specs=[HBM] * 7,
        out_specs=VMEM,
        scratch_shapes=[
            pltpu.SMEM((NB,), jnp.int32), row, row, row_i, row_i,
            pltpu.VMEM((NB, 8, OBS), jnp.int32), pltpu.VMEM((M, TX, TY), F32), pltpu.SemaphoreType.DMA((7,)),
        ],
        name="init",
    )(*(
        pltpu.with_memory_space_constraint(value, pltpu.HBM)
        for value in (
            batch_order, obs_value, obs_variance, obs_owner, obs_cell, jnp.swapaxes(obs_reach, 1, 2), ensemble
        )
    ))
    z, pay, edge, nv = call(
        start_kernel,
        out_shape=(z_shape,) + pay_shapes,
        in_specs=[VMEM] * 2,
        out_specs=(VMEM,) * 4,
        name="start",
    )(own, lax.ppermute(own, "gx", core))
    normed, ranks = [nv], []
    for k in range(NB):
        far = lax.ppermute(edge, "gx", side_x)
        sib_far = lax.ppermute(far, "gx", core)
        send = call(send_kernel, out_shape=shape(2, M, M), in_specs=[VMEM] * 3, out_specs=VMEM, name="send")(
            pay, far, sib_far
        )
        h = lax.ppermute(send, both, side_y)
        q0, rank = call(
            functools.partial(same_kernel, k),
            out_shape=(shape(2, M, M), shape(1, OBS)),
            in_specs=[SMEM] + [VMEM] * 4,
            out_specs=(VMEM, VMEM),
            name="same",
        )(batch_order, obs_owner, pay, far, sib_far)
        ranks.append(rank)
        h, q0 = lax.optimization_barrier((h, q0))
        g = lax.ppermute(h, "gx", core)
        if k + 1 < NB:
            z, pay, edge, nv = call(
                functools.partial(step_kernel, k + 1),
                out_shape=(z_shape,) + pay_shapes,
                in_specs=[VMEM] * 4,
                out_specs=(VMEM,) * 4,
                name="step",
            )(q0, h, g, z)
            normed.append(nv)
    small = lambda *dims: pl.BlockSpec(dims, lambda i: (0,) * len(dims))
    slab = pl.BlockSpec((M, 1, TX, TY), lambda i: (0, i, 0, 0))
    state = call(
        final_kernel,
        out_shape=shape(M, LEV, TX, TY),
        grid=(LEV,),
        in_specs=[small(2, M, M)] * 3 + [small(2, ROWS, NB * CAP + 128), slab],
        out_specs=slab,
        scratch_shapes=[pltpu.VMEM((M, 3 * M), BF16)],
        name="final",
    )(q0, h, g, z, ensemble)
    mine = jnp.concatenate(normed, axis=1)
    everyone = lax.all_to_all(jnp.broadcast_to(mine, (TILES, NB * CAP)), both, 0, 0, tiled=True)
    innovation = call(
        place_kernel,
        out_shape=shape(NB, OBS),
        in_specs=[SMEM] + [VMEM] * 6,
        out_specs=VMEM,
        name="place",
    )(batch_order, obs_owner, everyone, *ranks)
    return state, innovation


def solution(mesh):
    placed = (P(None, None, "gx", "gy"), P(), P(), P(), P(), P(), P())
    return jax.shard_map(
        local,
        mesh=mesh,
        in_specs=placed,
        out_specs=(P(None, None, "gx", "gy"), P()),
        check_vma=False,
    )
```

```python
import functools

import jax
import jax.numpy as jnp
from jax import lax
from jax.experimental import pallas as pl
from jax.experimental.pallas import tpu as pltpu
from jax.sharding import PartitionSpec as P

M = 80
LEV = 4
NB = 4
TX = 32
TY = 256
CAP = 64
OBS = 2048
TILES = 128
EPS = 1e-05
F32 = jnp.float32
BF16 = jnp.bfloat16
HIGH = lax.Precision.HIGHEST
SLAB = 16
PARTS = TX // SLAB

ROW_A = M
ROW_C = M + 1
ROW_W = M + 2
ROW_N = M + 11
ROWS = 96
TAPER = (0.25, 0.5, 0.25, 0.5, 1.0, 0.5, 0.25, 0.5, 0.25)


def split2(x):
    high = x.astype(BF16)
    return high, (x - high.astype(F32)).astype(BF16)


def split3(x):
    high = x.astype(BF16)
    rest = x - high.astype(F32)
    mid = rest.astype(BF16)
    return high, mid, (rest - mid.astype(F32)).astype(BF16)


def iota(shape, dim):
    return lax.broadcasted_iota(jnp.int32, shape, dim)


def dot(a, b, **kw):
    return jnp.dot(a, b, preferred_element_type=F32, **kw)


def dot_t(a, b, **kw):
    return lax.dot_general(a, b, (((1,), (1,)), ((), ())), preferred_element_type=F32, **kw)


def pack(rows):
    return jnp.concatenate([rows[: ROWS // 2], rows[ROWS // 2 :]], axis=1)


def unpack(packed):
    return jnp.concatenate([packed[:, :CAP], packed[:, CAP:]], axis=0)


def make_payload(prior, meta):
    valid = meta[0:1] > 0.5
    value = meta[1:2]
    variance = jnp.where(valid, meta[2:3], 1.0)
    center = jnp.sum(prior, axis=0, keepdims=True) / M
    deviation = prior - center
    spread = jnp.sum(deviation * deviation, axis=0, keepdims=True) / (M - 1)
    total = spread + variance
    miss = value - center
    normed = jnp.where(valid, miss / jnp.sqrt(total), 0.0)
    a = spread / total * miss
    c = jnp.sqrt(variance / total) - 1.0
    d = jnp.where(valid, 1.0 / ((M - 1) * (spread + EPS)), 0.0)
    rows = [deviation, a, c]
    for i in range(9):
        if i == 4:
            rows.append(d)
        else:
            at = 3 + (i if i < 4 else i - 1)
            rows.append(d * (meta[at : at + 1] * TAPER[i]))
    rows.append(jnp.zeros((ROWS - M - 11, CAP), F32))
    return pack(jnp.concatenate(rows, axis=0)), normed


def init_kernel(order_hbm, value_hbm, variance_hbm, owner_hbm, cell_hbm, reach_hbm, x_hbm, out,
                order, value, variance, owner, cell, reach, surface, sems):
    small = [
        pltpu.make_async_copy(source, target, sems.at[i])
        for i, (source, target) in enumerate([
            (order_hbm, order), (owner_hbm, owner), (cell_hbm, cell),
            (value_hbm, value), (variance_hbm, variance), (reach_hbm, reach),
        ])
    ]
    load = pltpu.make_async_copy(x_hbm.at[:, 0], surface, sems.at[6])
    for copy in small:
        copy.start()
    load.start()
    me = lax.axis_index("gx") * lax.axis_size("gy") + lax.axis_index("gy")
    small[0].wait()
    small[1].wait()
    owned = jnp.concatenate([owner[pl.ds(order[k], 1), :] for k in range(NB)], axis=0) == me
    ownf = jnp.where(owned, 1.0, 0.0)
    chunks = OBS // 128
    own64 = jnp.concatenate([ownf[:, 128 * c : 128 * c + 128] for c in range(chunks)], axis=0).astype(BF16)
    upper = jnp.where(iota((128, 128), 0) < iota((128, 128), 1), 1.0, 0.0).astype(BF16)
    rows = NB * chunks
    r0, r1 = iota((rows, rows), 0), iota((rows, rows), 1)
    before = jnp.where((r1 < r0) & (((r0 - r1) & (NB - 1)) == 0), 1.0, 0.0).astype(BF16)
    base = dot(dot(before, own64).astype(BF16), jnp.ones((128, 128), BF16))
    rank64 = dot(own64, upper) + base
    rank = jnp.concatenate([rank64[NB * c : NB * c + NB] for c in range(chunks)], axis=1)
    rank = jnp.where(owned, rank, -1.0)
    slots = iota((CAP, OBS), 0).astype(F32)
    for copy in small[2:]:
        copy.wait()
    metas = []
    for k in range(NB):
        b = order[k]
        hot = jnp.where(rank[k : k + 1] == slots, 1.0, 0.0).astype(BF16)
        where = cell[pl.ds(b, 1), :]
        vh, vm, vl = split3(value[pl.ds(b, 1), :])
        rh, rm, rl = split3(variance[pl.ds(b, 1), :])
        parts = [
            reach[b].astype(F32),
            lax.shift_right_logical(where, 8).astype(F32),
            (where & 255).astype(F32),
            vh.astype(F32), vm.astype(F32), vl.astype(F32),
            rh.astype(F32), rm.astype(F32), rl.astype(F32),
            jnp.ones((1, OBS), F32),
            jnp.zeros((15, OBS), F32),
        ]
        metas.append(dot_t(jnp.concatenate(parts, axis=0).astype(BF16), hot))
    got = jnp.concatenate(metas, axis=1)
    out[M:] = jnp.concatenate(
        [
            got[16:17],
            got[10:11] + got[11:12] + got[12:13],
            got[13:14] + got[14:15] + got[15:16],
            got[:8],
            jnp.zeros((5, NB * CAP), F32),
        ],
        axis=0,
    )
    hot_y = jnp.where(got[9:10] == iota((TY, NB * CAP), 0).astype(F32), 1.0, 0.0).astype(BF16)
    hot_x = jnp.where(got[8:9] == iota((TX, NB * CAP), 0).astype(F32), 1.0, 0.0)
    load.wait()
    group = 16
    for g in range(M // group):
        h, m, l = split3(surface[group * g : group * g + group].reshape(group * TX, TY))
        picked = dot(h, hot_y) + dot(m, hot_y) + dot(l, hot_y)
        out[group * g : group * g + group] = jnp.sum(
            picked.reshape(group, TX, NB * CAP) * hot_x[None], axis=1
        )


def core_of():
    return lax.rem(lax.axis_index("gx"), 2)


def edge(index, count):
    return (index == 0) | (index == count - 1)


def upward(index):
    return lax.rem(index + core_of(), 2) == 0


def emit(k, z, z_out, pay_out, edge_out, nv_out=None):
    pays = []
    at = slice(CAP * k, CAP * k + CAP)
    news = []
    for t in range(2):
        pay, normed = make_payload(z[t][:M, at], z[t][M:, at])
        pay_out[t] = pay
        z_out[t, ROW_N : ROW_N + 1, at] = normed
        pays.append(pay)
        news.append(normed)
    edge_out[...] = jnp.where(upward(lax.axis_index("gx") // 2), pays[1], pays[0])
    if nv_out is not None:
        first = core_of() == 0
        past = slice(0, CAP * k)
        row = jnp.concatenate([
            jnp.where(first, z[0][ROW_N : ROW_N + 1, past], z[1][ROW_N : ROW_N + 1, past]),
            jnp.where(first, news[0], news[1]),
        ], axis=1)
        nv_out[...] = jnp.broadcast_to(row[None], nv_out.shape)


def start_kernel(own, sib, z_out, pay_out, edge_out):
    first = core_of() == 0
    mine, other = own[...], sib[...]
    z = [jnp.where(first, mine, other), jnp.where(first, other, mine)]
    unit = jnp.where(iota((ROWS, 128), 0) == iota((ROWS, 128), 1), 1.0, 0.0)
    unit = jnp.where(iota((ROWS, 128), 0) < M, unit, 0.0)
    for t in range(2):
        z_out[t, :, : NB * CAP] = z[t]
        z_out[t, :, NB * CAP :] = unit
    emit(0, z, z_out, pay_out, edge_out)


def right_side(rows):
    return rows[ROW_A : ROW_A + 1] + rows[ROW_C : ROW_C + 1] * rows[:M]


def gains(pay, far, sib_far, weight):
    y, chips = lax.axis_index("gx") // 2, lax.axis_size("gx") // 2
    up = upward(y)
    first = core_of() == 0
    ends = edge(y, chips)
    far = jnp.where(ends & jnp.logical_not(first), 0.0, far[...])
    sib_far = jnp.where(ends & first, 0.0, sib_far[...])
    blocks = [jnp.where(up, sib_far, far), pay[0], pay[1], jnp.where(up, far, sib_far)]
    blocks = [unpack(b) for b in blocks]
    rights = [right_side(b) for b in blocks]
    results = []
    for t in range(2):
        left = jnp.concatenate([blocks[t + i][:M] * weight(blocks[t + i], 1 - i) for i in range(3)], axis=1)
        right = jnp.concatenate(rights[t : t + 3], axis=1)
        results.append(dot_t(right, left, precision=HIGH))
    return results


def factor(rows, dx, dy):
    at = ROW_W + 3 * (dx + 1) + dy + 1
    return rows[at : at + 1]


def send_kernel(pay, far, sib_far, out):
    up = upward(lax.axis_index("gy"))
    both = gains(pay, far, sib_far, lambda rows, dx: jnp.where(up, factor(rows, dx, 1), factor(rows, dx, -1)))
    for t in range(2):
        out[t] = both[t]


def same_kernel(k, order, owner, pay, far, sib_far, out, rank_out):
    both = gains(pay, far, sib_far, lambda rows, dx: factor(rows, dx, 0))
    for t in range(2):
        out[t] = both[t]
    row = owner[pl.ds(order[k], 1), :]
    upper = jnp.where(iota((128, 128), 0) < iota((128, 128), 1), 1.0, 0.0).astype(BF16)
    tiles = iota((TILES, 128), 0)
    base = jnp.zeros((TILES, 1), F32)
    for c in range(OBS // 128):
        at = slice(128 * c, 128 * c + 128)
        hot = jnp.where(row[:, at] == tiles, 1.0, 0.0)
        rank = dot(hot.astype(BF16), upper) + base
        rank_out[:, at] = jnp.sum(hot * rank, axis=0, keepdims=True)
        base = base + jnp.sum(hot, axis=1, keepdims=True)


def advance(z, gain):
    anomaly = z - jnp.sum(z, axis=0, keepdims=True) / M
    return z + dot(gain, anomaly, precision=HIGH)


def whole_gain(t, q0, h, g):
    first = core_of() == 0
    ends = edge(lax.axis_index("gy"), lax.axis_size("gy"))
    return q0[t] + jnp.where(ends & jnp.logical_not(first), 0.0, h[t]) + jnp.where(ends & first, 0.0, g[t])


def step_kernel(k, q0, h, g, z, z_out, pay_out, edge_out, nv_out=None):
    new = []
    for t in range(2):
        moved = advance(z[t, :M], whole_gain(t, q0, h, g))
        z_out[t, :M] = moved
        z_out[t, M:] = z[t, M:]
        new.append(jnp.concatenate([moved, z[t, M:]], axis=0))
    emit(k, new, z_out, pay_out, edge_out, nv_out)


def final_kernel(q0, h, g, z, x, out, mix):
    step = pl.program_id(0)

    @pl.when(step == 0)
    def _():
        c = core_of()
        t = advance(z[c, :M, NB * CAP :], whole_gain(c, q0, h, g))[:, :M]
        d = t - jnp.where(iota((M, M), 0) == iota((M, M), 1), 1.0, 0.0)
        dh, dl = split2(d)
        mix[...] = jnp.concatenate([dh, dh, dl], axis=1)

    w = mix[...]
    level, start = step // PARTS, lax.rem(step, PARTS) * SLAB
    for t in range(SLAB // 8):
        block = x[:, level, pl.ds(pl.multiple_of(start + 8 * t, 8), 8), :]
        turned = jnp.swapaxes(block, 0, 1)
        updates = []
        for i in range(8):
            h_, l_ = split2(turned[i])
            updates.append(dot(w, jnp.concatenate([h_, l_, h_], axis=0))[None])
        out[:, 0, 8 * t : 8 * t + 8, :] = block + jnp.swapaxes(jnp.concatenate(updates, axis=0), 0, 1)


def place_kernel(order, owner, nv, r0, r1, r2, r3, out):
    turned = nv[...].T
    slots = iota((CAP, 128), 0).astype(F32)
    for k, rank in enumerate((r0, r1, r2, r3)):
        b = order[k]
        table = turned[CAP * k : CAP * k + CAP]
        row = owner[pl.ds(b, 1), :]
        pieces = []
        for c in range(OBS // 128):
            at = slice(128 * c, 128 * c + 128)
            got = jnp.take_along_axis(table, jnp.broadcast_to(row[:, at], (CAP, 128)), axis=1)
            got = jnp.where(rank[:, at] == slots, got, 0.0)
            pieces.append(jnp.sum(got, axis=0, keepdims=True))
        out[pl.ds(b, 1), :] = jnp.concatenate(pieces, axis=1)


VMEM = pl.BlockSpec(memory_space=pltpu.VMEM)
SMEM = pl.BlockSpec(memory_space=pltpu.SMEM)
HBM = pl.BlockSpec(memory_space=pltpu.HBM)


def shape(*dims):
    return jax.ShapeDtypeStruct(dims, F32)


def swaps(pairs):
    return pairs + [(high, low) for low, high in pairs]


def local(ensemble, obs_value, obs_variance, obs_owner, obs_cell, obs_reach, batch_order):
    params = pltpu.CompilerParams(vmem_limit_bytes=24 * 2**20)
    call = functools.partial(pl.pallas_call, compiler_params=params)
    width, height = lax.axis_size("gx"), lax.axis_size("gy")
    both = ("gx", "gy")
    core = swaps([(x, x + 1) for x in range(0, width, 2)])
    chips = width // 2
    side_x = swaps([(2 * y + c, 2 * ((y + 1) % chips) + c) for c in range(2) for y in range(c, chips, 2)])
    side_y = swaps([
        (x * height + k, x * height + k + 1) for x in range(width) for k in range(x % 2, height - 1, 2)
    ] + [(x * height + k, (x + 2) * height + k) for x in range(1, width, 4) for k in (0, height - 1)])
    pay_shapes = (shape(2, ROWS // 2, 128), shape(ROWS // 2, 128))
    z_shape = shape(2, ROWS, NB * CAP + 128)
    row = pltpu.VMEM((NB, OBS), F32)
    row_i = pltpu.VMEM((NB, OBS), jnp.int32)
    own = call(
        init_kernel,
        out_shape=shape(ROWS, NB * CAP),
        in_specs=[HBM] * 7,
        out_specs=VMEM,
        scratch_shapes=[
            pltpu.SMEM((NB,), jnp.int32), row, row, row_i, row_i,
            pltpu.VMEM((NB, 8, OBS), jnp.int32), pltpu.VMEM((M, TX, TY), F32), pltpu.SemaphoreType.DMA((7,)),
        ],
        name="init",
    )(*(
        pltpu.with_memory_space_constraint(value, pltpu.HBM)
        for value in (
            batch_order, obs_value, obs_variance, obs_owner, obs_cell, jnp.swapaxes(obs_reach, 1, 2), ensemble
        )
    ))
    z, pay, edge = call(
        start_kernel,
        out_shape=(z_shape,) + pay_shapes,
        in_specs=[VMEM] * 2,
        out_specs=(VMEM,) * 3,
        name="start",
    )(own, lax.ppermute(own, "gx", core))
    ranks = []
    for k in range(NB):
        last = k + 1 == NB
        far = lax.ppermute(edge, "gx", side_x)
        if last:
            everyone = lax.all_to_all(nv, both, 0, 0, tiled=True).reshape(TILES, NB * CAP)
            far, everyone = lax.optimization_barrier((far, everyone))
        sib_far = lax.ppermute(far, "gx", core)
        send = call(send_kernel, out_shape=shape(2, M, M), in_specs=[VMEM] * 3, out_specs=VMEM, name="send")(
            pay, far, sib_far
        )
        h = lax.ppermute(send, both, side_y)
        q0, rank = call(
            functools.partial(same_kernel, k),
            out_shape=(shape(2, M, M), shape(1, OBS)),
            in_specs=[SMEM] + [VMEM] * 4,
            out_specs=(VMEM, VMEM),
            name="same",
        )(batch_order, obs_owner, pay, far, sib_far)
        ranks.append(rank)
        if last:
            innovation = call(
                place_kernel,
                out_shape=shape(NB, OBS),
                in_specs=[SMEM] + [VMEM] * 6,
                out_specs=VMEM,
                name="place",
            )(batch_order, obs_owner, everyone, *ranks)
            h, q0, innovation = lax.optimization_barrier((h, q0, innovation))
        else:
            h, q0 = lax.optimization_barrier((h, q0))
        g = lax.ppermute(h, "gx", core)
        if not last:
            wide = (shape(TILES, 1, NB * CAP),) if k + 2 == NB else ()
            z, pay, edge, *rest = call(
                functools.partial(step_kernel, k + 1),
                out_shape=(z_shape,) + pay_shapes + wide,
                in_specs=[VMEM] * 4,
                out_specs=(VMEM,) * (3 + len(wide)),
                name="step",
            )(q0, h, g, z)
            if rest:
                nv = rest[0]
    state = call(
        final_kernel,
        out_shape=shape(M, LEV, TX, TY),
        grid=(LEV * PARTS,),
        in_specs=[VMEM] * 5,
        out_specs=pl.BlockSpec((M, 1, SLAB, TY), lambda i: (0, i // PARTS, i % PARTS, 0)),
        scratch_shapes=[pltpu.VMEM((M, 3 * M), BF16)],
        name="final",
    )(q0, h, g, z, pltpu.with_memory_space_constraint(ensemble, pltpu.VMEM))
    return state, innovation


def solution(mesh):
    placed = (P(None, None, "gx", "gy"), P(), P(), P(), P(), P(), P())
    return jax.shard_map(
        local,
        mesh=mesh,
        in_specs=placed,
        out_specs=(P(None, None, "gx", "gy"), P()),
        check_vma=False,
    )
```

```python
import functools

import jax
import jax.numpy as jnp
from jax import lax
from jax.experimental import pallas as pl
from jax.experimental.pallas import tpu as pltpu
from jax.sharding import PartitionSpec as P

M = 80
LEV = 4
NB = 4
TX = 32
TY = 256
CAP = 64
OBS = 2048
TILES = 128
EPS = 1e-05
F32 = jnp.float32
BF16 = jnp.bfloat16
HIGH = lax.Precision.HIGHEST
SLAB = 16
PARTS = TX // SLAB
SLABS = LEV * PARTS

ROW_A = M
ROW_C = M + 1
ROW_W = M + 2
ROW_N = M + 11
ROWS = 96
TAPER = (0.25, 0.5, 0.25, 0.5, 1.0, 0.5, 0.25, 0.5, 0.25)


def split2(x):
    high = x.astype(BF16)
    return high, (x - high.astype(F32)).astype(BF16)


def split3(x):
    high = x.astype(BF16)
    rest = x - high.astype(F32)
    mid = rest.astype(BF16)
    return high, mid, (rest - mid.astype(F32)).astype(BF16)


def iota(shape, dim):
    return lax.broadcasted_iota(jnp.int32, shape, dim)


def dot(a, b, **kw):
    return jnp.dot(a, b, preferred_element_type=F32, **kw)


def dot_t(a, b, **kw):
    return lax.dot_general(a, b, (((1,), (1,)), ((), ())), preferred_element_type=F32, **kw)


def pack(rows):
    return jnp.concatenate([rows[: ROWS // 2], rows[ROWS // 2 :]], axis=1)


def unpack(packed):
    return jnp.concatenate([packed[:, :CAP], packed[:, CAP:]], axis=0)


def make_payload(prior, meta):
    valid = meta[0:1] > 0.5
    value = meta[1:2]
    variance = jnp.where(valid, meta[2:3], 1.0)
    center = jnp.sum(prior, axis=0, keepdims=True) / M
    deviation = prior - center
    spread = jnp.sum(deviation * deviation, axis=0, keepdims=True) / (M - 1)
    total = spread + variance
    miss = value - center
    normed = jnp.where(valid, miss / jnp.sqrt(total), 0.0)
    a = spread / total * miss
    c = jnp.sqrt(variance / total) - 1.0
    d = jnp.where(valid, 1.0 / ((M - 1) * (spread + EPS)), 0.0)
    rows = [deviation, a, c]
    for i in range(9):
        if i == 4:
            rows.append(d)
        else:
            at = 3 + (i if i < 4 else i - 1)
            rows.append(d * (meta[at : at + 1] * TAPER[i]))
    rows.append(jnp.zeros((ROWS - M - 11, CAP), F32))
    return pack(jnp.concatenate(rows, axis=0)), normed


def init_kernel(order_hbm, value_hbm, variance_hbm, owner_hbm, cell_hbm, reach_hbm, x_hbm, out,
                order, value, variance, owner, cell, reach, surface, sems):
    small = [
        pltpu.make_async_copy(source, target, sems.at[i])
        for i, (source, target) in enumerate([
            (order_hbm, order), (owner_hbm, owner), (cell_hbm, cell),
            (value_hbm, value), (variance_hbm, variance), (reach_hbm, reach),
        ])
    ]
    load = pltpu.make_async_copy(x_hbm.at[:, 0], surface, sems.at[6])
    for copy in small:
        copy.start()
    load.start()
    me = lax.axis_index("gx") * lax.axis_size("gy") + lax.axis_index("gy")
    small[0].wait()
    small[1].wait()
    owned = jnp.concatenate([owner[pl.ds(order[k], 1), :] for k in range(NB)], axis=0) == me
    ownf = jnp.where(owned, 1.0, 0.0)
    chunks = OBS // 128
    own64 = jnp.concatenate([ownf[:, 128 * c : 128 * c + 128] for c in range(chunks)], axis=0).astype(BF16)
    upper = jnp.where(iota((128, 128), 0) < iota((128, 128), 1), 1.0, 0.0).astype(BF16)
    rows = NB * chunks
    r0, r1 = iota((rows, rows), 0), iota((rows, rows), 1)
    before = jnp.where((r1 < r0) & (((r0 - r1) & (NB - 1)) == 0), 1.0, 0.0).astype(BF16)
    base = dot(dot(before, own64).astype(BF16), jnp.ones((128, 128), BF16))
    rank64 = dot(own64, upper) + base
    rank = jnp.concatenate([rank64[NB * c : NB * c + NB] for c in range(chunks)], axis=1)
    rank = jnp.where(owned, rank, -1.0)
    slots = iota((CAP, OBS), 0).astype(F32)
    for copy in small[2:]:
        copy.wait()
    metas = []
    for k in range(NB):
        b = order[k]
        hot = jnp.where(rank[k : k + 1] == slots, 1.0, 0.0).astype(BF16)
        where = cell[pl.ds(b, 1), :]
        vh, vm, vl = split3(value[pl.ds(b, 1), :])
        rh, rm, rl = split3(variance[pl.ds(b, 1), :])
        parts = [
            reach[b].astype(F32),
            lax.shift_right_logical(where, 8).astype(F32),
            (where & 255).astype(F32),
            vh.astype(F32), vm.astype(F32), vl.astype(F32),
            rh.astype(F32), rm.astype(F32), rl.astype(F32),
            jnp.ones((1, OBS), F32),
            jnp.zeros((15, OBS), F32),
        ]
        metas.append(dot_t(jnp.concatenate(parts, axis=0).astype(BF16), hot))
    got = jnp.concatenate(metas, axis=1)
    out[M:] = jnp.concatenate(
        [
            got[16:17],
            got[10:11] + got[11:12] + got[12:13],
            got[13:14] + got[14:15] + got[15:16],
            got[:8],
            jnp.zeros((5, NB * CAP), F32),
        ],
        axis=0,
    )
    hot_y = jnp.where(got[9:10] == iota((TY, NB * CAP), 0).astype(F32), 1.0, 0.0).astype(BF16)
    hot_x = jnp.where(got[8:9] == iota((TX, NB * CAP), 0).astype(F32), 1.0, 0.0)
    load.wait()
    group = 16
    for g in range(M // group):
        h, m, l = split3(surface[group * g : group * g + group].reshape(group * TX, TY))
        picked = dot(h, hot_y) + dot(m, hot_y) + dot(l, hot_y)
        out[group * g : group * g + group] = jnp.sum(
            picked.reshape(group, TX, NB * CAP) * hot_x[None], axis=1
        )


def core_of():
    return lax.rem(lax.axis_index("gx"), 2)


def edge(index, count):
    return (index == 0) | (index == count - 1)


def upward(index):
    return lax.rem(index + core_of(), 2) == 0


def emit(k, z, z_out, pay_out, edge_out, nv_out=None):
    pays = []
    at = slice(CAP * k, CAP * k + CAP)
    news = []
    for t in range(2):
        pay, normed = make_payload(z[t][:M, at], z[t][M:, at])
        pay_out[t] = pay
        z_out[t, ROW_N : ROW_N + 1, at] = normed
        pays.append(pay)
        news.append(normed)
    edge_out[...] = jnp.where(upward(lax.axis_index("gx") // 2), pays[1], pays[0])
    if nv_out is not None:
        first = core_of() == 0
        past = slice(0, CAP * k)
        nv_out[:, past] = jnp.where(first, z[0][ROW_N : ROW_N + 1, past], z[1][ROW_N : ROW_N + 1, past])
        nv_out[:, at] = jnp.where(first, news[0], news[1])


def start_kernel(own, sib, z_out, pay_out, edge_out):
    first = core_of() == 0
    mine, other = own[...], sib[...]
    z = [jnp.where(first, mine, other), jnp.where(first, other, mine)]
    unit = jnp.where(iota((ROWS, 128), 0) == iota((ROWS, 128), 1), 1.0, 0.0)
    unit = jnp.where(iota((ROWS, 128), 0) < M, unit, 0.0)
    for t in range(2):
        z_out[t, :, : NB * CAP] = z[t]
        z_out[t, :, NB * CAP :] = unit
    emit(0, z, z_out, pay_out, edge_out)


def right_side(rows):
    return rows[ROW_A : ROW_A + 1] + rows[ROW_C : ROW_C + 1] * rows[:M]


def gains(pay, far, sib_far, weight):
    y, chips = lax.axis_index("gx") // 2, lax.axis_size("gx") // 2
    up = upward(y)
    first = core_of() == 0
    ends = edge(y, chips)
    far = jnp.where(ends & jnp.logical_not(first), 0.0, far[...])
    sib_far = jnp.where(ends & first, 0.0, sib_far[...])
    blocks = [jnp.where(up, sib_far, far), pay[0], pay[1], jnp.where(up, far, sib_far)]
    blocks = [unpack(b) for b in blocks]
    rights = [right_side(b) for b in blocks]
    results = []
    for t in range(2):
        left = jnp.concatenate([blocks[t + i][:M] * weight(blocks[t + i], 1 - i) for i in range(3)], axis=1)
        right = jnp.concatenate(rights[t : t + 3], axis=1)
        results.append(dot_t(right, left, precision=HIGH))
    return results


def factor(rows, dx, dy):
    at = ROW_W + 3 * (dx + 1) + dy + 1
    return rows[at : at + 1]


def send_kernel(pay, far, sib_far, out):
    up = upward(lax.axis_index("gy"))
    both = gains(pay, far, sib_far, lambda rows, dx: jnp.where(up, factor(rows, dx, 1), factor(rows, dx, -1)))
    for t in range(2):
        out[t] = both[t]


def same_kernel(k, order, owner, pay, far, sib_far, out, rank_out):
    both = gains(pay, far, sib_far, lambda rows, dx: factor(rows, dx, 0))
    for t in range(2):
        out[t] = both[t]
    row = owner[pl.ds(order[k], 1), :]
    upper = jnp.where(iota((128, 128), 0) < iota((128, 128), 1), 1.0, 0.0).astype(BF16)
    tiles = iota((TILES, 128), 0)
    base = jnp.zeros((TILES, 1), F32)
    for c in range(OBS // 128):
        at = slice(128 * c, 128 * c + 128)
        hot = jnp.where(row[:, at] == tiles, 1.0, 0.0)
        rank = dot(hot.astype(BF16), upper) + base
        rank_out[:, at] = jnp.sum(hot * rank, axis=0, keepdims=True)
        base = base + jnp.sum(hot, axis=1, keepdims=True)


def advance(z, gain):
    anomaly = z - jnp.sum(z, axis=0, keepdims=True) / M
    return z + dot(gain, anomaly, precision=HIGH)


def whole_gain(t, q0, h, g):
    first = core_of() == 0
    ends = edge(lax.axis_index("gy"), lax.axis_size("gy"))
    return q0[t] + jnp.where(ends & jnp.logical_not(first), 0.0, h[t]) + jnp.where(ends & first, 0.0, g[t])


def step_kernel(k, q0, h, g, z, z_out, pay_out, edge_out, nv_out=None):
    new = []
    for t in range(2):
        moved = advance(z[t, :M], whole_gain(t, q0, h, g))
        z_out[t, :M] = moved
        z_out[t, M:] = z[t, M:]
        new.append(jnp.concatenate([moved, z[t, M:]], axis=0))
    emit(k, new, z_out, pay_out, edge_out, nv_out)


def final_kernel(q0, h, g, z, x, out, come, go, come_sems, go_sems):
    def part(ref, i):
        return ref.at[:, i // PARTS, pl.ds((i % PARTS) * SLAB, SLAB), :]

    loads = [pltpu.make_async_copy(part(x, i), come.at[i], come_sems.at[i]) for i in range(SLABS)]
    stores = [pltpu.make_async_copy(go.at[i], part(out, i), go_sems.at[i]) for i in range(SLABS)]
    for load in loads:
        load.start()
    c = core_of()
    t = advance(z[c, :M, NB * CAP :], whole_gain(c, q0, h, g))[:, :M]
    th, tl = split2(t)
    w = jnp.concatenate([th, th, tl], axis=1)
    for i in range(SLABS):
        loads[i].wait()
        for j in range(0, SLAB, 8):
            turned = jnp.swapaxes(come[i, :, j : j + 8, :], 0, 1)
            rows = []
            for r in range(8):
                xh, xl = split2(turned[r])
                rows.append(dot(w, jnp.concatenate([xh, xl, xh], axis=0))[None])
            go[i, :, j : j + 8, :] = jnp.swapaxes(jnp.concatenate(rows, axis=0), 0, 1)
        stores[i].start()
    for store in stores:
        store.wait()


def place_kernel(order, owner, nv, r0, r1, r2, r3, out):
    high, low = split2(nv[...].T)
    tiles = iota((TILES, OBS), 0)
    slots = iota((CAP, OBS), 0).astype(F32)
    for k, rank in enumerate((r0, r1, r2, r3)):
        b = order[k]
        at = slice(CAP * k, CAP * k + CAP)
        hot = jnp.where(owner[pl.ds(b, 1), :] == tiles, 1.0, 0.0).astype(BF16)
        got = dot(jnp.concatenate([high[at], low[at]], axis=1), jnp.concatenate([hot, hot], axis=0))
        out[pl.ds(b, 1), :] = jnp.sum(jnp.where(rank[...] == slots, got, 0.0), axis=0, keepdims=True)


VMEM = pl.BlockSpec(memory_space=pltpu.VMEM)
SMEM = pl.BlockSpec(memory_space=pltpu.SMEM)
HBM = pl.BlockSpec(memory_space=pltpu.HBM)


def shape(*dims):
    return jax.ShapeDtypeStruct(dims, F32)


def swaps(pairs):
    return pairs + [(high, low) for low, high in pairs]


def local(ensemble, obs_value, obs_variance, obs_owner, obs_cell, obs_reach, batch_order):
    params = pltpu.CompilerParams(vmem_limit_bytes=32 * 2**20)
    call = functools.partial(pl.pallas_call, compiler_params=params)
    width, height = lax.axis_size("gx"), lax.axis_size("gy")
    both = ("gx", "gy")
    core = swaps([(x, x + 1) for x in range(0, width, 2)])
    chips = width // 2
    side_x = swaps([(2 * y + c, 2 * ((y + 1) % chips) + c) for c in range(2) for y in range(c, chips, 2)])
    side_y = swaps([
        (x * height + k, x * height + k + 1) for x in range(width) for k in range(x % 2, height - 1, 2)
    ] + [(x * height + k, (x + 2) * height + k) for x in range(1, width, 4) for k in (0, height - 1)])
    pay_shapes = (shape(2, ROWS // 2, 128), shape(ROWS // 2, 128))
    z_shape = shape(2, ROWS, NB * CAP + 128)
    row = pltpu.VMEM((NB, OBS), F32)
    row_i = pltpu.VMEM((NB, OBS), jnp.int32)
    own = call(
        init_kernel,
        out_shape=shape(ROWS, NB * CAP),
        in_specs=[HBM] * 7,
        out_specs=VMEM,
        scratch_shapes=[
            pltpu.SMEM((NB,), jnp.int32), row, row, row_i, row_i,
            pltpu.VMEM((NB, 8, OBS), jnp.int32), pltpu.VMEM((M, TX, TY), F32), pltpu.SemaphoreType.DMA((7,)),
        ],
        name="init",
    )(*(
        pltpu.with_memory_space_constraint(value, pltpu.HBM)
        for value in (
            batch_order, obs_value, obs_variance, obs_owner, obs_cell, jnp.swapaxes(obs_reach, 1, 2), ensemble
        )
    ))
    z, pay, edge = call(
        start_kernel,
        out_shape=(z_shape,) + pay_shapes,
        in_specs=[VMEM] * 2,
        out_specs=(VMEM,) * 3,
        name="start",
    )(own, lax.ppermute(own, "gx", core))
    ranks = []
    for k in range(NB):
        last = k + 1 == NB
        far = lax.ppermute(edge, "gx", side_x)
        if last:
            spread = jnp.broadcast_to(nv, (TILES, NB * CAP))
            everyone = lax.all_to_all(spread, both, 0, 0, tiled=True)
        sib_far = lax.ppermute(far, "gx", core)
        send = call(send_kernel, out_shape=shape(2, M, M), in_specs=[VMEM] * 3, out_specs=VMEM, name="send")(
            pay, far, sib_far
        )
        h = lax.ppermute(send, both, side_y)
        q0, rank = call(
            functools.partial(same_kernel, k),
            out_shape=(shape(2, M, M), shape(1, OBS)),
            in_specs=[SMEM] + [VMEM] * 4,
            out_specs=(VMEM, VMEM),
            name="same",
        )(batch_order, obs_owner, pay, far, sib_far)
        ranks.append(rank)
        h, q0 = lax.optimization_barrier((h, q0))
        g = lax.ppermute(h, "gx", core)
        if not last:
            wide = (shape(1, NB * CAP),) if k + 2 == NB else ()
            z, pay, edge, *rest = call(
                functools.partial(step_kernel, k + 1),
                out_shape=(z_shape,) + pay_shapes + wide,
                in_specs=[VMEM] * 4,
                out_specs=(VMEM,) * (3 + len(wide)),
                name="step",
            )(q0, h, g, z)
            if rest:
                nv = rest[0]
    slabs = pltpu.VMEM((SLABS, M, SLAB, TY), F32)
    state = call(
        final_kernel,
        out_shape=shape(M, LEV, TX, TY),
        in_specs=[VMEM] * 4 + [HBM],
        out_specs=HBM,
        scratch_shapes=[slabs, slabs, pltpu.SemaphoreType.DMA((SLABS,)), pltpu.SemaphoreType.DMA((SLABS,))],
        name="final",
    )(q0, h, g, z, pltpu.with_memory_space_constraint(ensemble, pltpu.HBM))
    state, everyone = lax.optimization_barrier((state, everyone))
    innovation = call(
        place_kernel,
        out_shape=shape(NB, OBS),
        in_specs=[SMEM] + [VMEM] * 6,
        out_specs=VMEM,
        name="place",
    )(batch_order, obs_owner, everyone, *ranks)
    return state, innovation


def solution(mesh):
    placed = (P(None, None, "gx", "gy"), P(), P(), P(), P(), P(), P())
    return jax.shard_map(
        local,
        mesh=mesh,
        in_specs=placed,
        out_specs=(P(None, None, "gx", "gy"), P()),
        check_vma=False,
    )
```

```python
import functools

import jax
import jax.numpy as jnp
from jax import lax
from jax.experimental import pallas as pl
from jax.experimental.pallas import tpu as pltpu
from jax.sharding import PartitionSpec as P

M = 80
LEV = 4
NB = 4
TX = 32
TY = 256
CAP = 64
OBS = 2048
TILES = 128
EPS = 1e-05
F32 = jnp.float32
BF16 = jnp.bfloat16
HIGH = lax.Precision.HIGHEST
SLAB = 16
PARTS = TX // SLAB
SLABS = LEV * PARTS

ROW_A = M
ROW_C = M + 1
ROW_W = M + 2
ROW_N = M + 11
ROWS = 96
TAPER = (0.25, 0.5, 0.25, 0.5, 1.0, 0.5, 0.25, 0.5, 0.25)


def split2(x):
    high = x.astype(BF16)
    return high, (x - high.astype(F32)).astype(BF16)


def split3(x):
    high = x.astype(BF16)
    rest = x - high.astype(F32)
    mid = rest.astype(BF16)
    return high, mid, (rest - mid.astype(F32)).astype(BF16)


def iota(shape, dim):
    return lax.broadcasted_iota(jnp.int32, shape, dim)


def dot(a, b, **kw):
    return jnp.dot(a, b, preferred_element_type=F32, **kw)


def dot_t(a, b, **kw):
    return lax.dot_general(a, b, (((1,), (1,)), ((), ())), preferred_element_type=F32, **kw)


def pack(rows):
    return jnp.concatenate([rows[: ROWS // 2], rows[ROWS // 2 :]], axis=1)


def unpack(packed):
    return jnp.concatenate([packed[:, :CAP], packed[:, CAP:]], axis=0)


def make_payload(prior, meta):
    valid = meta[0:1] > 0.5
    value = meta[1:2]
    variance = jnp.where(valid, meta[2:3], 1.0)
    center = jnp.sum(prior, axis=0, keepdims=True) / M
    deviation = prior - center
    spread = jnp.sum(deviation * deviation, axis=0, keepdims=True) / (M - 1)
    total = spread + variance
    miss = value - center
    normed = jnp.where(valid, miss / jnp.sqrt(total), 0.0)
    a = spread / total * miss
    c = jnp.sqrt(variance / total) - 1.0
    d = jnp.where(valid, 1.0 / ((M - 1) * (spread + EPS)), 0.0)
    rows = [deviation, a, c]
    for i in range(9):
        if i == 4:
            rows.append(d)
        else:
            at = 3 + (i if i < 4 else i - 1)
            rows.append(d * (meta[at : at + 1] * TAPER[i]))
    rows.append(jnp.zeros((ROWS - M - 11, CAP), F32))
    return pack(jnp.concatenate(rows, axis=0)), normed


def init_kernel(order_hbm, value_hbm, variance_hbm, owner_hbm, cell_hbm, reach_hbm, x_hbm, out,
                order, value, variance, owner, cell, reach, surface, sems):
    small = [
        pltpu.make_async_copy(source, target, sems.at[i])
        for i, (source, target) in enumerate([
            (order_hbm, order), (owner_hbm, owner), (cell_hbm, cell),
            (value_hbm, value), (variance_hbm, variance), (reach_hbm, reach),
        ])
    ]
    load = pltpu.make_async_copy(x_hbm.at[:, 0], surface, sems.at[6])
    for copy in small:
        copy.start()
    load.start()
    me = lax.axis_index("gx") * lax.axis_size("gy") + lax.axis_index("gy")
    small[0].wait()
    small[1].wait()
    owned = jnp.concatenate([owner[pl.ds(order[k], 1), :] for k in range(NB)], axis=0) == me
    ownf = jnp.where(owned, 1.0, 0.0)
    chunks = OBS // 128
    own64 = jnp.concatenate([ownf[:, 128 * c : 128 * c + 128] for c in range(chunks)], axis=0).astype(BF16)
    upper = jnp.where(iota((128, 128), 0) < iota((128, 128), 1), 1.0, 0.0).astype(BF16)
    rows = NB * chunks
    r0, r1 = iota((rows, rows), 0), iota((rows, rows), 1)
    before = jnp.where((r1 < r0) & (((r0 - r1) & (NB - 1)) == 0), 1.0, 0.0).astype(BF16)
    base = dot(dot(before, own64).astype(BF16), jnp.ones((128, 128), BF16))
    rank64 = dot(own64, upper) + base
    rank = jnp.concatenate([rank64[NB * c : NB * c + NB] for c in range(chunks)], axis=1)
    rank = jnp.where(owned, rank, -1.0)
    slots = iota((CAP, OBS), 0).astype(F32)
    for copy in small[2:]:
        copy.wait()
    metas = []
    for k in range(NB):
        b = order[k]
        hot = jnp.where(rank[k : k + 1] == slots, 1.0, 0.0).astype(BF16)
        where = cell[pl.ds(b, 1), :]
        vh, vm, vl = split3(value[pl.ds(b, 1), :])
        rh, rm, rl = split3(variance[pl.ds(b, 1), :])
        parts = [
            reach[b].astype(F32),
            lax.shift_right_logical(where, 8).astype(F32),
            (where & 255).astype(F32),
            vh.astype(F32), vm.astype(F32), vl.astype(F32),
            rh.astype(F32), rm.astype(F32), rl.astype(F32),
            jnp.ones((1, OBS), F32),
            jnp.zeros((15, OBS), F32),
        ]
        metas.append(dot_t(jnp.concatenate(parts, axis=0).astype(BF16), hot))
    got = jnp.concatenate(metas, axis=1)
    out[M:] = jnp.concatenate(
        [
            got[16:17],
            got[10:11] + got[11:12] + got[12:13],
            got[13:14] + got[14:15] + got[15:16],
            got[:8],
            jnp.zeros((5, NB * CAP), F32),
        ],
        axis=0,
    )
    hot_y = jnp.where(got[9:10] == iota((TY, NB * CAP), 0).astype(F32), 1.0, 0.0).astype(BF16)
    hot_x = jnp.where(got[8:9] == iota((TX, NB * CAP), 0).astype(F32), 1.0, 0.0)
    load.wait()
    group = 16
    for g in range(M // group):
        h, m, l = split3(surface[group * g : group * g + group].reshape(group * TX, TY))
        picked = dot(h, hot_y) + dot(m, hot_y) + dot(l, hot_y)
        out[group * g : group * g + group] = jnp.sum(
            picked.reshape(group, TX, NB * CAP) * hot_x[None], axis=1
        )


def core_of():
    return lax.rem(lax.axis_index("gx"), 2)


def edge(index, count):
    return (index == 0) | (index == count - 1)


def upward(index):
    return lax.rem(index + core_of(), 2) == 0


def emit(k, z, z_out, pay_out, edge_out, news_out=None):
    pays = []
    at = slice(CAP * k, CAP * k + CAP)
    news = []
    for t in range(2):
        pay, normed = make_payload(z[t][:M, at], z[t][M:, at])
        pay_out[t] = pay
        z_out[t, ROW_N : ROW_N + 1, at] = normed
        pays.append(pay)
        news.append(normed)
    edge_out[: ROWS // 2] = jnp.where(upward(lax.axis_index("gx") // 2), pays[1], pays[0])
    if news_out is not None:
        rows = [
            jnp.concatenate([z[t][ROW_N : ROW_N + 1, CAP * i : CAP * i + CAP] for t in range(2)], axis=1) for i in range(k)
        ]
        rows.append(jnp.concatenate(news, axis=1))
        rows.append(jnp.zeros((8 - NB, 2 * CAP), F32))
        block = jnp.concatenate(rows, axis=0)
        edge_out[ROWS // 2 :] = block
        news_out[...] = block


def start_kernel(own, sib, z_out, pay_out, edge_out):
    first = core_of() == 0
    mine, other = own[...], sib[...]
    z = [jnp.where(first, mine, other), jnp.where(first, other, mine)]
    unit = jnp.where(iota((ROWS, 128), 0) == iota((ROWS, 128), 1), 1.0, 0.0)
    unit = jnp.where(iota((ROWS, 128), 0) < M, unit, 0.0)
    for t in range(2):
        z_out[t, :, : NB * CAP] = z[t]
        z_out[t, :, NB * CAP :] = unit
    emit(0, z, z_out, pay_out, edge_out)


def right_side(rows):
    return rows[ROW_A : ROW_A + 1] + rows[ROW_C : ROW_C + 1] * rows[:M]


def gains(pay, far, sib_far, weight):
    y, chips = lax.axis_index("gx") // 2, lax.axis_size("gx") // 2
    up = upward(y)
    first = core_of() == 0
    ends = edge(y, chips)
    far = jnp.where(ends & jnp.logical_not(first), 0.0, far[: ROWS // 2])
    sib_far = jnp.where(ends & first, 0.0, sib_far[: ROWS // 2])
    blocks = [jnp.where(up, sib_far, far), pay[0], pay[1], jnp.where(up, far, sib_far)]
    blocks = [unpack(b) for b in blocks]
    rights = [right_side(b) for b in blocks]
    results = []
    for t in range(2):
        left = jnp.concatenate([blocks[t + i][:M] * weight(blocks[t + i], 1 - i) for i in range(3)], axis=1)
        right = jnp.concatenate(rights[t : t + 3], axis=1)
        results.append(dot_t(right, left, precision=HIGH))
    return results


def factor(rows, dx, dy):
    at = ROW_W + 3 * (dx + 1) + dy + 1
    return rows[at : at + 1]


def send_kernel(pay, far, sib_far, out):
    up = upward(lax.axis_index("gy"))
    both = gains(pay, far, sib_far, lambda rows, dx: jnp.where(up, factor(rows, dx, 1), factor(rows, dx, -1)))
    for t in range(2):
        out[t] = both[t]


def same_kernel(k, order, owner, pay, far, sib_far, out, rank_out):
    both = gains(pay, far, sib_far, lambda rows, dx: factor(rows, dx, 0))
    for t in range(2):
        out[t] = both[t]
    row = owner[pl.ds(order[k], 1), :]
    upper = jnp.where(iota((128, 128), 0) < iota((128, 128), 1), 1.0, 0.0).astype(BF16)
    tiles = iota((TILES, 128), 0)
    base = jnp.zeros((TILES, 1), F32)
    for c in range(OBS // 128):
        at = slice(128 * c, 128 * c + 128)
        hot = jnp.where(row[:, at] == tiles, 1.0, 0.0)
        rank = dot(hot.astype(BF16), upper) + base
        rank_out[:, at] = jnp.sum(hot * rank, axis=0, keepdims=True)
        base = base + jnp.sum(hot, axis=1, keepdims=True)


def same_last_kernel(k, order, owner, pay, far, sib_far, news, across, out, rank_out, column):
    first = core_of() == 0
    at = slice(ROWS // 2, ROWS // 2 + NB)
    mine, other = far[at], sib_far[at]
    column[0:NB] = news[:NB]
    column[NB : 2 * NB] = jnp.where(first, mine, other)
    column[2 * NB : 3 * NB] = across[:NB]
    column[3 * NB :] = jnp.where(first, other, mine)
    same_kernel(k, order, owner, pay, far, sib_far, out, rank_out)


def advance(z, gain):
    anomaly = z - jnp.sum(z, axis=0, keepdims=True) / M
    return z + dot(gain, anomaly, precision=HIGH)


def whole_gain(t, q0, h, g):
    first = core_of() == 0
    ends = edge(lax.axis_index("gy"), lax.axis_size("gy"))
    return q0[t] + jnp.where(ends & jnp.logical_not(first), 0.0, h[t]) + jnp.where(ends & first, 0.0, g[t])


def step_kernel(k, q0, h, g, z, z_out, pay_out, edge_out, news_out=None):
    new = []
    for t in range(2):
        moved = advance(z[t, :M], whole_gain(t, q0, h, g))
        z_out[t, :M] = moved
        z_out[t, M:] = z[t, M:]
        new.append(jnp.concatenate([moved, z[t, M:]], axis=0))
    emit(k, new, z_out, pay_out, edge_out, news_out)


def final_kernel(q0, h, g, z, x, out, come, go, come_sems, go_sems):
    def part(ref, i):
        return ref.at[:, i // PARTS, pl.ds((i % PARTS) * SLAB, SLAB), :]

    loads = [pltpu.make_async_copy(part(x, i), come.at[i], come_sems.at[i]) for i in range(SLABS)]
    stores = [pltpu.make_async_copy(go.at[i], part(out, i), go_sems.at[i]) for i in range(SLABS)]
    for load in loads:
        load.start()
    c = core_of()
    t = advance(z[c, :M, NB * CAP :], whole_gain(c, q0, h, g))[:, :M]
    th, tl = split2(t)
    w = jnp.concatenate([th, th, tl], axis=1)
    for i in range(SLABS):
        loads[i].wait()
        for j in range(0, SLAB, 8):
            turned = jnp.swapaxes(come[i, :, j : j + 8, :], 0, 1)
            rows = []
            for r in range(8):
                xh, xl = split2(turned[r])
                rows.append(dot(w, jnp.concatenate([xh, xl, xh], axis=0))[None])
            go[i, :, j : j + 8, :] = jnp.swapaxes(jnp.concatenate(rows, axis=0), 0, 1)
        stores[i].start()
    for store in stores:
        store.wait()


def place_kernel(order, owner, n0, n1, n2, n3, r0, r1, r2, r3, out):
    me = lax.axis_index("gx") * lax.axis_size("gy") + lax.axis_index("gy")
    chips = iota((TILES // 2, OBS), 0)
    seats = iota((2 * CAP, OBS), 0)
    for k, rank in enumerate((r0, r1, r2, r3)):
        b = order[k]
        tile = owner[pl.ds(b, 1), :]
        away = tile ^ me
        block = ((away >> 2) & 3) * 16 + (away & 3) * 4 + ((away >> 5) & 3)
        hot = jnp.where(block == chips, 1.0, 0.0).astype(BF16)
        rows = jnp.concatenate([n[pl.ds(k, 16, stride=NB), :] for n in (n0, n1, n2, n3)], axis=0)
        high, low = split2(rows.T)
        got = dot(jnp.concatenate([high, low], axis=1), jnp.concatenate([hot, hot], axis=0))
        seat = ((tile >> 4) & 1) * CAP + rank[...].astype(jnp.int32)
        out[pl.ds(b, 1), :] = jnp.sum(jnp.where(seat == seats, got, 0.0), axis=0, keepdims=True)


VMEM = pl.BlockSpec(memory_space=pltpu.VMEM)
SMEM = pl.BlockSpec(memory_space=pltpu.SMEM)
HBM = pl.BlockSpec(memory_space=pltpu.HBM)


def shape(*dims):
    return jax.ShapeDtypeStruct(dims, F32)


def swaps(pairs):
    return pairs + [(high, low) for low, high in pairs]


def local(ensemble, obs_value, obs_variance, obs_owner, obs_cell, obs_reach, batch_order):
    params = pltpu.CompilerParams(vmem_limit_bytes=32 * 2**20)
    call = functools.partial(pl.pallas_call, compiler_params=params)
    width, height = lax.axis_size("gx"), lax.axis_size("gy")
    both = ("gx", "gy")
    core = swaps([(x, x + 1) for x in range(0, width, 2)])
    chips = width // 2
    side_x = swaps([(2 * y + c, 2 * ((y + 1) % chips) + c) for c in range(2) for y in range(c, chips, 2)])
    side_y = swaps([
        (x * height + k, x * height + k + 1) for x in range(width) for k in range(x % 2, height - 1, 2)
    ] + [(x * height + k, (x + 2) * height + k) for x in range(1, width, 4) for k in (0, height - 1)])
    pay_shapes = (shape(2, ROWS // 2, 128), shape(ROWS // 2, 128))
    z_shape = shape(2, ROWS, NB * CAP + 128)
    row = pltpu.VMEM((NB, OBS), F32)
    row_i = pltpu.VMEM((NB, OBS), jnp.int32)
    own = call(
        init_kernel,
        out_shape=shape(ROWS, NB * CAP),
        in_specs=[HBM] * 7,
        out_specs=VMEM,
        scratch_shapes=[
            pltpu.SMEM((NB,), jnp.int32), row, row, row_i, row_i,
            pltpu.VMEM((NB, 8, OBS), jnp.int32), pltpu.VMEM((M, TX, TY), F32), pltpu.SemaphoreType.DMA((7,)),
        ],
        name="init",
    )(*(
        pltpu.with_memory_space_constraint(value, pltpu.HBM)
        for value in (
            batch_order, obs_value, obs_variance, obs_owner, obs_cell, jnp.swapaxes(obs_reach, 1, 2), ensemble
        )
    ))
    z, pay, edge = call(
        start_kernel,
        out_shape=(z_shape,) + pay_shapes,
        in_specs=[VMEM] * 2,
        out_specs=(VMEM,) * 3,
        name="start",
    )(own, lax.ppermute(own, "gx", core))
    ranks = []
    xor = lambda value, bits: lax.ppermute(value, both, [(q, q ^ bits) for q in range(width * height)])
    for k in range(NB):
        last = k + 1 == NB
        far = lax.ppermute(edge, "gx", side_x)
        if last:
            across = xor(news, 2 * 32)
        sib_far = lax.ppermute(far, "gx", core)
        send = call(send_kernel, out_shape=shape(2, M, M), in_specs=[VMEM] * 3, out_specs=VMEM, name="send")(
            pay, far, sib_far
        )
        send, sib_far = lax.optimization_barrier((send, sib_far))
        h = lax.ppermute(send, both, side_y)
        extra = ((news, across), (shape(4 * NB, 128),)) if last else ((), ())
        q0, rank, *rest = call(
            functools.partial(same_last_kernel if last else same_kernel, k),
            out_shape=(shape(2, M, M), shape(1, OBS)) + extra[1],
            in_specs=[SMEM] + [VMEM] * (4 + len(extra[0])),
            out_specs=(VMEM,) * (2 + len(extra[1])),
            name="same",
        )(batch_order, obs_owner, pay, far, sib_far, *extra[0])
        if last:
            column = rest[0]
            plane = jnp.concatenate([column] + [xor(column, j) for j in range(1, 4)], axis=0)
        ranks.append(rank)
        h, q0 = lax.optimization_barrier((h, q0))
        g = lax.ppermute(h, "gx", core)
        if last:
            planes = [plane] + [xor(plane, 4 * j) for j in range(1, 4)]
        else:
            tail = k + 2 == NB
            edge_shape = (shape(ROWS // 2 + 8, 128), shape(8, 128)) if tail else pay_shapes[1:]
            z, pay, edge, *rest = call(
                functools.partial(step_kernel, k + 1),
                out_shape=(z_shape, pay_shapes[0]) + edge_shape,
                in_specs=[VMEM] * 4,
                out_specs=(VMEM,) * (4 if tail else 3),
                name="step",
            )(q0, h, g, z)
            if tail:
                news = rest[0]
    slabs = pltpu.VMEM((SLABS, M, SLAB, TY), F32)
    state = call(
        final_kernel,
        out_shape=shape(M, LEV, TX, TY),
        in_specs=[VMEM] * 4 + [HBM],
        out_specs=HBM,
        scratch_shapes=[slabs, slabs, pltpu.SemaphoreType.DMA((SLABS,)), pltpu.SemaphoreType.DMA((SLABS,))],
        cost_estimate=pl.CostEstimate(flops=6 * M * M * LEV * TX * TY, bytes_accessed=8 * M * LEV * TX * TY, transcendentals=0),
        name="final",
    )(q0, h, g, z, pltpu.with_memory_space_constraint(ensemble, pltpu.HBM))
    state, planes = lax.optimization_barrier((state, planes))
    innovation = call(
        place_kernel,
        out_shape=shape(NB, OBS),
        in_specs=[SMEM] + [VMEM] * 9,
        out_specs=VMEM,
        name="place",
    )(batch_order, obs_owner, *planes, *ranks)
    return state, innovation


def solution(mesh):
    placed = (P(None, None, "gx", "gy"), P(), P(), P(), P(), P(), P())
    return jax.shard_map(
        local,
        mesh=mesh,
        in_specs=placed,
        out_specs=(P(None, None, "gx", "gy"), P()),
        check_vma=False,
    )
```

```python
import functools

import jax
import jax.numpy as jnp
from jax import lax
from jax.experimental import pallas as pl
from jax.experimental.pallas import tpu as pltpu
from jax.sharding import PartitionSpec as P

M = 80
LEV = 4
NB = 4
TX = 32
TY = 256
CAP = 64
OBS = 2048
TILES = 128
EPS = 1e-05
F32 = jnp.float32
BF16 = jnp.bfloat16
HIGH = lax.Precision.HIGHEST
SLAB = 16
PARTS = TX // SLAB
SLABS = LEV * PARTS

ROW_A = M
ROW_C = M + 1
ROW_W = M + 2
ROW_N = M + 11
ROWS = 96
TAPER = (0.25, 0.5, 0.25, 0.5, 1.0, 0.5, 0.25, 0.5, 0.25)


def split2(x):
    high = x.astype(BF16)
    return high, (x - high.astype(F32)).astype(BF16)


def split3(x):
    high = x.astype(BF16)
    rest = x - high.astype(F32)
    mid = rest.astype(BF16)
    return high, mid, (rest - mid.astype(F32)).astype(BF16)


def iota(shape, dim):
    return lax.broadcasted_iota(jnp.int32, shape, dim)


def dot(a, b, **kw):
    return jnp.dot(a, b, preferred_element_type=F32, **kw)


def dot_t(a, b, **kw):
    return lax.dot_general(a, b, (((1,), (1,)), ((), ())), preferred_element_type=F32, **kw)


def pack(rows):
    return jnp.concatenate([rows[: ROWS // 2], rows[ROWS // 2 :]], axis=1)


def unpack(packed):
    return jnp.concatenate([packed[:, :CAP], packed[:, CAP:]], axis=0)


def make_payload(prior, meta):
    valid = meta[0:1] > 0.5
    value = meta[1:2]
    variance = jnp.where(valid, meta[2:3], 1.0)
    center = jnp.sum(prior, axis=0, keepdims=True) / M
    deviation = prior - center
    spread = jnp.sum(deviation * deviation, axis=0, keepdims=True) / (M - 1)
    total = spread + variance
    miss = value - center
    normed = jnp.where(valid, miss / jnp.sqrt(total), 0.0)
    a = spread / total * miss
    c = jnp.sqrt(variance / total) - 1.0
    d = jnp.where(valid, 1.0 / ((M - 1) * (spread + EPS)), 0.0)
    rows = [deviation, a, c]
    for i in range(9):
        if i == 4:
            rows.append(d)
        else:
            at = 3 + (i if i < 4 else i - 1)
            rows.append(d * (meta[at : at + 1] * TAPER[i]))
    rows.append(jnp.zeros((ROWS - M - 11, CAP), F32))
    return pack(jnp.concatenate(rows, axis=0)), normed


def init_kernel(order_hbm, value_hbm, variance_hbm, owner_hbm, cell_hbm, reach_hbm, x_hbm, out,
                order, value, variance, owner, cell, reach, surface, sems):
    small = [
        pltpu.make_async_copy(source, target, sems.at[i])
        for i, (source, target) in enumerate([
            (order_hbm, order), (owner_hbm, owner), (cell_hbm, cell),
            (value_hbm, value), (variance_hbm, variance), (reach_hbm, reach),
        ])
    ]
    load = pltpu.make_async_copy(x_hbm.at[:, 0], surface, sems.at[6])
    for copy in small:
        copy.start()
    load.start()
    me = lax.axis_index("gx") * lax.axis_size("gy") + lax.axis_index("gy")
    small[0].wait()
    small[1].wait()
    owned = jnp.concatenate([owner[pl.ds(order[k], 1), :] for k in range(NB)], axis=0) == me
    ownf = jnp.where(owned, 1.0, 0.0)
    chunks = OBS // 128
    own64 = jnp.concatenate([ownf[:, 128 * c : 128 * c + 128] for c in range(chunks)], axis=0).astype(BF16)
    upper = jnp.where(iota((128, 128), 0) < iota((128, 128), 1), 1.0, 0.0).astype(BF16)
    rows = NB * chunks
    r0, r1 = iota((rows, rows), 0), iota((rows, rows), 1)
    before = jnp.where((r1 < r0) & (((r0 - r1) & (NB - 1)) == 0), 1.0, 0.0).astype(BF16)
    base = dot(dot(before, own64).astype(BF16), jnp.ones((128, 128), BF16))
    rank64 = dot(own64, upper) + base
    rank = jnp.concatenate([rank64[NB * c : NB * c + NB] for c in range(chunks)], axis=1)
    rank = jnp.where(owned, rank, -1.0)
    slots = iota((CAP, OBS), 0).astype(F32)
    for copy in small[2:]:
        copy.wait()
    metas = []
    for k in range(NB):
        b = order[k]
        hot = jnp.where(rank[k : k + 1] == slots, 1.0, 0.0).astype(BF16)
        where = cell[pl.ds(b, 1), :]
        vh, vm, vl = split3(value[pl.ds(b, 1), :])
        rh, rm, rl = split3(variance[pl.ds(b, 1), :])
        parts = [
            reach[b].astype(F32),
            lax.shift_right_logical(where, 8).astype(F32),
            (where & 255).astype(F32),
            vh.astype(F32), vm.astype(F32), vl.astype(F32),
            rh.astype(F32), rm.astype(F32), rl.astype(F32),
            jnp.ones((1, OBS), F32),
            jnp.zeros((15, OBS), F32),
        ]
        metas.append(dot_t(jnp.concatenate(parts, axis=0).astype(BF16), hot))
    got = jnp.concatenate(metas, axis=1)
    out[M:] = jnp.concatenate(
        [
            got[16:17],
            got[10:11] + got[11:12] + got[12:13],
            got[13:14] + got[14:15] + got[15:16],
            got[:8],
            jnp.zeros((5, NB * CAP), F32),
        ],
        axis=0,
    )
    hot_y = jnp.where(got[9:10] == iota((TY, NB * CAP), 0).astype(F32), 1.0, 0.0).astype(BF16)
    hot_x = jnp.where(got[8:9] == iota((TX, NB * CAP), 0).astype(F32), 1.0, 0.0)
    load.wait()
    group = 16
    for g in range(M // group):
        h, m, l = split3(surface[group * g : group * g + group].reshape(group * TX, TY))
        picked = dot(h, hot_y) + dot(m, hot_y) + dot(l, hot_y)
        out[group * g : group * g + group] = jnp.sum(
            picked.reshape(group, TX, NB * CAP) * hot_x[None], axis=1
        )


def core_of():
    return lax.rem(lax.axis_index("gx"), 2)


def edge(index, count):
    return (index == 0) | (index == count - 1)


def upward(index):
    return lax.rem(index + core_of(), 2) == 0


def emit(k, z, z_out, pay_out, edge_out, nv_out=None):
    pays = []
    at = slice(CAP * k, CAP * k + CAP)
    news = []
    for t in range(2):
        pay, normed = make_payload(z[t][:M, at], z[t][M:, at])
        pay_out[t] = pay
        z_out[t, ROW_N : ROW_N + 1, at] = normed
        pays.append(pay)
        news.append(normed)
    edge_out[...] = jnp.where(upward(lax.axis_index("gx") // 2), pays[1], pays[0])
    if nv_out is not None:
        first = core_of() == 0
        past = slice(0, CAP * k)
        nv_out[:, past] = jnp.where(first, z[0][ROW_N : ROW_N + 1, past], z[1][ROW_N : ROW_N + 1, past])
        nv_out[:, at] = jnp.where(first, news[0], news[1])


def start_kernel(own, sib, z_out, pay_out, edge_out):
    first = core_of() == 0
    mine, other = own[...], sib[...]
    z = [jnp.where(first, mine, other), jnp.where(first, other, mine)]
    unit = jnp.where(iota((ROWS, 128), 0) == iota((ROWS, 128), 1), 1.0, 0.0)
    unit = jnp.where(iota((ROWS, 128), 0) < M, unit, 0.0)
    for t in range(2):
        z_out[t, :, : NB * CAP] = z[t]
        z_out[t, :, NB * CAP :] = unit
    emit(0, z, z_out, pay_out, edge_out)


def right_side(rows):
    return rows[ROW_A : ROW_A + 1] + rows[ROW_C : ROW_C + 1] * rows[:M]


def gains(pay, far, sib_far, weight):
    y, chips = lax.axis_index("gx") // 2, lax.axis_size("gx") // 2
    up = upward(y)
    first = core_of() == 0
    ends = edge(y, chips)
    far = jnp.where(ends & jnp.logical_not(first), 0.0, far[...])
    sib_far = jnp.where(ends & first, 0.0, sib_far[...])
    blocks = [jnp.where(up, sib_far, far), pay[0], pay[1], jnp.where(up, far, sib_far)]
    blocks = [unpack(b) for b in blocks]
    rights = [right_side(b) for b in blocks]
    results = []
    for t in range(2):
        left = jnp.concatenate([blocks[t + i][:M] * weight(blocks[t + i], 1 - i) for i in range(3)], axis=1)
        right = jnp.concatenate(rights[t : t + 3], axis=1)
        results.append(dot_t(right, left, precision=HIGH))
    return results


def factor(rows, dx, dy):
    at = ROW_W + 3 * (dx + 1) + dy + 1
    return rows[at : at + 1]


def send_kernel(pay, far, sib_far, out):
    up = upward(lax.axis_index("gy"))
    both = gains(pay, far, sib_far, lambda rows, dx: jnp.where(up, factor(rows, dx, 1), factor(rows, dx, -1)))
    for t in range(2):
        out[t] = both[t]


def same_kernel(k, order, owner, pay, far, sib_far, out, rank_out):
    both = gains(pay, far, sib_far, lambda rows, dx: factor(rows, dx, 0))
    for t in range(2):
        out[t] = both[t]
    row = owner[pl.ds(order[k], 1), :]
    upper = jnp.where(iota((128, 128), 0) < iota((128, 128), 1), 1.0, 0.0).astype(BF16)
    tiles = iota((TILES, 128), 0)
    base = jnp.zeros((TILES, 1), F32)
    for c in range(OBS // 128):
        at = slice(128 * c, 128 * c + 128)
        hot = jnp.where(row[:, at] == tiles, 1.0, 0.0)
        rank = dot(hot.astype(BF16), upper) + base
        rank_out[:, at] = jnp.sum(hot * rank, axis=0, keepdims=True)
        base = base + jnp.sum(hot, axis=1, keepdims=True)


def advance(z, gain):
    anomaly = z - jnp.sum(z, axis=0, keepdims=True) / M
    return z + dot(gain, anomaly, precision=HIGH)


def whole_gain(t, q0, h, g):
    first = core_of() == 0
    ends = edge(lax.axis_index("gy"), lax.axis_size("gy"))
    return q0[t] + jnp.where(ends & jnp.logical_not(first), 0.0, h[t]) + jnp.where(ends & first, 0.0, g[t])


def step_kernel(k, q0, h, g, z, z_out, pay_out, edge_out, nv_out=None):
    new = []
    for t in range(2):
        moved = advance(z[t, :M], whole_gain(t, q0, h, g))
        z_out[t, :M] = moved
        z_out[t, M:] = z[t, M:]
        new.append(jnp.concatenate([moved, z[t, M:]], axis=0))
    emit(k, new, z_out, pay_out, edge_out, nv_out)


def final_kernel(q0, h, g, z, x, out, come, go, come_sems, go_sems):
    def part(ref, i):
        return ref.at[:, i // PARTS, pl.ds((i % PARTS) * SLAB, SLAB), :]

    loads = [pltpu.make_async_copy(part(x, i), come.at[i], come_sems.at[i]) for i in range(SLABS)]
    stores = [pltpu.make_async_copy(go.at[i], part(out, i), go_sems.at[i]) for i in range(SLABS)]
    for load in loads:
        load.start()
    c = core_of()
    t = advance(z[c, :M, NB * CAP :], whole_gain(c, q0, h, g))[:, :M]
    th, tl = split2(t)
    w = jnp.concatenate([th, th, tl], axis=1)
    for i in range(SLABS):
        loads[i].wait()
        for j in range(0, SLAB, 8):
            turned = jnp.swapaxes(come[i, :, j : j + 8, :], 0, 1)
            rows = []
            for r in range(8):
                xh, xl = split2(turned[r])
                rows.append(dot(w, jnp.concatenate([xh, xl, xh], axis=0))[None])
            go[i, :, j : j + 8, :] = jnp.swapaxes(jnp.concatenate(rows, axis=0), 0, 1)
        stores[i].start()
    for store in stores:
        store.wait()


def place_kernel(order, owner, nv, r0, r1, r2, r3, out):
    high, low = split2(nv[...].T)
    tiles = iota((TILES, OBS), 0)
    slots = iota((CAP, OBS), 0).astype(F32)
    for k, rank in enumerate((r0, r1, r2, r3)):
        b = order[k]
        at = slice(CAP * k, CAP * k + CAP)
        hot = jnp.where(owner[pl.ds(b, 1), :] == tiles, 1.0, 0.0).astype(BF16)
        got = dot(jnp.concatenate([high[at], low[at]], axis=1), jnp.concatenate([hot, hot], axis=0))
        out[pl.ds(b, 1), :] = jnp.sum(jnp.where(rank[...] == slots, got, 0.0), axis=0, keepdims=True)


VMEM = pl.BlockSpec(memory_space=pltpu.VMEM)
SMEM = pl.BlockSpec(memory_space=pltpu.SMEM)
HBM = pl.BlockSpec(memory_space=pltpu.HBM)


def shape(*dims):
    return jax.ShapeDtypeStruct(dims, F32)


def swaps(pairs):
    return pairs + [(high, low) for low, high in pairs]


def local(ensemble, obs_value, obs_variance, obs_owner, obs_cell, obs_reach, batch_order):
    params = pltpu.CompilerParams(vmem_limit_bytes=32 * 2**20)
    call = functools.partial(pl.pallas_call, compiler_params=params)
    width, height = lax.axis_size("gx"), lax.axis_size("gy")
    both = ("gx", "gy")
    core = swaps([(x, x + 1) for x in range(0, width, 2)])
    chips = width // 2
    side_x = swaps([(2 * y + c, 2 * ((y + 1) % chips) + c) for c in range(2) for y in range(c, chips, 2)])
    side_y = swaps([
        (x * height + k, x * height + k + 1) for x in range(width) for k in range(x % 2, height - 1, 2)
    ] + [(x * height + k, (x + 2) * height + k) for x in range(1, width, 4) for k in (0, height - 1)])
    pay_shapes = (shape(2, ROWS // 2, 128), shape(ROWS // 2, 128))
    z_shape = shape(2, ROWS, NB * CAP + 128)
    row = pltpu.VMEM((NB, OBS), F32)
    row_i = pltpu.VMEM((NB, OBS), jnp.int32)
    own = call(
        init_kernel,
        out_shape=shape(ROWS, NB * CAP),
        in_specs=[HBM] * 7,
        out_specs=VMEM,
        scratch_shapes=[
            pltpu.SMEM((NB,), jnp.int32), row, row, row_i, row_i,
            pltpu.VMEM((NB, 8, OBS), jnp.int32), pltpu.VMEM((M, TX, TY), F32), pltpu.SemaphoreType.DMA((7,)),
        ],
        name="init",
    )(*(
        pltpu.with_memory_space_constraint(value, pltpu.HBM)
        for value in (
            batch_order, obs_value, obs_variance, obs_owner, obs_cell, jnp.swapaxes(obs_reach, 1, 2), ensemble
        )
    ))
    z, pay, edge = call(
        start_kernel,
        out_shape=(z_shape,) + pay_shapes,
        in_specs=[VMEM] * 2,
        out_specs=(VMEM,) * 3,
        name="start",
    )(own, lax.ppermute(own, "gx", core))
    ranks = []
    for k in range(NB):
        last = k + 1 == NB
        far = lax.ppermute(edge, "gx", side_x)
        sib_far = lax.ppermute(far, "gx", core)
        send = call(send_kernel, out_shape=shape(2, M, M), in_specs=[VMEM] * 3, out_specs=VMEM, name="send")(
            pay, far, sib_far
        )
        h = lax.ppermute(send, both, side_y)
        q0, rank = call(
            functools.partial(same_kernel, k),
            out_shape=(shape(2, M, M), shape(1, OBS)),
            in_specs=[SMEM] + [VMEM] * 4,
            out_specs=(VMEM, VMEM),
            name="same",
        )(batch_order, obs_owner, pay, far, sib_far)
        ranks.append(rank)
        if last:
            h, q0, nv = lax.optimization_barrier((h, q0, nv))
            spread = jnp.broadcast_to(nv, (TILES, NB * CAP))
            everyone = lax.all_to_all(spread, both, 0, 0, tiled=True)
        else:
            h, q0 = lax.optimization_barrier((h, q0))
        g = lax.ppermute(h, "gx", core)
        if not last:
            wide = (shape(1, NB * CAP),) if k + 2 == NB else ()
            z, pay, edge, *rest = call(
                functools.partial(step_kernel, k + 1),
                out_shape=(z_shape,) + pay_shapes + wide,
                in_specs=[VMEM] * 4,
                out_specs=(VMEM,) * (3 + len(wide)),
                name="step",
            )(q0, h, g, z)
            if rest:
                nv = rest[0]
    slabs = pltpu.VMEM((SLABS, M, SLAB, TY), F32)
    state = call(
        final_kernel,
        out_shape=shape(M, LEV, TX, TY),
        in_specs=[VMEM] * 4 + [HBM],
        out_specs=HBM,
        scratch_shapes=[slabs, slabs, pltpu.SemaphoreType.DMA((SLABS,)), pltpu.SemaphoreType.DMA((SLABS,))],
        cost_estimate=pl.CostEstimate(flops=6 * M * M * LEV * TX * TY, bytes_accessed=8 * M * LEV * TX * TY, transcendentals=0),
        name="final",
    )(q0, h, g, z, pltpu.with_memory_space_constraint(ensemble, pltpu.HBM))
    state, everyone = lax.optimization_barrier((state, everyone))
    innovation = call(
        place_kernel,
        out_shape=shape(NB, OBS),
        in_specs=[SMEM] + [VMEM] * 6,
        out_specs=VMEM,
        name="place",
    )(batch_order, obs_owner, everyone, *ranks)
    return state, innovation


def solution(mesh):
    placed = (P(None, None, "gx", "gy"), P(), P(), P(), P(), P(), P())
    return jax.shard_map(
        local,
        mesh=mesh,
        in_specs=placed,
        out_specs=(P(None, None, "gx", "gy"), P()),
        check_vma=False,
    )
```

```python
import functools

import jax
import jax.numpy as jnp
from jax import lax
from jax.experimental import pallas as pl
from jax.experimental.pallas import tpu as pltpu
from jax.sharding import PartitionSpec as P

M = 80
LEV = 4
NB = 4
TX = 32
TY = 256
CAP = 64
OBS = 2048
TILES = 128
EPS = 1e-05
F32 = jnp.float32
BF16 = jnp.bfloat16
HIGH = lax.Precision.HIGHEST
SLAB = 16
PARTS = TX // SLAB
SLABS = LEV * PARTS

ROW_A = M
ROW_C = M + 1
ROW_W = M + 2
ROW_N = M + 11
ROWS = 96
TAPER = (0.25, 0.5, 0.25, 0.5, 1.0, 0.5, 0.25, 0.5, 0.25)


def split2(x):
    high = x.astype(BF16)
    return high, (x - high.astype(F32)).astype(BF16)


def split3(x):
    high = x.astype(BF16)
    rest = x - high.astype(F32)
    mid = rest.astype(BF16)
    return high, mid, (rest - mid.astype(F32)).astype(BF16)


def iota(shape, dim):
    return lax.broadcasted_iota(jnp.int32, shape, dim)


def dot(a, b, **kw):
    return jnp.dot(a, b, preferred_element_type=F32, **kw)


def dot_t(a, b, **kw):
    return lax.dot_general(a, b, (((1,), (1,)), ((), ())), preferred_element_type=F32, **kw)


def pack(rows):
    return jnp.concatenate([rows[: ROWS // 2], rows[ROWS // 2 :]], axis=1)


def unpack(packed):
    return jnp.concatenate([packed[:, :CAP], packed[:, CAP:]], axis=0)


def make_payload(prior, meta):
    valid = meta[0:1] > 0.5
    value = meta[1:2]
    variance = jnp.where(valid, meta[2:3], 1.0)
    center = jnp.sum(prior, axis=0, keepdims=True) / M
    deviation = prior - center
    spread = jnp.sum(deviation * deviation, axis=0, keepdims=True) / (M - 1)
    total = spread + variance
    miss = value - center
    normed = jnp.where(valid, miss / jnp.sqrt(total), 0.0)
    a = spread / total * miss
    c = jnp.sqrt(variance / total) - 1.0
    d = jnp.where(valid, 1.0 / ((M - 1) * (spread + EPS)), 0.0)
    rows = [deviation, a, c]
    for i in range(9):
        if i == 4:
            rows.append(d)
        else:
            at = 3 + (i if i < 4 else i - 1)
            rows.append(d * (meta[at : at + 1] * TAPER[i]))
    rows.append(jnp.zeros((ROWS - M - 11, CAP), F32))
    return pack(jnp.concatenate(rows, axis=0)), normed


def init_kernel(order_hbm, value_hbm, variance_hbm, owner_hbm, cell_hbm, reach_hbm, x_hbm, out,
                order, value, variance, owner, cell, reach, surface, sems):
    small = [
        pltpu.make_async_copy(source, target, sems.at[i])
        for i, (source, target) in enumerate([
            (order_hbm, order), (owner_hbm, owner), (cell_hbm, cell),
            (value_hbm, value), (variance_hbm, variance), (reach_hbm, reach),
        ])
    ]
    load = pltpu.make_async_copy(x_hbm.at[:, 0], surface, sems.at[6])
    for copy in small:
        copy.start()
    load.start()
    me = lax.axis_index("gx") * lax.axis_size("gy") + lax.axis_index("gy")
    small[0].wait()
    small[1].wait()
    owned = jnp.concatenate([owner[pl.ds(order[k], 1), :] for k in range(NB)], axis=0) == me
    ownf = jnp.where(owned, 1.0, 0.0)
    chunks = OBS // 128
    own64 = jnp.concatenate([ownf[:, 128 * c : 128 * c + 128] for c in range(chunks)], axis=0).astype(BF16)
    upper = jnp.where(iota((128, 128), 0) < iota((128, 128), 1), 1.0, 0.0).astype(BF16)
    rows = NB * chunks
    r0, r1 = iota((rows, rows), 0), iota((rows, rows), 1)
    before = jnp.where((r1 < r0) & (((r0 - r1) & (NB - 1)) == 0), 1.0, 0.0).astype(BF16)
    base = dot(dot(before, own64).astype(BF16), jnp.ones((128, 128), BF16))
    rank64 = dot(own64, upper) + base
    rank = jnp.concatenate([rank64[NB * c : NB * c + NB] for c in range(chunks)], axis=1)
    rank = jnp.where(owned, rank, -1.0)
    slots = iota((CAP, OBS), 0).astype(F32)
    for copy in small[2:]:
        copy.wait()
    metas = []
    for k in range(NB):
        b = order[k]
        hot = jnp.where(rank[k : k + 1] == slots, 1.0, 0.0).astype(BF16)
        where = cell[pl.ds(b, 1), :]
        vh, vm, vl = split3(value[pl.ds(b, 1), :])
        rh, rm, rl = split3(variance[pl.ds(b, 1), :])
        parts = [
            reach[b].astype(F32),
            lax.shift_right_logical(where, 8).astype(F32),
            (where & 255).astype(F32),
            vh.astype(F32), vm.astype(F32), vl.astype(F32),
            rh.astype(F32), rm.astype(F32), rl.astype(F32),
            jnp.ones((1, OBS), F32),
            jnp.zeros((15, OBS), F32),
        ]
        metas.append(dot_t(jnp.concatenate(parts, axis=0).astype(BF16), hot))
    got = jnp.concatenate(metas, axis=1)
    out[M:] = jnp.concatenate(
        [
            got[16:17],
            got[10:11] + got[11:12] + got[12:13],
            got[13:14] + got[14:15] + got[15:16],
            got[:8],
            jnp.zeros((5, NB * CAP), F32),
        ],
        axis=0,
    )
    hot_y = jnp.where(got[9:10] == iota((TY, NB * CAP), 0).astype(F32), 1.0, 0.0).astype(BF16)
    hot_x = jnp.where(got[8:9] == iota((TX, NB * CAP), 0).astype(F32), 1.0, 0.0)
    load.wait()
    group = 16
    for g in range(M // group):
        h, m, l = split3(surface[group * g : group * g + group].reshape(group * TX, TY))
        picked = dot(h, hot_y) + dot(m, hot_y) + dot(l, hot_y)
        out[group * g : group * g + group] = jnp.sum(
            picked.reshape(group, TX, NB * CAP) * hot_x[None], axis=1
        )


def core_of():
    return lax.rem(lax.axis_index("gx"), 2)


def edge(index, count):
    return (index == 0) | (index == count - 1)


def upward(index):
    return lax.rem(index + core_of(), 2) == 0


def emit(k, z, z_out, pay_out, edge_out, nv_out=None):
    pays = []
    at = slice(CAP * k, CAP * k + CAP)
    news = []
    for t in range(2):
        pay, normed = make_payload(z[t][:M, at], z[t][M:, at])
        pay_out[t] = pay
        z_out[t, ROW_N : ROW_N + 1, at] = normed
        pays.append(pay)
        news.append(normed)
    edge_out[...] = jnp.where(upward(lax.axis_index("gx") // 2), pays[1], pays[0])
    if nv_out is not None:
        first = core_of() == 0
        past = slice(0, CAP * k)
        nv_out[:, past] = jnp.where(first, z[0][ROW_N : ROW_N + 1, past], z[1][ROW_N : ROW_N + 1, past])
        nv_out[:, at] = jnp.where(first, news[0], news[1])


def start_kernel(own, sib, z_out, pay_out, edge_out):
    first = core_of() == 0
    mine, other = own[...], sib[...]
    z = [jnp.where(first, mine, other), jnp.where(first, other, mine)]
    unit = jnp.where(iota((ROWS, 128), 0) == iota((ROWS, 128), 1), 1.0, 0.0)
    unit = jnp.where(iota((ROWS, 128), 0) < M, unit, 0.0)
    for t in range(2):
        z_out[t, :, : NB * CAP] = z[t]
        z_out[t, :, NB * CAP :] = unit
    emit(0, z, z_out, pay_out, edge_out)


def right_side(rows):
    return rows[ROW_A : ROW_A + 1] + rows[ROW_C : ROW_C + 1] * rows[:M]


def gains(pay, far, sib_far, weight):
    y, chips = lax.axis_index("gx") // 2, lax.axis_size("gx") // 2
    up = upward(y)
    first = core_of() == 0
    ends = edge(y, chips)
    far = jnp.where(ends & jnp.logical_not(first), 0.0, far[...])
    sib_far = jnp.where(ends & first, 0.0, sib_far[...])
    blocks = [jnp.where(up, sib_far, far), pay[0], pay[1], jnp.where(up, far, sib_far)]
    blocks = [unpack(b) for b in blocks]
    rights = [right_side(b) for b in blocks]
    results = []
    for t in range(2):
        left = jnp.concatenate([blocks[t + i][:M] * weight(blocks[t + i], 1 - i) for i in range(3)], axis=1)
        right = jnp.concatenate(rights[t : t + 3], axis=1)
        results.append(dot_t(right, left, precision=HIGH))
    return results


def factor(rows, dx, dy):
    at = ROW_W + 3 * (dx + 1) + dy + 1
    return rows[at : at + 1]


def send_kernel(pay, far, sib_far, out):
    up = upward(lax.axis_index("gy"))
    both = gains(pay, far, sib_far, lambda rows, dx: jnp.where(up, factor(rows, dx, 1), factor(rows, dx, -1)))
    for t in range(2):
        out[t] = both[t]


def same_kernel(k, order, owner, pay, far, sib_far, out, rank_out):
    both = gains(pay, far, sib_far, lambda rows, dx: factor(rows, dx, 0))
    for t in range(2):
        out[t] = both[t]
    row = owner[pl.ds(order[k], 1), :]
    upper = jnp.where(iota((128, 128), 0) < iota((128, 128), 1), 1.0, 0.0).astype(BF16)
    tiles = iota((TILES, 128), 0)
    base = jnp.zeros((TILES, 1), F32)
    for c in range(OBS // 128):
        at = slice(128 * c, 128 * c + 128)
        hot = jnp.where(row[:, at] == tiles, 1.0, 0.0)
        rank = dot(hot.astype(BF16), upper) + base
        rank_out[:, at] = jnp.sum(hot * rank, axis=0, keepdims=True)
        base = base + jnp.sum(hot, axis=1, keepdims=True)


def advance(z, gain):
    anomaly = z - jnp.sum(z, axis=0, keepdims=True) / M
    return z + dot(gain, anomaly, precision=HIGH)


def whole_gain(t, q0, h, g):
    first = core_of() == 0
    ends = edge(lax.axis_index("gy"), lax.axis_size("gy"))
    return q0[t] + jnp.where(ends & jnp.logical_not(first), 0.0, h[t]) + jnp.where(ends & first, 0.0, g[t])


def step_kernel(k, q0, h, g, z, z_out, pay_out, edge_out, nv_out=None):
    new = []
    for t in range(2):
        moved = advance(z[t, :M], whole_gain(t, q0, h, g))
        z_out[t, :M] = moved
        z_out[t, M:] = z[t, M:]
        new.append(jnp.concatenate([moved, z[t, M:]], axis=0))
    emit(k, new, z_out, pay_out, edge_out, nv_out)


def final_kernel(q0, h, g, z, x, out, come, go, come_sems, go_sems):
    def part(ref, i):
        return ref.at[:, i // PARTS, pl.ds((i % PARTS) * SLAB, SLAB), :]

    loads = [pltpu.make_async_copy(part(x, i), come.at[i], come_sems.at[i]) for i in range(SLABS)]
    stores = [pltpu.make_async_copy(go.at[i], part(out, i), go_sems.at[i]) for i in range(SLABS)]
    for load in loads:
        load.start()
    c = core_of()
    t = advance(z[c, :M, NB * CAP :], whole_gain(c, q0, h, g))[:, :M]
    th, tl = split2(t)
    w = jnp.concatenate([th, th, tl], axis=1)
    for i in range(SLABS):
        loads[i].wait()
        for j in range(0, SLAB, 8):
            turned = jnp.swapaxes(come[i, :, j : j + 8, :], 0, 1)
            rows = []
            for r in range(8):
                xh, xl = split2(turned[r])
                rows.append(dot(w, jnp.concatenate([xh, xl, xh], axis=0))[None])
            go[i, :, j : j + 8, :] = jnp.swapaxes(jnp.concatenate(rows, axis=0), 0, 1)
        stores[i].start()
    for store in stores:
        store.wait()


def place_kernel(order, owner, nv, r0, r1, r2, r3, out):
    high, low = split2(nv[...].T)
    tiles = iota((TILES, OBS), 0)
    slots = iota((CAP, OBS), 0).astype(F32)
    for k, rank in enumerate((r0, r1, r2, r3)):
        b = order[k]
        at = slice(CAP * k, CAP * k + CAP)
        hot = jnp.where(owner[pl.ds(b, 1), :] == tiles, 1.0, 0.0).astype(BF16)
        got = dot(jnp.concatenate([high[at], low[at]], axis=0), hot)
        got = jnp.where(rank[...] == slots, got[:CAP] + got[CAP:], 0.0)
        out[pl.ds(b, 1), :] = jnp.sum(got, axis=0, keepdims=True)


VMEM = pl.BlockSpec(memory_space=pltpu.VMEM)
SMEM = pl.BlockSpec(memory_space=pltpu.SMEM)
HBM = pl.BlockSpec(memory_space=pltpu.HBM)


def shape(*dims):
    return jax.ShapeDtypeStruct(dims, F32)


def swaps(pairs):
    return pairs + [(high, low) for low, high in pairs]


def local(ensemble, obs_value, obs_variance, obs_owner, obs_cell, obs_reach, batch_order):
    params = pltpu.CompilerParams(vmem_limit_bytes=32 * 2**20)
    call = functools.partial(pl.pallas_call, compiler_params=params)
    width, height = lax.axis_size("gx"), lax.axis_size("gy")
    both = ("gx", "gy")
    core = swaps([(x, x + 1) for x in range(0, width, 2)])
    chips = width // 2
    side_x = swaps([(2 * y + c, 2 * ((y + 1) % chips) + c) for c in range(2) for y in range(c, chips, 2)])
    side_y = swaps([
        (x * height + k, x * height + k + 1) for x in range(width) for k in range(x % 2, height - 1, 2)
    ] + [(x * height + k, (x + 2) * height + k) for x in range(1, width, 4) for k in (0, height - 1)])
    pay_shapes = (shape(2, ROWS // 2, 128), shape(ROWS // 2, 128))
    z_shape = shape(2, ROWS, NB * CAP + 128)
    row = pltpu.VMEM((NB, OBS), F32)
    row_i = pltpu.VMEM((NB, OBS), jnp.int32)
    own = call(
        init_kernel,
        out_shape=shape(ROWS, NB * CAP),
        in_specs=[HBM] * 7,
        out_specs=VMEM,
        scratch_shapes=[
            pltpu.SMEM((NB,), jnp.int32), row, row, row_i, row_i,
            pltpu.VMEM((NB, 8, OBS), jnp.int32), pltpu.VMEM((M, TX, TY), F32), pltpu.SemaphoreType.DMA((7,)),
        ],
        name="init",
    )(*(
        pltpu.with_memory_space_constraint(value, pltpu.HBM)
        for value in (
            batch_order, obs_value, obs_variance, obs_owner, obs_cell, jnp.swapaxes(obs_reach, 1, 2), ensemble
        )
    ))
    z, pay, edge = call(
        start_kernel,
        out_shape=(z_shape,) + pay_shapes,
        in_specs=[VMEM] * 2,
        out_specs=(VMEM,) * 3,
        name="start",
    )(own, lax.ppermute(own, "gx", core))
    ranks = []
    for k in range(NB):
        last = k + 1 == NB
        far = lax.ppermute(edge, "gx", side_x)
        if last:
            spread = jnp.broadcast_to(nv, (TILES, NB * CAP))
            everyone = lax.all_to_all(spread, both, 0, 0, tiled=True)
        sib_far = lax.ppermute(far, "gx", core)
        send = call(send_kernel, out_shape=shape(2, M, M), in_specs=[VMEM] * 3, out_specs=VMEM, name="send")(
            pay, far, sib_far
        )
        h = lax.ppermute(send, both, side_y)
        q0, rank = call(
            functools.partial(same_kernel, k),
            out_shape=(shape(2, M, M), shape(1, OBS)),
            in_specs=[SMEM] + [VMEM] * 4,
            out_specs=(VMEM, VMEM),
            name="same",
        )(batch_order, obs_owner, pay, far, sib_far)
        ranks.append(rank)
        h, q0 = lax.optimization_barrier((h, q0))
        g = lax.ppermute(h, "gx", core)
        if not last:
            wide = (shape(1, NB * CAP),) if k + 2 == NB else ()
            z, pay, edge, *rest = call(
                functools.partial(step_kernel, k + 1),
                out_shape=(z_shape,) + pay_shapes + wide,
                in_specs=[VMEM] * 4,
                out_specs=(VMEM,) * (3 + len(wide)),
                name="step",
            )(q0, h, g, z)
            if rest:
                nv = rest[0]
    slabs = pltpu.VMEM((SLABS, M, SLAB, TY), F32)
    state = call(
        final_kernel,
        out_shape=shape(M, LEV, TX, TY),
        in_specs=[VMEM] * 4 + [HBM],
        out_specs=HBM,
        scratch_shapes=[slabs, slabs, pltpu.SemaphoreType.DMA((SLABS,)), pltpu.SemaphoreType.DMA((SLABS,))],
        cost_estimate=pl.CostEstimate(flops=6 * M * M * LEV * TX * TY, bytes_accessed=8 * M * LEV * TX * TY, transcendentals=0),
        name="final",
    )(q0, h, g, z, pltpu.with_memory_space_constraint(ensemble, pltpu.HBM))
    state, everyone = lax.optimization_barrier((state, everyone))
    innovation = call(
        place_kernel,
        out_shape=shape(NB, OBS),
        in_specs=[SMEM] + [VMEM] * 6,
        out_specs=VMEM,
        name="place",
    )(batch_order, obs_owner, everyone, *ranks)
    return state, innovation


def solution(mesh):
    placed = (P(None, None, "gx", "gy"), P(), P(), P(), P(), P(), P())
    return jax.shard_map(
        local,
        mesh=mesh,
        in_specs=placed,
        out_specs=(P(None, None, "gx", "gy"), P()),
        check_vma=False,
    )
```

```python
import functools

import jax
import jax.numpy as jnp
from jax import lax
from jax.experimental import pallas as pl
from jax.experimental.pallas import tpu as pltpu
from jax.sharding import PartitionSpec as P

M = 80
LEV = 4
NB = 4
TX = 32
TY = 256
CAP = 64
OBS = 2048
TILES = 128
EPS = 1e-05
F32 = jnp.float32
BF16 = jnp.bfloat16
HIGH = lax.Precision.HIGHEST
SLAB = 16
PARTS = TX // SLAB
SLABS = LEV * PARTS

ROW_A = M
ROW_C = M + 1
ROW_W = M + 2
ROW_N = M + 11
ROWS = 96
TAPER = (0.25, 0.5, 0.25, 0.5, 1.0, 0.5, 0.25, 0.5, 0.25)


def split2(x):
    high = x.astype(BF16)
    return high, (x - high.astype(F32)).astype(BF16)


def split3(x):
    high = x.astype(BF16)
    rest = x - high.astype(F32)
    mid = rest.astype(BF16)
    return high, mid, (rest - mid.astype(F32)).astype(BF16)


def iota(shape, dim):
    return lax.broadcasted_iota(jnp.int32, shape, dim)


def dot(a, b, **kw):
    return jnp.dot(a, b, preferred_element_type=F32, **kw)


def dot_t(a, b, **kw):
    return lax.dot_general(a, b, (((1,), (1,)), ((), ())), preferred_element_type=F32, **kw)


def pack(rows):
    return jnp.concatenate([rows[: ROWS // 2], rows[ROWS // 2 :]], axis=1)


def unpack(packed):
    return jnp.concatenate([packed[:, :CAP], packed[:, CAP:]], axis=0)


def make_payload(prior, meta):
    valid = meta[0:1] > 0.5
    value = meta[1:2]
    variance = jnp.where(valid, meta[2:3], 1.0)
    center = jnp.sum(prior, axis=0, keepdims=True) / M
    deviation = prior - center
    spread = jnp.sum(deviation * deviation, axis=0, keepdims=True) / (M - 1)
    total = spread + variance
    miss = value - center
    normed = jnp.where(valid, miss / jnp.sqrt(total), 0.0)
    a = spread / total * miss
    c = jnp.sqrt(variance / total) - 1.0
    d = jnp.where(valid, 1.0 / ((M - 1) * (spread + EPS)), 0.0)
    rows = [deviation, a, c]
    for i in range(9):
        if i == 4:
            rows.append(d)
        else:
            at = 3 + (i if i < 4 else i - 1)
            rows.append(d * (meta[at : at + 1] * TAPER[i]))
    rows.append(jnp.zeros((ROWS - M - 11, CAP), F32))
    return pack(jnp.concatenate(rows, axis=0)), normed


def init_kernel(order_hbm, value_hbm, variance_hbm, owner_hbm, cell_hbm, reach_hbm, x_hbm, out,
                order, value, variance, owner, cell, reach, surface, sems):
    small = [
        pltpu.make_async_copy(source, target, sems.at[i])
        for i, (source, target) in enumerate([
            (order_hbm, order), (owner_hbm, owner), (cell_hbm, cell),
            (value_hbm, value), (variance_hbm, variance), (reach_hbm, reach),
        ])
    ]
    load = pltpu.make_async_copy(x_hbm.at[:, 0], surface, sems.at[6])
    for copy in small:
        copy.start()
    load.start()
    me = lax.axis_index("gx") * lax.axis_size("gy") + lax.axis_index("gy")
    small[0].wait()
    small[1].wait()
    owned = jnp.concatenate([owner[pl.ds(order[k], 1), :] for k in range(NB)], axis=0) == me
    ownf = jnp.where(owned, 1.0, 0.0)
    chunks = OBS // 128
    own64 = jnp.concatenate([ownf[:, 128 * c : 128 * c + 128] for c in range(chunks)], axis=0).astype(BF16)
    upper = jnp.where(iota((128, 128), 0) < iota((128, 128), 1), 1.0, 0.0).astype(BF16)
    rows = NB * chunks
    r0, r1 = iota((rows, rows), 0), iota((rows, rows), 1)
    before = jnp.where((r1 < r0) & (((r0 - r1) & (NB - 1)) == 0), 1.0, 0.0).astype(BF16)
    base = dot(dot(before, own64).astype(BF16), jnp.ones((128, 128), BF16))
    rank64 = dot(own64, upper) + base
    rank = jnp.concatenate([rank64[NB * c : NB * c + NB] for c in range(chunks)], axis=1)
    rank = jnp.where(owned, rank, -1.0)
    slots = iota((CAP, OBS), 0).astype(F32)
    for copy in small[2:]:
        copy.wait()
    metas = []
    for k in range(NB):
        b = order[k]
        hot = jnp.where(rank[k : k + 1] == slots, 1.0, 0.0).astype(BF16)
        where = cell[pl.ds(b, 1), :]
        vh, vm, vl = split3(value[pl.ds(b, 1), :])
        rh, rm, rl = split3(variance[pl.ds(b, 1), :])
        parts = [
            reach[b].astype(F32),
            lax.shift_right_logical(where, 8).astype(F32),
            (where & 255).astype(F32),
            vh.astype(F32), vm.astype(F32), vl.astype(F32),
            rh.astype(F32), rm.astype(F32), rl.astype(F32),
            jnp.ones((1, OBS), F32),
            jnp.zeros((15, OBS), F32),
        ]
        metas.append(dot_t(jnp.concatenate(parts, axis=0).astype(BF16), hot))
    got = jnp.concatenate(metas, axis=1)
    out[M:] = jnp.concatenate(
        [
            got[16:17],
            got[10:11] + got[11:12] + got[12:13],
            got[13:14] + got[14:15] + got[15:16],
            got[:8],
            jnp.zeros((5, NB * CAP), F32),
        ],
        axis=0,
    )
    hot_y = jnp.where(got[9:10] == iota((TY, NB * CAP), 0).astype(F32), 1.0, 0.0).astype(BF16)
    hot_x = jnp.where(got[8:9] == iota((TX, NB * CAP), 0).astype(F32), 1.0, 0.0)
    load.wait()
    group = 16
    for g in range(M // group):
        h, m, l = split3(surface[group * g : group * g + group].reshape(group * TX, TY))
        picked = dot(h, hot_y) + dot(m, hot_y) + dot(l, hot_y)
        out[group * g : group * g + group] = jnp.sum(
            picked.reshape(group, TX, NB * CAP) * hot_x[None], axis=1
        )


def core_of():
    return lax.rem(lax.axis_index("gx"), 2)


def edge(index, count):
    return (index == 0) | (index == count - 1)


def upward(index):
    return lax.rem(index + core_of(), 2) == 0


def emit(k, z, z_out, pay_out, edge_out, news_out=None):
    pays = []
    at = slice(CAP * k, CAP * k + CAP)
    news = []
    for t in range(2):
        pay, normed = make_payload(z[t][:M, at], z[t][M:, at])
        pay_out[t] = pay
        z_out[t, ROW_N : ROW_N + 1, at] = normed
        pays.append(pay)
        news.append(normed)
    edge_out[: ROWS // 2] = jnp.where(upward(lax.axis_index("gx") // 2), pays[1], pays[0])
    if news_out is not None:
        rows = [
            jnp.concatenate([z[t][ROW_N : ROW_N + 1, CAP * i : CAP * i + CAP] for t in range(2)], axis=1) for i in range(k)
        ]
        rows.append(jnp.concatenate(news, axis=1))
        rows.append(jnp.zeros((8 - NB, 2 * CAP), F32))
        block = jnp.concatenate(rows, axis=0)
        edge_out[ROWS // 2 :] = block
        news_out[...] = block


def start_kernel(own, sib, z_out, pay_out, edge_out):
    first = core_of() == 0
    mine, other = own[...], sib[...]
    z = [jnp.where(first, mine, other), jnp.where(first, other, mine)]
    unit = jnp.where(iota((ROWS, 128), 0) == iota((ROWS, 128), 1), 1.0, 0.0)
    unit = jnp.where(iota((ROWS, 128), 0) < M, unit, 0.0)
    for t in range(2):
        z_out[t, :, : NB * CAP] = z[t]
        z_out[t, :, NB * CAP :] = unit
    emit(0, z, z_out, pay_out, edge_out)


def right_side(rows):
    return rows[ROW_A : ROW_A + 1] + rows[ROW_C : ROW_C + 1] * rows[:M]


def gains(pay, far, sib_far, weight):
    y, chips = lax.axis_index("gx") // 2, lax.axis_size("gx") // 2
    up = upward(y)
    first = core_of() == 0
    ends = edge(y, chips)
    far = jnp.where(ends & jnp.logical_not(first), 0.0, far[: ROWS // 2])
    sib_far = jnp.where(ends & first, 0.0, sib_far[: ROWS // 2])
    blocks = [jnp.where(up, sib_far, far), pay[0], pay[1], jnp.where(up, far, sib_far)]
    blocks = [unpack(b) for b in blocks]
    rights = [right_side(b) for b in blocks]
    results = []
    for t in range(2):
        left = jnp.concatenate([blocks[t + i][:M] * weight(blocks[t + i], 1 - i) for i in range(3)], axis=1)
        right = jnp.concatenate(rights[t : t + 3], axis=1)
        results.append(dot_t(right, left, precision=HIGH))
    return results


def factor(rows, dx, dy):
    at = ROW_W + 3 * (dx + 1) + dy + 1
    return rows[at : at + 1]


def send_kernel(pay, far, sib_far, out):
    up = upward(lax.axis_index("gy"))
    both = gains(pay, far, sib_far, lambda rows, dx: jnp.where(up, factor(rows, dx, 1), factor(rows, dx, -1)))
    for t in range(2):
        out[t] = both[t]


def same_kernel(k, order, owner, pay, far, sib_far, out, rank_out):
    both = gains(pay, far, sib_far, lambda rows, dx: factor(rows, dx, 0))
    for t in range(2):
        out[t] = both[t]
    row = owner[pl.ds(order[k], 1), :]
    upper = jnp.where(iota((128, 128), 0) < iota((128, 128), 1), 1.0, 0.0).astype(BF16)
    tiles = iota((TILES, 128), 0)
    base = jnp.zeros((TILES, 1), F32)
    for c in range(OBS // 128):
        at = slice(128 * c, 128 * c + 128)
        hot = jnp.where(row[:, at] == tiles, 1.0, 0.0)
        rank = dot(hot.astype(BF16), upper) + base
        rank_out[:, at] = jnp.sum(hot * rank, axis=0, keepdims=True)
        base = base + jnp.sum(hot, axis=1, keepdims=True)


def column_kernel(news, far, sib_far, across, out):
    first = core_of() == 0
    at = slice(ROWS // 2, ROWS // 2 + NB)
    mine, other = far[at], sib_far[at]
    column = jnp.concatenate(
        [news[:NB], jnp.where(first, mine, other), across[:NB], jnp.where(first, other, mine)], axis=0
    )
    out[...] = jnp.broadcast_to(column[None], out.shape)


def advance(z, gain):
    anomaly = z - jnp.sum(z, axis=0, keepdims=True) / M
    return z + dot(gain, anomaly, precision=HIGH)


def whole_gain(t, q0, h, g):
    first = core_of() == 0
    ends = edge(lax.axis_index("gy"), lax.axis_size("gy"))
    return q0[t] + jnp.where(ends & jnp.logical_not(first), 0.0, h[t]) + jnp.where(ends & first, 0.0, g[t])


def step_kernel(k, q0, h, g, z, z_out, pay_out, edge_out, news_out=None):
    new = []
    for t in range(2):
        moved = advance(z[t, :M], whole_gain(t, q0, h, g))
        z_out[t, :M] = moved
        z_out[t, M:] = z[t, M:]
        new.append(jnp.concatenate([moved, z[t, M:]], axis=0))
    emit(k, new, z_out, pay_out, edge_out, news_out)


def final_kernel(q0, h, g, z, x, out, come, go, come_sems, go_sems):
    def part(ref, i):
        return ref.at[:, i // PARTS, pl.ds((i % PARTS) * SLAB, SLAB), :]

    loads = [pltpu.make_async_copy(part(x, i), come.at[i], come_sems.at[i]) for i in range(SLABS)]
    stores = [pltpu.make_async_copy(go.at[i], part(out, i), go_sems.at[i]) for i in range(SLABS)]
    for load in loads:
        load.start()
    c = core_of()
    t = advance(z[c, :M, NB * CAP :], whole_gain(c, q0, h, g))[:, :M]
    th, tl = split2(t)
    w = jnp.concatenate([th, th, tl], axis=1)
    for i in range(SLABS):
        loads[i].wait()
        for j in range(0, SLAB, 8):
            turned = jnp.swapaxes(come[i, :, j : j + 8, :], 0, 1)
            rows = []
            for r in range(8):
                xh, xl = split2(turned[r])
                rows.append(dot(w, jnp.concatenate([xh, xl, xh], axis=0))[None])
            go[i, :, j : j + 8, :] = jnp.swapaxes(jnp.concatenate(rows, axis=0), 0, 1)
        stores[i].start()
    for store in stores:
        store.wait()


def place_kernel(order, owner, gathered, r0, r1, r2, r3, out):
    y = lax.axis_index("gx") // 2
    chips = iota((TILES // 2, OBS), 0)
    seats = iota((2 * CAP, OBS), 0)
    rows = gathered.reshape(TILES // 2 * NB, 2 * CAP)
    for k, rank in enumerate((r0, r1, r2, r3)):
        b = order[k]
        tile = owner[pl.ds(b, 1), :]
        chip = (tile & 15) * 4 + ((tile >> 5) ^ y)
        hot = jnp.where(chip == chips, 1.0, 0.0).astype(BF16)
        high, low = split2(rows[pl.ds(k, TILES // 2, stride=NB), :].T)
        got = dot(jnp.concatenate([high, low], axis=1), jnp.concatenate([hot, hot], axis=0))
        seat = ((tile >> 4) & 1) * CAP + rank[...].astype(jnp.int32)
        out[pl.ds(b, 1), :] = jnp.sum(jnp.where(seat == seats, got, 0.0), axis=0, keepdims=True)


VMEM = pl.BlockSpec(memory_space=pltpu.VMEM)
SMEM = pl.BlockSpec(memory_space=pltpu.SMEM)
HBM = pl.BlockSpec(memory_space=pltpu.HBM)


def shape(*dims):
    return jax.ShapeDtypeStruct(dims, F32)


def swaps(pairs):
    return pairs + [(high, low) for low, high in pairs]


def local(ensemble, obs_value, obs_variance, obs_owner, obs_cell, obs_reach, batch_order):
    params = pltpu.CompilerParams(vmem_limit_bytes=32 * 2**20)
    call = functools.partial(pl.pallas_call, compiler_params=params)
    width, height = lax.axis_size("gx"), lax.axis_size("gy")
    both = ("gx", "gy")
    core = swaps([(x, x + 1) for x in range(0, width, 2)])
    chips = width // 2
    side_x = swaps([(2 * y + c, 2 * ((y + 1) % chips) + c) for c in range(2) for y in range(c, chips, 2)])
    side_y = swaps([
        (x * height + k, x * height + k + 1) for x in range(width) for k in range(x % 2, height - 1, 2)
    ] + [(x * height + k, (x + 2) * height + k) for x in range(1, width, 4) for k in (0, height - 1)])
    pay_shapes = (shape(2, ROWS // 2, 128), shape(ROWS // 2, 128))
    z_shape = shape(2, ROWS, NB * CAP + 128)
    row = pltpu.VMEM((NB, OBS), F32)
    row_i = pltpu.VMEM((NB, OBS), jnp.int32)
    own = call(
        init_kernel,
        out_shape=shape(ROWS, NB * CAP),
        in_specs=[HBM] * 7,
        out_specs=VMEM,
        scratch_shapes=[
            pltpu.SMEM((NB,), jnp.int32), row, row, row_i, row_i,
            pltpu.VMEM((NB, 8, OBS), jnp.int32), pltpu.VMEM((M, TX, TY), F32), pltpu.SemaphoreType.DMA((7,)),
        ],
        name="init",
    )(*(
        pltpu.with_memory_space_constraint(value, pltpu.HBM)
        for value in (
            batch_order, obs_value, obs_variance, obs_owner, obs_cell, jnp.swapaxes(obs_reach, 1, 2), ensemble
        )
    ))
    z, pay, edge = call(
        start_kernel,
        out_shape=(z_shape,) + pay_shapes,
        in_specs=[VMEM] * 2,
        out_specs=(VMEM,) * 3,
        name="start",
    )(own, lax.ppermute(own, "gx", core))
    ranks = []
    for k in range(NB):
        last = k + 1 == NB
        far = lax.ppermute(edge, "gx", side_x)
        sib_far = lax.ppermute(far, "gx", core)
        send = call(send_kernel, out_shape=shape(2, M, M), in_specs=[VMEM] * 3, out_specs=VMEM, name="send")(
            pay, far, sib_far
        )
        send, sib_far = lax.optimization_barrier((send, sib_far))
        h = lax.ppermute(send, both, side_y)
        q0, rank = call(
            functools.partial(same_kernel, k),
            out_shape=(shape(2, M, M), shape(1, OBS)),
            in_specs=[SMEM] + [VMEM] * 4,
            out_specs=(VMEM, VMEM),
            name="same",
        )(batch_order, obs_owner, pay, far, sib_far)
        ranks.append(rank)
        if last:
            across = lax.ppermute(sib_far[ROWS // 2 :], "gx", side_x)
            column = call(
                column_kernel, out_shape=shape(height, 4 * NB, 128), in_specs=[VMEM] * 4, out_specs=VMEM, name="column"
            )(news, far, sib_far, across)
            gathered = lax.all_to_all(column, "gy", 0, 0, tiled=True)
        h, q0 = lax.optimization_barrier((h, q0))
        g = lax.ppermute(h, "gx", core)
        if not last:
            tail = k + 2 == NB
            edge_shape = (shape(ROWS // 2 + 8, 128), shape(8, 128)) if tail else pay_shapes[1:]
            z, pay, edge, *rest = call(
                functools.partial(step_kernel, k + 1),
                out_shape=(z_shape, pay_shapes[0]) + edge_shape,
                in_specs=[VMEM] * 4,
                out_specs=(VMEM,) * (4 if tail else 3),
                name="step",
            )(q0, h, g, z)
            if tail:
                news = rest[0]
    slabs = pltpu.VMEM((SLABS, M, SLAB, TY), F32)
    state = call(
        final_kernel,
        out_shape=shape(M, LEV, TX, TY),
        in_specs=[VMEM] * 4 + [HBM],
        out_specs=HBM,
        scratch_shapes=[slabs, slabs, pltpu.SemaphoreType.DMA((SLABS,)), pltpu.SemaphoreType.DMA((SLABS,))],
        cost_estimate=pl.CostEstimate(flops=6 * M * M * LEV * TX * TY, bytes_accessed=8 * M * LEV * TX * TY, transcendentals=0),
        name="final",
    )(q0, h, g, z, pltpu.with_memory_space_constraint(ensemble, pltpu.HBM))
    state, gathered = lax.optimization_barrier((state, gathered))
    innovation = call(
        place_kernel,
        out_shape=shape(NB, OBS),
        in_specs=[SMEM] + [VMEM] * 6,
        out_specs=VMEM,
        name="place",
    )(batch_order, obs_owner, gathered, *ranks)
    return state, innovation


def solution(mesh):
    placed = (P(None, None, "gx", "gy"), P(), P(), P(), P(), P(), P())
    return jax.shard_map(
        local,
        mesh=mesh,
        in_specs=placed,
        out_specs=(P(None, None, "gx", "gy"), P()),
        check_vma=False,
    )
```

```python
import functools

import jax
import jax.numpy as jnp
from jax import lax
from jax.experimental import pallas as pl
from jax.experimental.pallas import tpu as pltpu
from jax.sharding import PartitionSpec as P

M = 80
LEV = 4
NB = 4
TX = 32
TY = 256
CAP = 64
OBS = 2048
TILES = 128
EPS = 1e-05
F32 = jnp.float32
BF16 = jnp.bfloat16
HIGH = lax.Precision.HIGHEST
SLAB = 16
PARTS = TX // SLAB
SLABS = LEV * PARTS

ROW_A = M
ROW_C = M + 1
ROW_W = M + 2
ROW_N = M + 11
ROWS = 96
TAPER = (0.25, 0.5, 0.25, 0.5, 1.0, 0.5, 0.25, 0.5, 0.25)


def split2(x):
    high = x.astype(BF16)
    return high, (x - high.astype(F32)).astype(BF16)


def split3(x):
    high = x.astype(BF16)
    rest = x - high.astype(F32)
    mid = rest.astype(BF16)
    return high, mid, (rest - mid.astype(F32)).astype(BF16)


def iota(shape, dim):
    return lax.broadcasted_iota(jnp.int32, shape, dim)


def dot(a, b, **kw):
    return jnp.dot(a, b, preferred_element_type=F32, **kw)


def dot_t(a, b, **kw):
    return lax.dot_general(a, b, (((1,), (1,)), ((), ())), preferred_element_type=F32, **kw)


def pack(rows):
    return jnp.concatenate([rows[: ROWS // 2], rows[ROWS // 2 :]], axis=1)


def unpack(packed):
    return jnp.concatenate([packed[:, :CAP], packed[:, CAP:]], axis=0)


def make_payload(prior, meta):
    valid = meta[0:1] > 0.5
    value = meta[1:2]
    variance = jnp.where(valid, meta[2:3], 1.0)
    center = jnp.sum(prior, axis=0, keepdims=True) / M
    deviation = prior - center
    spread = jnp.sum(deviation * deviation, axis=0, keepdims=True) / (M - 1)
    total = spread + variance
    miss = value - center
    normed = jnp.where(valid, miss / jnp.sqrt(total), 0.0)
    a = spread / total * miss
    c = jnp.sqrt(variance / total) - 1.0
    d = jnp.where(valid, 1.0 / ((M - 1) * (spread + EPS)), 0.0)
    rows = [deviation, a, c]
    for i in range(9):
        if i == 4:
            rows.append(d)
        else:
            at = 3 + (i if i < 4 else i - 1)
            rows.append(d * (meta[at : at + 1] * TAPER[i]))
    rows.append(jnp.zeros((ROWS - M - 11, CAP), F32))
    return pack(jnp.concatenate(rows, axis=0)), normed


def init_kernel(order_hbm, value_hbm, variance_hbm, owner_hbm, cell_hbm, reach_hbm, x_hbm, out,
                order, value, variance, owner, cell, reach, surface, sems):
    small = [
        pltpu.make_async_copy(source, target, sems.at[i])
        for i, (source, target) in enumerate([
            (order_hbm, order), (owner_hbm, owner), (cell_hbm, cell),
            (value_hbm, value), (variance_hbm, variance), (reach_hbm, reach),
        ])
    ]
    load = pltpu.make_async_copy(x_hbm.at[:, 0], surface, sems.at[6])
    for copy in small:
        copy.start()
    load.start()
    me = lax.axis_index("gx") * lax.axis_size("gy") + lax.axis_index("gy")
    small[0].wait()
    small[1].wait()
    owned = jnp.concatenate([owner[pl.ds(order[k], 1), :] for k in range(NB)], axis=0) == me
    ownf = jnp.where(owned, 1.0, 0.0)
    chunks = OBS // 128
    own64 = jnp.concatenate([ownf[:, 128 * c : 128 * c + 128] for c in range(chunks)], axis=0).astype(BF16)
    upper = jnp.where(iota((128, 128), 0) < iota((128, 128), 1), 1.0, 0.0).astype(BF16)
    rows = NB * chunks
    r0, r1 = iota((rows, rows), 0), iota((rows, rows), 1)
    before = jnp.where((r1 < r0) & (((r0 - r1) & (NB - 1)) == 0), 1.0, 0.0).astype(BF16)
    base = dot(dot(before, own64).astype(BF16), jnp.ones((128, 128), BF16))
    rank64 = dot(own64, upper) + base
    rank = jnp.concatenate([rank64[NB * c : NB * c + NB] for c in range(chunks)], axis=1)
    rank = jnp.where(owned, rank, -1.0)
    slots = iota((CAP, OBS), 0).astype(F32)
    for copy in small[2:]:
        copy.wait()
    metas = []
    for k in range(NB):
        b = order[k]
        hot = jnp.where(rank[k : k + 1] == slots, 1.0, 0.0).astype(BF16)
        where = cell[pl.ds(b, 1), :]
        vh, vm, vl = split3(value[pl.ds(b, 1), :])
        rh, rm, rl = split3(variance[pl.ds(b, 1), :])
        parts = [
            reach[b].astype(F32),
            lax.shift_right_logical(where, 8).astype(F32),
            (where & 255).astype(F32),
            vh.astype(F32), vm.astype(F32), vl.astype(F32),
            rh.astype(F32), rm.astype(F32), rl.astype(F32),
            jnp.ones((1, OBS), F32),
            jnp.zeros((15, OBS), F32),
        ]
        metas.append(dot_t(jnp.concatenate(parts, axis=0).astype(BF16), hot))
    got = jnp.concatenate(metas, axis=1)
    out[M:] = jnp.concatenate(
        [
            got[16:17],
            got[10:11] + got[11:12] + got[12:13],
            got[13:14] + got[14:15] + got[15:16],
            got[:8],
            jnp.zeros((5, NB * CAP), F32),
        ],
        axis=0,
    )
    hot_y = jnp.where(got[9:10] == iota((TY, NB * CAP), 0).astype(F32), 1.0, 0.0).astype(BF16)
    hot_x = jnp.where(got[8:9] == iota((TX, NB * CAP), 0).astype(F32), 1.0, 0.0)
    load.wait()
    group = 16
    for g in range(M // group):
        h, m, l = split3(surface[group * g : group * g + group].reshape(group * TX, TY))
        picked = dot(h, hot_y) + dot(m, hot_y) + dot(l, hot_y)
        out[group * g : group * g + group] = jnp.sum(
            picked.reshape(group, TX, NB * CAP) * hot_x[None], axis=1
        )


def core_of():
    return lax.rem(lax.axis_index("gx"), 2)


def edge(index, count):
    return (index == 0) | (index == count - 1)


def upward(index):
    return lax.rem(index + core_of(), 2) == 0


def emit(k, z, z_out, pay_out, edge_out, news_out=None):
    pays = []
    at = slice(CAP * k, CAP * k + CAP)
    news = []
    for t in range(2):
        pay, normed = make_payload(z[t][:M, at], z[t][M:, at])
        pay_out[t] = pay
        z_out[t, ROW_N : ROW_N + 1, at] = normed
        pays.append(pay)
        news.append(normed)
    edge_out[: ROWS // 2] = jnp.where(upward(lax.axis_index("gx") // 2), pays[1], pays[0])
    if news_out is not None:
        rows = [
            jnp.concatenate([z[t][ROW_N : ROW_N + 1, CAP * i : CAP * i + CAP] for t in range(2)], axis=1) for i in range(k)
        ]
        rows.append(jnp.concatenate(news, axis=1))
        rows.append(jnp.zeros((8 - NB, 2 * CAP), F32))
        block = jnp.concatenate(rows, axis=0)
        edge_out[ROWS // 2 :] = block
        news_out[...] = block


def start_kernel(own, sib, z_out, pay_out, edge_out):
    first = core_of() == 0
    mine, other = own[...], sib[...]
    z = [jnp.where(first, mine, other), jnp.where(first, other, mine)]
    unit = jnp.where(iota((ROWS, 128), 0) == iota((ROWS, 128), 1), 1.0, 0.0)
    unit = jnp.where(iota((ROWS, 128), 0) < M, unit, 0.0)
    for t in range(2):
        z_out[t, :, : NB * CAP] = z[t]
        z_out[t, :, NB * CAP :] = unit
    emit(0, z, z_out, pay_out, edge_out)


def right_side(rows):
    return rows[ROW_A : ROW_A + 1] + rows[ROW_C : ROW_C + 1] * rows[:M]


def gains(pay, far, sib_far, weight):
    y, chips = lax.axis_index("gx") // 2, lax.axis_size("gx") // 2
    up = upward(y)
    first = core_of() == 0
    ends = edge(y, chips)
    far = jnp.where(ends & jnp.logical_not(first), 0.0, far[: ROWS // 2])
    sib_far = jnp.where(ends & first, 0.0, sib_far[: ROWS // 2])
    blocks = [jnp.where(up, sib_far, far), pay[0], pay[1], jnp.where(up, far, sib_far)]
    blocks = [unpack(b) for b in blocks]
    rights = [right_side(b) for b in blocks]
    results = []
    for t in range(2):
        left = jnp.concatenate([blocks[t + i][:M] * weight(blocks[t + i], 1 - i) for i in range(3)], axis=1)
        right = jnp.concatenate(rights[t : t + 3], axis=1)
        results.append(dot_t(right, left, precision=HIGH))
    return results


def factor(rows, dx, dy):
    at = ROW_W + 3 * (dx + 1) + dy + 1
    return rows[at : at + 1]


def send_kernel(pay, far, sib_far, out):
    up = upward(lax.axis_index("gy"))
    both = gains(pay, far, sib_far, lambda rows, dx: jnp.where(up, factor(rows, dx, 1), factor(rows, dx, -1)))
    for t in range(2):
        out[t] = both[t]


def same_kernel(k, order, owner, pay, far, sib_far, out, rank_out):
    both = gains(pay, far, sib_far, lambda rows, dx: factor(rows, dx, 0))
    for t in range(2):
        out[t] = both[t]
    row = owner[pl.ds(order[k], 1), :]
    upper = jnp.where(iota((128, 128), 0) < iota((128, 128), 1), 1.0, 0.0).astype(BF16)
    tiles = iota((TILES, 128), 0)
    base = jnp.zeros((TILES, 1), F32)
    for c in range(OBS // 128):
        at = slice(128 * c, 128 * c + 128)
        hot = jnp.where(row[:, at] == tiles, 1.0, 0.0)
        rank = dot(hot.astype(BF16), upper) + base
        rank_out[:, at] = jnp.sum(hot * rank, axis=0, keepdims=True)
        base = base + jnp.sum(hot, axis=1, keepdims=True)


def column_kernel(news, far, sib_far, across, out):
    first = core_of() == 0
    at = slice(ROWS // 2, ROWS // 2 + NB)
    mine, other = far[at], sib_far[at]
    column = jnp.concatenate(
        [news[:NB], jnp.where(first, mine, other), across[:NB], jnp.where(first, other, mine)], axis=0
    )
    out[...] = jnp.broadcast_to(column[None], out.shape)


def advance(z, gain):
    anomaly = z - jnp.sum(z, axis=0, keepdims=True) / M
    return z + dot(gain, anomaly, precision=HIGH)


def whole_gain(t, q0, h, g):
    first = core_of() == 0
    ends = edge(lax.axis_index("gy"), lax.axis_size("gy"))
    return q0[t] + jnp.where(ends & jnp.logical_not(first), 0.0, h[t]) + jnp.where(ends & first, 0.0, g[t])


def step_kernel(k, q0, h, g, z, z_out, pay_out, edge_out, news_out=None):
    new = []
    for t in range(2):
        moved = advance(z[t, :M], whole_gain(t, q0, h, g))
        z_out[t, :M] = moved
        z_out[t, M:] = z[t, M:]
        new.append(jnp.concatenate([moved, z[t, M:]], axis=0))
    emit(k, new, z_out, pay_out, edge_out, news_out)


def final_kernel(q0, h, g, z, x, out, come, go, come_sems, go_sems):
    def part(ref, i):
        return ref.at[:, i // PARTS, pl.ds((i % PARTS) * SLAB, SLAB), :]

    loads = [pltpu.make_async_copy(part(x, i), come.at[i], come_sems.at[i]) for i in range(SLABS)]
    stores = [pltpu.make_async_copy(go.at[i], part(out, i), go_sems.at[i]) for i in range(SLABS)]
    for load in loads:
        load.start()
    c = core_of()
    t = advance(z[c, :M, NB * CAP :], whole_gain(c, q0, h, g))[:, :M]
    th, tl = split2(t)
    w = jnp.concatenate([th, th, tl], axis=1)
    for i in range(SLABS):
        loads[i].wait()
        for j in range(0, SLAB, 8):
            turned = jnp.swapaxes(come[i, :, j : j + 8, :], 0, 1)
            rows = []
            for r in range(8):
                xh, xl = split2(turned[r])
                rows.append(dot(w, jnp.concatenate([xh, xl, xh], axis=0))[None])
            go[i, :, j : j + 8, :] = jnp.swapaxes(jnp.concatenate(rows, axis=0), 0, 1)
        stores[i].start()
    for store in stores:
        store.wait()


def place_kernel(order, owner, gathered, r0, r1, r2, r3, out):
    y = lax.axis_index("gx") // 2
    tiles = iota((TILES, OBS), 0)
    slots = iota((CAP, OBS), 0).astype(F32)
    rows = gathered.reshape(TILES // 2 * NB, 2 * CAP)
    for k, rank in enumerate((r0, r1, r2, r3)):
        b = order[k]
        tile = owner[pl.ds(b, 1), :]
        place = ((tile >> 4) & 1) * (TILES // 2) + (tile & 15) * 4 + ((tile >> 5) ^ y)
        turned = rows[pl.ds(k, TILES // 2, stride=NB), :].T
        table = jnp.concatenate([turned[:CAP], turned[CAP:]], axis=1)
        if k < NB // 2:
            chunks = [slice(at, at + 128) for at in range(0, OBS, 128)]
            got = jnp.concatenate([
                jnp.take_along_axis(table, jnp.broadcast_to(place[:, at], (CAP, 128)), axis=1) for at in chunks
            ], axis=1)
        else:
            hot = jnp.where(place == tiles, 1.0, 0.0).astype(BF16)
            both = dot(jnp.concatenate(split2(table), axis=0), hot)
            got = both[:CAP] + both[CAP:]
        out[pl.ds(b, 1), :] = jnp.sum(jnp.where(rank[...] == slots, got, 0.0), axis=0, keepdims=True)


VMEM = pl.BlockSpec(memory_space=pltpu.VMEM)
SMEM = pl.BlockSpec(memory_space=pltpu.SMEM)
HBM = pl.BlockSpec(memory_space=pltpu.HBM)


def shape(*dims):
    return jax.ShapeDtypeStruct(dims, F32)


def swaps(pairs):
    return pairs + [(high, low) for low, high in pairs]


def local(ensemble, obs_value, obs_variance, obs_owner, obs_cell, obs_reach, batch_order):
    params = pltpu.CompilerParams(vmem_limit_bytes=32 * 2**20)
    call = functools.partial(pl.pallas_call, compiler_params=params)
    width, height = lax.axis_size("gx"), lax.axis_size("gy")
    both = ("gx", "gy")
    core = swaps([(x, x + 1) for x in range(0, width, 2)])
    chips = width // 2
    side_x = swaps([(2 * y + c, 2 * ((y + 1) % chips) + c) for c in range(2) for y in range(c, chips, 2)])
    side_y = swaps([
        (x * height + k, x * height + k + 1) for x in range(width) for k in range(x % 2, height - 1, 2)
    ] + [(x * height + k, (x + 2) * height + k) for x in range(1, width, 4) for k in (0, height - 1)])
    pay_shapes = (shape(2, ROWS // 2, 128), shape(ROWS // 2, 128))
    z_shape = shape(2, ROWS, NB * CAP + 128)
    row = pltpu.VMEM((NB, OBS), F32)
    row_i = pltpu.VMEM((NB, OBS), jnp.int32)
    own = call(
        init_kernel,
        out_shape=shape(ROWS, NB * CAP),
        in_specs=[HBM] * 7,
        out_specs=VMEM,
        scratch_shapes=[
            pltpu.SMEM((NB,), jnp.int32), row, row, row_i, row_i,
            pltpu.VMEM((NB, 8, OBS), jnp.int32), pltpu.VMEM((M, TX, TY), F32), pltpu.SemaphoreType.DMA((7,)),
        ],
        name="init",
    )(*(
        pltpu.with_memory_space_constraint(value, pltpu.HBM)
        for value in (
            batch_order, obs_value, obs_variance, obs_owner, obs_cell, jnp.swapaxes(obs_reach, 1, 2), ensemble
        )
    ))
    z, pay, edge = call(
        start_kernel,
        out_shape=(z_shape,) + pay_shapes,
        in_specs=[VMEM] * 2,
        out_specs=(VMEM,) * 3,
        name="start",
    )(own, lax.ppermute(own, "gx", core))
    ranks = []
    for k in range(NB):
        last = k + 1 == NB
        far = lax.ppermute(edge, "gx", side_x)
        sib_far = lax.ppermute(far, "gx", core)
        send = call(send_kernel, out_shape=shape(2, M, M), in_specs=[VMEM] * 3, out_specs=VMEM, name="send")(
            pay, far, sib_far
        )
        send, sib_far = lax.optimization_barrier((send, sib_far))
        h = lax.ppermute(send, both, side_y)
        q0, rank = call(
            functools.partial(same_kernel, k),
            out_shape=(shape(2, M, M), shape(1, OBS)),
            in_specs=[SMEM] + [VMEM] * 4,
            out_specs=(VMEM, VMEM),
            name="same",
        )(batch_order, obs_owner, pay, far, sib_far)
        ranks.append(rank)
        if last:
            across = lax.ppermute(sib_far[ROWS // 2 :], "gx", side_x)
            column = call(
                column_kernel, out_shape=shape(height, 4 * NB, 128), in_specs=[VMEM] * 4, out_specs=VMEM, name="column"
            )(news, far, sib_far, across)
        if last:
            h, q0, column = lax.optimization_barrier((h, q0, column))
            gathered = lax.all_to_all(column, "gy", 0, 0, tiled=True)
        else:
            h, q0 = lax.optimization_barrier((h, q0))
        g = lax.ppermute(h, "gx", core)
        if not last:
            tail = k + 2 == NB
            edge_shape = (shape(ROWS // 2 + 8, 128), shape(8, 128)) if tail else pay_shapes[1:]
            z, pay, edge, *rest = call(
                functools.partial(step_kernel, k + 1),
                out_shape=(z_shape, pay_shapes[0]) + edge_shape,
                in_specs=[VMEM] * 4,
                out_specs=(VMEM,) * (4 if tail else 3),
                name="step",
            )(q0, h, g, z)
            if tail:
                news = rest[0]
    slabs = pltpu.VMEM((SLABS, M, SLAB, TY), F32)
    state = call(
        final_kernel,
        out_shape=shape(M, LEV, TX, TY),
        in_specs=[VMEM] * 4 + [HBM],
        out_specs=HBM,
        scratch_shapes=[slabs, slabs, pltpu.SemaphoreType.DMA((SLABS,)), pltpu.SemaphoreType.DMA((SLABS,))],
        cost_estimate=pl.CostEstimate(flops=6 * M * M * LEV * TX * TY, bytes_accessed=8 * M * LEV * TX * TY, transcendentals=0),
        name="final",
    )(q0, h, g, z, pltpu.with_memory_space_constraint(ensemble, pltpu.HBM))
    state, gathered = lax.optimization_barrier((state, gathered))
    innovation = call(
        place_kernel,
        out_shape=shape(NB, OBS),
        in_specs=[SMEM] + [VMEM] * 6,
        out_specs=VMEM,
        name="place",
    )(batch_order, obs_owner, gathered, *ranks)
    return state, innovation


def solution(mesh):
    placed = (P(None, None, "gx", "gy"), P(), P(), P(), P(), P(), P())
    return jax.shard_map(
        local,
        mesh=mesh,
        in_specs=placed,
        out_specs=(P(None, None, "gx", "gy"), P()),
        check_vma=False,
    )
```

```python
import functools

import jax
import jax.numpy as jnp
from jax import lax
from jax.experimental import pallas as pl
from jax.experimental.pallas import tpu as pltpu
from jax.sharding import PartitionSpec as P

M = 80
LEV = 4
NB = 4
TX = 32
TY = 256
CAP = 64
OBS = 2048
TILES = 128
EPS = 1e-05
F32 = jnp.float32
BF16 = jnp.bfloat16
SLAB = 16
PARTS = TX // SLAB
SLABS = LEV * PARTS

ROW_A = M
ROW_C = M + 1
ROW_W = M + 2
ROW_N = M + 11
ROWS = 96
TAPER = (0.25, 0.5, 0.25, 0.5, 1.0, 0.5, 0.25, 0.5, 0.25)


def split2(x):
    high = x.astype(BF16)
    return high, (x - high.astype(F32)).astype(BF16)


def split3(x):
    high = x.astype(BF16)
    rest = x - high.astype(F32)
    mid = rest.astype(BF16)
    return high, mid, (rest - mid.astype(F32)).astype(BF16)


def iota(shape, dim):
    return lax.broadcasted_iota(jnp.int32, shape, dim)


def dot(a, b, **kw):
    return jnp.dot(a, b, preferred_element_type=F32, **kw)


def dot_t(a, b, **kw):
    return lax.dot_general(a, b, (((1,), (1,)), ((), ())), preferred_element_type=F32, **kw)


def dot3(a, b, product=dot):
    ah, al = split2(a)
    bh, bl = split2(b)
    return product(ah, bh) + (product(ah, bl) + product(al, bh))


def pack(rows):
    return jnp.concatenate([rows[: ROWS // 2], rows[ROWS // 2 :]], axis=1)


def unpack(packed):
    return jnp.concatenate([packed[:, :CAP], packed[:, CAP:]], axis=0)


def make_payload(prior, meta):
    valid = meta[0:1] > 0.5
    value = meta[1:2]
    variance = jnp.where(valid, meta[2:3], 1.0)
    center = jnp.sum(prior, axis=0, keepdims=True) / M
    deviation = prior - center
    spread = jnp.sum(deviation * deviation, axis=0, keepdims=True) / (M - 1)
    total = spread + variance
    miss = value - center
    normed = jnp.where(valid, miss / jnp.sqrt(total), 0.0)
    a = spread / total * miss
    c = jnp.sqrt(variance / total) - 1.0
    d = jnp.where(valid, 1.0 / ((M - 1) * (spread + EPS)), 0.0)
    rows = [deviation, a, c]
    for i in range(9):
        if i == 4:
            rows.append(d)
        else:
            at = 3 + (i if i < 4 else i - 1)
            rows.append(d * (meta[at : at + 1] * TAPER[i]))
    rows.append(jnp.zeros((ROWS - M - 11, CAP), F32))
    return pack(jnp.concatenate(rows, axis=0)), normed


def init_kernel(order_hbm, value_hbm, variance_hbm, owner_hbm, cell_hbm, reach_hbm, x_hbm, out,
                order, value, variance, owner, cell, reach, surface, sems):
    small = [
        pltpu.make_async_copy(source, target, sems.at[i])
        for i, (source, target) in enumerate([
            (order_hbm, order), (owner_hbm, owner), (cell_hbm, cell),
            (value_hbm, value), (variance_hbm, variance), (reach_hbm, reach),
        ])
    ]
    load = pltpu.make_async_copy(x_hbm.at[:, 0], surface, sems.at[6])
    for copy in small:
        copy.start()
    load.start()
    me = lax.axis_index("gx") * lax.axis_size("gy") + lax.axis_index("gy")
    small[0].wait()
    small[1].wait()
    owned = jnp.concatenate([owner[pl.ds(order[k], 1), :] for k in range(NB)], axis=0) == me
    ownf = jnp.where(owned, 1.0, 0.0)
    chunks = OBS // 128
    own64 = jnp.concatenate([ownf[:, 128 * c : 128 * c + 128] for c in range(chunks)], axis=0).astype(BF16)
    upper = jnp.where(iota((128, 128), 0) < iota((128, 128), 1), 1.0, 0.0).astype(BF16)
    rows = NB * chunks
    r0, r1 = iota((rows, rows), 0), iota((rows, rows), 1)
    before = jnp.where((r1 < r0) & (((r0 - r1) & (NB - 1)) == 0), 1.0, 0.0).astype(BF16)
    base = dot(dot(before, own64).astype(BF16), jnp.ones((128, 128), BF16))
    rank64 = dot(own64, upper) + base
    rank = jnp.concatenate([rank64[NB * c : NB * c + NB] for c in range(chunks)], axis=1)
    rank = jnp.where(owned, rank, -1.0)
    slots = iota((CAP, OBS), 0).astype(F32)
    for copy in small[2:]:
        copy.wait()
    metas = []
    for k in range(NB):
        b = order[k]
        hot = jnp.where(rank[k : k + 1] == slots, 1.0, 0.0).astype(BF16)
        where = cell[pl.ds(b, 1), :]
        vh, vm, vl = split3(value[pl.ds(b, 1), :])
        rh, rm, rl = split3(variance[pl.ds(b, 1), :])
        parts = [
            reach[b].astype(F32),
            lax.shift_right_logical(where, 8).astype(F32),
            (where & 255).astype(F32),
            vh.astype(F32), vm.astype(F32), vl.astype(F32),
            rh.astype(F32), rm.astype(F32), rl.astype(F32),
            jnp.ones((1, OBS), F32),
            jnp.zeros((15, OBS), F32),
        ]
        metas.append(dot_t(jnp.concatenate(parts, axis=0).astype(BF16), hot))
    got = jnp.concatenate(metas, axis=1)
    out[M:] = jnp.concatenate(
        [
            got[16:17],
            got[10:11] + got[11:12] + got[12:13],
            got[13:14] + got[14:15] + got[15:16],
            got[:8],
            jnp.zeros((5, NB * CAP), F32),
        ],
        axis=0,
    )
    hot_y = jnp.where(got[9:10] == iota((TY, NB * CAP), 0).astype(F32), 1.0, 0.0).astype(BF16)
    hot_x = jnp.where(got[8:9] == iota((TX, NB * CAP), 0).astype(F32), 1.0, 0.0)
    load.wait()
    group = 16
    for g in range(M // group):
        h, m, l = split3(surface[group * g : group * g + group].reshape(group * TX, TY))
        picked = dot(h, hot_y) + dot(m, hot_y) + dot(l, hot_y)
        out[group * g : group * g + group] = jnp.sum(
            picked.reshape(group, TX, NB * CAP) * hot_x[None], axis=1
        )


def core_of():
    return lax.rem(lax.axis_index("gx"), 2)


def edge(index, count):
    return (index == 0) | (index == count - 1)


def upward(index):
    return lax.rem(index + core_of(), 2) == 0


def emit(k, z, z_out, pay_out, edge_out, news_out=None):
    pays = []
    at = slice(CAP * k, CAP * k + CAP)
    news = []
    for t in range(2):
        pay, normed = make_payload(z[t][:M, at], z[t][M:, at])
        pay_out[t] = pay
        z_out[t, ROW_N : ROW_N + 1, at] = normed
        pays.append(pay)
        news.append(normed)
    edge_out[: ROWS // 2] = jnp.where(upward(lax.axis_index("gx") // 2), pays[1], pays[0])
    if news_out is not None:
        rows = [
            jnp.concatenate([z[t][ROW_N : ROW_N + 1, CAP * i : CAP * i + CAP] for t in range(2)], axis=1) for i in range(k)
        ]
        rows.append(jnp.concatenate(news, axis=1))
        rows.append(jnp.zeros((8 - NB, 2 * CAP), F32))
        block = jnp.concatenate(rows, axis=0)
        edge_out[ROWS // 2 :] = block
        news_out[...] = block


def start_kernel(own, sib, z_out, pay_out, edge_out):
    first = core_of() == 0
    mine, other = own[...], sib[...]
    z = [jnp.where(first, mine, other), jnp.where(first, other, mine)]
    unit = jnp.where(iota((ROWS, 128), 0) == iota((ROWS, 128), 1), 1.0, 0.0)
    unit = jnp.where(iota((ROWS, 128), 0) < M, unit, 0.0)
    for t in range(2):
        z_out[t, :, : NB * CAP] = z[t]
        z_out[t, :, NB * CAP :] = unit
    emit(0, z, z_out, pay_out, edge_out)


def right_side(rows):
    return rows[ROW_A : ROW_A + 1] + rows[ROW_C : ROW_C + 1] * rows[:M]


def factor(rows, dx, dy):
    at = ROW_W + 3 * (dx + 1) + dy + 1
    return rows[at : at + 1]


def toward(rows, dx):
    return jnp.where(upward(lax.axis_index("gy")), factor(rows, dx, 1), factor(rows, dx, -1))


def level(rows, dx):
    return factor(rows, dx, 0)


def inner(pay, weight):
    blocks = [unpack(pay[t]) for t in range(2)]
    right = jnp.concatenate([right_side(b) for b in blocks], axis=1)
    return [
        dot3(right, jnp.concatenate([b[:M] * weight(b, t - i) for i, b in enumerate(blocks)], axis=1), dot_t)
        for t in range(2)
    ]


def outer(far, sib_far, weight):
    y, chips = lax.axis_index("gx") // 2, lax.axis_size("gx") // 2
    up = upward(y)
    first = core_of() == 0
    ends = edge(y, chips)
    far = jnp.where(ends & jnp.logical_not(first), 0.0, far[: ROWS // 2])
    sib_far = jnp.where(ends & first, 0.0, sib_far[: ROWS // 2])
    blocks = [unpack(jnp.where(up, sib_far, far)), unpack(jnp.where(up, far, sib_far))]
    return [dot3(right_side(b), b[:M] * weight(b, dx), dot_t) for b, dx in zip(blocks, (1, -1))]


def own_kernel(k, order, owner, pay, toward_out, level_out, rank_out):
    for t, value in enumerate(inner(pay, toward)):
        toward_out[t] = value
    for t, value in enumerate(inner(pay, level)):
        level_out[t] = value
    row = owner[pl.ds(order[k], 1), :]
    upper = jnp.where(iota((128, 128), 0) < iota((128, 128), 1), 1.0, 0.0).astype(BF16)
    tiles = iota((TILES, 128), 0)
    base = jnp.zeros((TILES, 1), F32)
    for c in range(OBS // 128):
        at = slice(128 * c, 128 * c + 128)
        hot = jnp.where(row[:, at] == tiles, 1.0, 0.0)
        rank = dot(hot.astype(BF16), upper) + base
        rank_out[:, at] = jnp.sum(hot * rank, axis=0, keepdims=True)
        base = base + jnp.sum(hot, axis=1, keepdims=True)


def send_kernel(own, far, sib_far, out):
    for t, value in enumerate(outer(far, sib_far, toward)):
        out[t] = own[t] + value


def same_kernel(own, far, sib_far, out):
    for t, value in enumerate(outer(far, sib_far, level)):
        out[t] = own[t] + value


def column_kernel(news, far, sib_far, across, out):
    first = core_of() == 0
    at = slice(ROWS // 2, ROWS // 2 + NB)
    mine, other = far[at], sib_far[at]
    column = jnp.concatenate(
        [news[:NB], jnp.where(first, mine, other), across[:NB], jnp.where(first, other, mine)], axis=0
    )
    out[...] = jnp.broadcast_to(column[None], out.shape)


def advance(z, gain):
    anomaly = z - jnp.sum(z, axis=0, keepdims=True) / M
    return z + dot3(gain, anomaly)


def whole_gain(t, q0, h, g):
    first = core_of() == 0
    ends = edge(lax.axis_index("gy"), lax.axis_size("gy"))
    return q0[t] + jnp.where(ends & jnp.logical_not(first), 0.0, h[t]) + jnp.where(ends & first, 0.0, g[t])


def step_kernel(k, q0, h, g, z, z_out, pay_out, edge_out, news_out=None):
    new = []
    for t in range(2):
        moved = advance(z[t, :M], whole_gain(t, q0, h, g))
        z_out[t, :M] = moved
        z_out[t, M:] = z[t, M:]
        new.append(jnp.concatenate([moved, z[t, M:]], axis=0))
    emit(k, new, z_out, pay_out, edge_out, news_out)


def final_kernel(q0, h, g, z, x, out, come, go, come_sems, go_sems):
    def part(ref, i):
        return ref.at[:, i // PARTS, pl.ds((i % PARTS) * SLAB, SLAB), :]

    loads = [pltpu.make_async_copy(part(x, i), come.at[i], come_sems.at[i]) for i in range(SLABS)]
    stores = [pltpu.make_async_copy(go.at[i], part(out, i), go_sems.at[i]) for i in range(SLABS)]
    for load in loads:
        load.start()
    c = core_of()
    t = advance(z[c, :M, NB * CAP :], whole_gain(c, q0, h, g))[:, :M]
    th, tl = split2(t)
    w = jnp.concatenate([th, th, tl], axis=1)
    for i in range(SLABS):
        loads[i].wait()
        for j in range(0, SLAB, 8):
            turned = jnp.swapaxes(come[i, :, j : j + 8, :], 0, 1)
            rows = []
            for r in range(8):
                xh, xl = split2(turned[r])
                rows.append(dot(w, jnp.concatenate([xh, xl, xh], axis=0))[None])
            go[i, :, j : j + 8, :] = jnp.swapaxes(jnp.concatenate(rows, axis=0), 0, 1)
        stores[i].start()
    for store in stores:
        store.wait()


def place_kernel(order, owner, gathered, r0, r1, r2, r3, out):
    y = lax.axis_index("gx") // 2
    tiles = iota((TILES, OBS), 0)
    slots = iota((CAP, OBS), 0).astype(F32)
    rows = gathered.reshape(TILES // 2 * NB, 2 * CAP)
    for k, rank in enumerate((r0, r1, r2, r3)):
        b = order[k]
        tile = owner[pl.ds(b, 1), :]
        place = ((tile >> 4) & 1) * (TILES // 2) + (tile & 15) * 4 + ((tile >> 5) ^ y)
        turned = rows[pl.ds(k, TILES // 2, stride=NB), :].T
        table = jnp.concatenate([turned[:CAP], turned[CAP:]], axis=1)
        if k < NB // 2:
            chunks = [slice(at, at + 128) for at in range(0, OBS, 128)]
            got = jnp.concatenate([
                jnp.take_along_axis(table, jnp.broadcast_to(place[:, at], (CAP, 128)), axis=1) for at in chunks
            ], axis=1)
        else:
            hot = jnp.where(place == tiles, 1.0, 0.0).astype(BF16)
            both = dot(jnp.concatenate(split2(table), axis=0), hot)
            got = both[:CAP] + both[CAP:]
        out[pl.ds(b, 1), :] = jnp.sum(jnp.where(rank[...] == slots, got, 0.0), axis=0, keepdims=True)


VMEM = pl.BlockSpec(memory_space=pltpu.VMEM)
SMEM = pl.BlockSpec(memory_space=pltpu.SMEM)
HBM = pl.BlockSpec(memory_space=pltpu.HBM)


def shape(*dims):
    return jax.ShapeDtypeStruct(dims, F32)


def swaps(pairs):
    return pairs + [(high, low) for low, high in pairs]


def local(ensemble, obs_value, obs_variance, obs_owner, obs_cell, obs_reach, batch_order):
    params = pltpu.CompilerParams(vmem_limit_bytes=32 * 2**20)
    call = functools.partial(pl.pallas_call, compiler_params=params)
    width, height = lax.axis_size("gx"), lax.axis_size("gy")
    both = ("gx", "gy")
    core = swaps([(x, x + 1) for x in range(0, width, 2)])
    chips = width // 2
    side_x = swaps([(2 * y + c, 2 * ((y + 1) % chips) + c) for c in range(2) for y in range(c, chips, 2)])
    side_y = swaps([
        (x * height + k, x * height + k + 1) for x in range(width) for k in range(x % 2, height - 1, 2)
    ] + [(x * height + k, (x + 2) * height + k) for x in range(1, width, 4) for k in (0, height - 1)])
    pay_shapes = (shape(2, ROWS // 2, 128), shape(ROWS // 2, 128))
    z_shape = shape(2, ROWS, NB * CAP + 128)
    row = pltpu.VMEM((NB, OBS), F32)
    row_i = pltpu.VMEM((NB, OBS), jnp.int32)
    own = call(
        init_kernel,
        out_shape=shape(ROWS, NB * CAP),
        in_specs=[HBM] * 7,
        out_specs=VMEM,
        scratch_shapes=[
            pltpu.SMEM((NB,), jnp.int32), row, row, row_i, row_i,
            pltpu.VMEM((NB, 8, OBS), jnp.int32), pltpu.VMEM((M, TX, TY), F32), pltpu.SemaphoreType.DMA((7,)),
        ],
        name="init",
    )(*(
        pltpu.with_memory_space_constraint(value, pltpu.HBM)
        for value in (
            batch_order, obs_value, obs_variance, obs_owner, obs_cell, jnp.swapaxes(obs_reach, 1, 2), ensemble
        )
    ))
    z, pay, edge = call(
        start_kernel,
        out_shape=(z_shape,) + pay_shapes,
        in_specs=[VMEM] * 2,
        out_specs=(VMEM,) * 3,
        name="start",
    )(own, lax.ppermute(own, "gx", core))
    ranks = []
    for k in range(NB):
        last = k + 1 == NB
        far = lax.ppermute(edge, "gx", side_x)
        own_toward, own_level, rank = call(
            functools.partial(own_kernel, k),
            out_shape=(shape(2, M, M), shape(2, M, M), shape(1, OBS)),
            in_specs=[SMEM, VMEM, VMEM],
            out_specs=(VMEM,) * 3,
            name="own",
        )(batch_order, obs_owner, pay)
        far, own_toward = lax.optimization_barrier((far, own_toward))
        sib_far = lax.ppermute(far, "gx", core)
        send = call(send_kernel, out_shape=shape(2, M, M), in_specs=[VMEM] * 3, out_specs=VMEM, name="send")(
            own_toward, far, sib_far
        )
        send, sib_far = lax.optimization_barrier((send, sib_far))
        h = lax.ppermute(send, both, side_y)
        q0 = call(same_kernel, out_shape=shape(2, M, M), in_specs=[VMEM] * 3, out_specs=VMEM, name="same")(
            own_level, far, sib_far
        )
        ranks.append(rank)
        if last:
            across = lax.ppermute(sib_far[ROWS // 2 :], "gx", side_x)
            column = call(
                column_kernel, out_shape=shape(height, 4 * NB, 128), in_specs=[VMEM] * 4, out_specs=VMEM, name="column"
            )(news, far, sib_far, across)
        if last:
            h, q0, column = lax.optimization_barrier((h, q0, column))
            gathered = lax.all_to_all(column, "gy", 0, 0, tiled=True)
        else:
            h, q0 = lax.optimization_barrier((h, q0))
        g = lax.ppermute(h, "gx", core)
        if not last:
            tail = k + 2 == NB
            edge_shape = (shape(ROWS // 2 + 8, 128), shape(8, 128)) if tail else pay_shapes[1:]
            z, pay, edge, *rest = call(
                functools.partial(step_kernel, k + 1),
                out_shape=(z_shape, pay_shapes[0]) + edge_shape,
                in_specs=[VMEM] * 4,
                out_specs=(VMEM,) * (4 if tail else 3),
                name="step",
            )(q0, h, g, z)
            if tail:
                news = rest[0]
    slabs = pltpu.VMEM((SLABS, M, SLAB, TY), F32)
    state = call(
        final_kernel,
        out_shape=shape(M, LEV, TX, TY),
        in_specs=[VMEM] * 4 + [HBM],
        out_specs=HBM,
        scratch_shapes=[slabs, slabs, pltpu.SemaphoreType.DMA((SLABS,)), pltpu.SemaphoreType.DMA((SLABS,))],
        cost_estimate=pl.CostEstimate(flops=6 * M * M * LEV * TX * TY, bytes_accessed=8 * M * LEV * TX * TY, transcendentals=0),
        name="final",
    )(q0, h, g, z, pltpu.with_memory_space_constraint(ensemble, pltpu.HBM))
    state, gathered = lax.optimization_barrier((state, gathered))
    innovation = call(
        place_kernel,
        out_shape=shape(NB, OBS),
        in_specs=[SMEM] + [VMEM] * 6,
        out_specs=VMEM,
        name="place",
    )(batch_order, obs_owner, gathered, *ranks)
    return state, innovation


def solution(mesh):
    placed = (P(None, None, "gx", "gy"), P(), P(), P(), P(), P(), P())
    return jax.shard_map(
        local,
        mesh=mesh,
        in_specs=placed,
        out_specs=(P(None, None, "gx", "gy"), P()),
        check_vma=False,
    )
```

```python
import functools

import jax
import jax.numpy as jnp
from jax import lax
from jax.experimental import pallas as pl
from jax.experimental.pallas import tpu as pltpu
from jax.sharding import PartitionSpec as P

M = 80
LEV = 4
NB = 4
TX = 32
TY = 256
CAP = 64
OBS = 2048
TILES = 128
EPS = 1e-05
F32 = jnp.float32
BF16 = jnp.bfloat16
SLAB = 16
PARTS = TX // SLAB
SLABS = LEV * PARTS
EARLY = 2

ROW_A = M
ROW_C = M + 1
ROW_W = M + 2
ROW_N = M + 11
ROWS = 96
TAPER = (0.25, 0.5, 0.25, 0.5, 1.0, 0.5, 0.25, 0.5, 0.25)


def split2(x):
    high = x.astype(BF16)
    return high, (x - high.astype(F32)).astype(BF16)


def split3(x):
    high = x.astype(BF16)
    rest = x - high.astype(F32)
    mid = rest.astype(BF16)
    return high, mid, (rest - mid.astype(F32)).astype(BF16)


def iota(shape, dim):
    return lax.broadcasted_iota(jnp.int32, shape, dim)


def dot(a, b, **kw):
    return jnp.dot(a, b, preferred_element_type=F32, **kw)


def dot_t(a, b, **kw):
    return lax.dot_general(a, b, (((1,), (1,)), ((), ())), preferred_element_type=F32, **kw)


def dot3(a, b, product=dot):
    ah, al = split2(a)
    bh, bl = split2(b)
    return product(ah, bh) + (product(ah, bl) + product(al, bh))


def pack(rows):
    return jnp.concatenate([rows[: ROWS // 2], rows[ROWS // 2 :]], axis=1)


def unpack(packed):
    return jnp.concatenate([packed[:, :CAP], packed[:, CAP:]], axis=0)


def make_payload(prior, meta):
    valid = meta[0:1] > 0.5
    value = meta[1:2]
    variance = jnp.where(valid, meta[2:3], 1.0)
    center = jnp.sum(prior, axis=0, keepdims=True) / M
    deviation = prior - center
    spread = jnp.sum(deviation * deviation, axis=0, keepdims=True) / (M - 1)
    total = spread + variance
    miss = value - center
    normed = jnp.where(valid, miss / jnp.sqrt(total), 0.0)
    a = spread / total * miss
    c = jnp.sqrt(variance / total) - 1.0
    d = jnp.where(valid, 1.0 / ((M - 1) * (spread + EPS)), 0.0)
    rows = [deviation, a, c]
    for i in range(9):
        if i == 4:
            rows.append(d)
        else:
            at = 3 + (i if i < 4 else i - 1)
            rows.append(d * (meta[at : at + 1] * TAPER[i]))
    rows.append(jnp.zeros((ROWS - M - 11, CAP), F32))
    return pack(jnp.concatenate(rows, axis=0)), normed


def init_kernel(order_hbm, value_hbm, variance_hbm, owner_hbm, cell_hbm, reach_hbm, x_hbm, out,
                order, value, variance, owner, cell, reach, surface, sems):
    small = [
        pltpu.make_async_copy(source, target, sems.at[i])
        for i, (source, target) in enumerate([
            (order_hbm, order), (owner_hbm, owner), (cell_hbm, cell),
            (value_hbm, value), (variance_hbm, variance), (reach_hbm, reach),
        ])
    ]
    load = pltpu.make_async_copy(x_hbm.at[:, 0], surface, sems.at[6])
    for copy in small:
        copy.start()
    load.start()
    me = lax.axis_index("gx") * lax.axis_size("gy") + lax.axis_index("gy")
    small[0].wait()
    small[1].wait()
    owned = jnp.concatenate([owner[pl.ds(order[k], 1), :] for k in range(NB)], axis=0) == me
    ownf = jnp.where(owned, 1.0, 0.0)
    chunks = OBS // 128
    own64 = jnp.concatenate([ownf[:, 128 * c : 128 * c + 128] for c in range(chunks)], axis=0).astype(BF16)
    upper = jnp.where(iota((128, 128), 0) < iota((128, 128), 1), 1.0, 0.0).astype(BF16)
    rows = NB * chunks
    r0, r1 = iota((rows, rows), 0), iota((rows, rows), 1)
    before = jnp.where((r1 < r0) & (((r0 - r1) & (NB - 1)) == 0), 1.0, 0.0).astype(BF16)
    base = dot(dot(before, own64).astype(BF16), jnp.ones((128, 128), BF16))
    rank64 = dot(own64, upper) + base
    rank = jnp.concatenate([rank64[NB * c : NB * c + NB] for c in range(chunks)], axis=1)
    rank = jnp.where(owned, rank, -1.0)
    slots = iota((CAP, OBS), 0).astype(F32)
    for copy in small[2:]:
        copy.wait()
    metas = []
    for k in range(NB):
        b = order[k]
        hot = jnp.where(rank[k : k + 1] == slots, 1.0, 0.0).astype(BF16)
        where = cell[pl.ds(b, 1), :]
        vh, vm, vl = split3(value[pl.ds(b, 1), :])
        rh, rm, rl = split3(variance[pl.ds(b, 1), :])
        parts = [
            reach[b].astype(F32),
            lax.shift_right_logical(where, 8).astype(F32),
            (where & 255).astype(F32),
            vh.astype(F32), vm.astype(F32), vl.astype(F32),
            rh.astype(F32), rm.astype(F32), rl.astype(F32),
            jnp.ones((1, OBS), F32),
            jnp.zeros((15, OBS), F32),
        ]
        metas.append(dot_t(jnp.concatenate(parts, axis=0).astype(BF16), hot))
    got = jnp.concatenate(metas, axis=1)
    out[M:] = jnp.concatenate(
        [
            got[16:17],
            got[10:11] + got[11:12] + got[12:13],
            got[13:14] + got[14:15] + got[15:16],
            got[:8],
            jnp.zeros((5, NB * CAP), F32),
        ],
        axis=0,
    )
    hot_y = jnp.where(got[9:10] == iota((TY, NB * CAP), 0).astype(F32), 1.0, 0.0).astype(BF16)
    hot_x = jnp.where(got[8:9] == iota((TX, NB * CAP), 0).astype(F32), 1.0, 0.0)
    load.wait()
    group = 16
    for g in range(M // group):
        h, m, l = split3(surface[group * g : group * g + group].reshape(group * TX, TY))
        picked = dot(h, hot_y) + dot(m, hot_y) + dot(l, hot_y)
        out[group * g : group * g + group] = jnp.sum(
            picked.reshape(group, TX, NB * CAP) * hot_x[None], axis=1
        )


def core_of():
    return lax.rem(lax.axis_index("gx"), 2)


def edge(index, count):
    return (index == 0) | (index == count - 1)


def upward(index):
    return lax.rem(index + core_of(), 2) == 0


def emit(k, z, z_out, pay_out, edge_out, news_out=None):
    pays = []
    at = slice(CAP * k, CAP * k + CAP)
    news = []
    for t in range(2):
        pay, normed = make_payload(z[t][:M, at], z[t][M:, at])
        pay_out[t] = pay
        z_out[t, ROW_N : ROW_N + 1, at] = normed
        pays.append(pay)
        news.append(normed)
    edge_out[: ROWS // 2] = jnp.where(upward(lax.axis_index("gx") // 2), pays[1], pays[0])
    if news_out is not None:
        rows = [
            jnp.concatenate([z[t][ROW_N : ROW_N + 1, CAP * i : CAP * i + CAP] for t in range(2)], axis=1) for i in range(k)
        ]
        rows.append(jnp.concatenate(news, axis=1))
        rows.append(jnp.zeros((8 - NB, 2 * CAP), F32))
        block = jnp.concatenate(rows, axis=0)
        edge_out[ROWS // 2 :] = block
        news_out[...] = block


def start_kernel(own, sib, z_out, pay_out, edge_out):
    first = core_of() == 0
    mine, other = own[...], sib[...]
    z = [jnp.where(first, mine, other), jnp.where(first, other, mine)]
    unit = jnp.where(iota((ROWS, 128), 0) == iota((ROWS, 128), 1), 1.0, 0.0)
    unit = jnp.where(iota((ROWS, 128), 0) < M, unit, 0.0)
    for t in range(2):
        z_out[t, :, : NB * CAP] = z[t]
        z_out[t, :, NB * CAP :] = unit
    emit(0, z, z_out, pay_out, edge_out)


def right_side(rows):
    return rows[ROW_A : ROW_A + 1] + rows[ROW_C : ROW_C + 1] * rows[:M]


def factor(rows, dx, dy):
    at = ROW_W + 3 * (dx + 1) + dy + 1
    return rows[at : at + 1]


def toward(rows, dx):
    return jnp.where(upward(lax.axis_index("gy")), factor(rows, dx, 1), factor(rows, dx, -1))


def level(rows, dx):
    return factor(rows, dx, 0)


def inner(pay, weight):
    blocks = [unpack(pay[t]) for t in range(2)]
    right = jnp.concatenate([right_side(b) for b in blocks], axis=1)
    return [
        dot3(right, jnp.concatenate([b[:M] * weight(b, t - i) for i, b in enumerate(blocks)], axis=1), dot_t)
        for t in range(2)
    ]


def outer(far, sib_far, weight):
    y, chips = lax.axis_index("gx") // 2, lax.axis_size("gx") // 2
    up = upward(y)
    first = core_of() == 0
    ends = edge(y, chips)
    far = jnp.where(ends & jnp.logical_not(first), 0.0, far[: ROWS // 2])
    sib_far = jnp.where(ends & first, 0.0, sib_far[: ROWS // 2])
    blocks = [unpack(jnp.where(up, sib_far, far)), unpack(jnp.where(up, far, sib_far))]
    return [dot3(right_side(b), b[:M] * weight(b, dx), dot_t) for b, dx in zip(blocks, (1, -1))]


def own_kernel(k, order, owner, pay, toward_out, level_out, rank_out):
    for t, value in enumerate(inner(pay, toward)):
        toward_out[t] = value
    for t, value in enumerate(inner(pay, level)):
        level_out[t] = value
    row = owner[pl.ds(order[k], 1), :]
    upper = jnp.where(iota((128, 128), 0) < iota((128, 128), 1), 1.0, 0.0).astype(BF16)
    tiles = iota((TILES, 128), 0)
    base = jnp.zeros((TILES, 1), F32)
    for c in range(OBS // 128):
        at = slice(128 * c, 128 * c + 128)
        hot = jnp.where(row[:, at] == tiles, 1.0, 0.0)
        rank = dot(hot.astype(BF16), upper) + base
        rank_out[:, at] = jnp.sum(hot * rank, axis=0, keepdims=True)
        base = base + jnp.sum(hot, axis=1, keepdims=True)


def send_kernel(own, far, sib_far, out):
    for t, value in enumerate(outer(far, sib_far, toward)):
        out[t] = own[t] + value


def same_kernel(own, far, sib_far, out):
    for t, value in enumerate(outer(far, sib_far, level)):
        out[t] = own[t] + value


def column_kernel(news, far, sib_far, across, out):
    first = core_of() == 0
    at = slice(ROWS // 2, ROWS // 2 + NB)
    mine, other = far[at], sib_far[at]
    column = jnp.concatenate(
        [news[:NB], jnp.where(first, mine, other), across[:NB], jnp.where(first, other, mine)], axis=0
    )
    out[...] = jnp.broadcast_to(column[None], out.shape)


def advance(z, gain):
    anomaly = z - jnp.sum(z, axis=0, keepdims=True) / M
    return z + dot3(gain, anomaly)


def whole_gain(t, q0, h, g):
    first = core_of() == 0
    ends = edge(lax.axis_index("gy"), lax.axis_size("gy"))
    return q0[t] + jnp.where(ends & jnp.logical_not(first), 0.0, h[t]) + jnp.where(ends & first, 0.0, g[t])


def step_kernel(k, q0, h, g, z, z_out, pay_out, edge_out, news_out=None):
    new = []
    for t in range(2):
        moved = advance(z[t, :M], whole_gain(t, q0, h, g))
        z_out[t, :M] = moved
        z_out[t, M:] = z[t, M:]
        new.append(jnp.concatenate([moved, z[t, M:]], axis=0))
    emit(k, new, z_out, pay_out, edge_out, news_out)


def early_kernel(x, out, sems):
    loads = [pltpu.make_async_copy(part(x, i), out.at[i], sems.at[i]) for i in range(EARLY)]
    for load in loads:
        load.start()
    for load in loads:
        load.wait()


def part(ref, i, at=0, rows=SLAB):
    return ref.at[:, i // PARTS, pl.ds((i % PARTS) * SLAB + at, rows), :]


def final_kernel(q0, h, g, z, early, x, out, come, go, come_sems, go_sems):
    loads = [pltpu.make_async_copy(part(x, i), come.at[i - EARLY], come_sems.at[i - EARLY]) for i in range(EARLY, SLABS)]
    for load in loads:
        load.start()
    c = core_of()
    t = advance(z[c, :M, NB * CAP :], whole_gain(c, q0, h, g))[:, :M]
    th, tl = split2(t)
    w = jnp.concatenate([th, th, tl], axis=1)
    stores = []
    for i in range(SLABS):
        if i >= EARLY:
            loads[i - EARLY].wait()
        for j in range(0, SLAB, 8):
            block = early[i, :, j : j + 8, :] if i < EARLY else come[i - EARLY, :, j : j + 8, :]
            turned = jnp.swapaxes(block, 0, 1)
            rows = []
            for r in range(8):
                xh, xl = split2(turned[r])
                rows.append(dot(w, jnp.concatenate([xh, xl, xh], axis=0))[None])
            go[i, :, j : j + 8, :] = jnp.swapaxes(jnp.concatenate(rows, axis=0), 0, 1)
            sem = go_sems.at[i * (SLAB // 8) + j // 8]
            stores.append(pltpu.make_async_copy(go.at[i, :, pl.ds(j, 8), :], part(out, i, j, 8), sem))
            stores[-1].start()
    for store in stores:
        store.wait()


def place_kernel(order, owner, gathered, r0, r1, r2, r3, out):
    y = lax.axis_index("gx") // 2
    tiles = iota((TILES, OBS), 0)
    slots = iota((CAP, OBS), 0).astype(F32)
    rows = gathered.reshape(TILES // 2 * NB, 2 * CAP)
    for k, rank in enumerate((r0, r1, r2, r3)):
        b = order[k]
        tile = owner[pl.ds(b, 1), :]
        place = ((tile >> 4) & 1) * (TILES // 2) + (tile & 15) * 4 + ((tile >> 5) ^ y)
        turned = rows[pl.ds(k, TILES // 2, stride=NB), :].T
        table = jnp.concatenate([turned[:CAP], turned[CAP:]], axis=1)
        if k < NB // 2:
            chunks = [slice(at, at + 128) for at in range(0, OBS, 128)]
            got = jnp.concatenate([
                jnp.take_along_axis(table, jnp.broadcast_to(place[:, at], (CAP, 128)), axis=1) for at in chunks
            ], axis=1)
        else:
            hot = jnp.where(place == tiles, 1.0, 0.0).astype(BF16)
            both = dot(jnp.concatenate(split2(table), axis=0), hot)
            got = both[:CAP] + both[CAP:]
        out[pl.ds(b, 1), :] = jnp.sum(jnp.where(rank[...] == slots, got, 0.0), axis=0, keepdims=True)


VMEM = pl.BlockSpec(memory_space=pltpu.VMEM)
SMEM = pl.BlockSpec(memory_space=pltpu.SMEM)
HBM = pl.BlockSpec(memory_space=pltpu.HBM)


def shape(*dims):
    return jax.ShapeDtypeStruct(dims, F32)


def swaps(pairs):
    return pairs + [(high, low) for low, high in pairs]


def local(ensemble, obs_value, obs_variance, obs_owner, obs_cell, obs_reach, batch_order):
    params = pltpu.CompilerParams(vmem_limit_bytes=32 * 2**20)
    call = functools.partial(pl.pallas_call, compiler_params=params)
    width, height = lax.axis_size("gx"), lax.axis_size("gy")
    both = ("gx", "gy")
    core = swaps([(x, x + 1) for x in range(0, width, 2)])
    chips = width // 2
    side_x = swaps([(2 * y + c, 2 * ((y + 1) % chips) + c) for c in range(2) for y in range(c, chips, 2)])
    side_y = swaps([
        (x * height + k, x * height + k + 1) for x in range(width) for k in range(x % 2, height - 1, 2)
    ] + [(x * height + k, (x + 2) * height + k) for x in range(1, width, 4) for k in (0, height - 1)])
    pay_shapes = (shape(2, ROWS // 2, 128), shape(ROWS // 2, 128))
    z_shape = shape(2, ROWS, NB * CAP + 128)
    row = pltpu.VMEM((NB, OBS), F32)
    row_i = pltpu.VMEM((NB, OBS), jnp.int32)
    own = call(
        init_kernel,
        out_shape=shape(ROWS, NB * CAP),
        in_specs=[HBM] * 7,
        out_specs=VMEM,
        scratch_shapes=[
            pltpu.SMEM((NB,), jnp.int32), row, row, row_i, row_i,
            pltpu.VMEM((NB, 8, OBS), jnp.int32), pltpu.VMEM((M, TX, TY), F32), pltpu.SemaphoreType.DMA((7,)),
        ],
        name="init",
    )(*(
        pltpu.with_memory_space_constraint(value, pltpu.HBM)
        for value in (
            batch_order, obs_value, obs_variance, obs_owner, obs_cell, jnp.swapaxes(obs_reach, 1, 2), ensemble
        )
    ))
    z, pay, edge = call(
        start_kernel,
        out_shape=(z_shape,) + pay_shapes,
        in_specs=[VMEM] * 2,
        out_specs=(VMEM,) * 3,
        name="start",
    )(own, lax.ppermute(own, "gx", core))
    ranks = []
    state_hbm = pltpu.with_memory_space_constraint(ensemble, pltpu.HBM)
    for k in range(NB):
        last = k + 1 == NB
        far = lax.ppermute(edge, "gx", side_x)
        own_toward, own_level, rank = call(
            functools.partial(own_kernel, k),
            out_shape=(shape(2, M, M), shape(2, M, M), shape(1, OBS)),
            in_specs=[SMEM, VMEM, VMEM],
            out_specs=(VMEM,) * 3,
            name="own",
        )(batch_order, obs_owner, pay)
        if last:
            early = call(
                early_kernel,
                out_shape=shape(EARLY, M, SLAB, TY),
                in_specs=[HBM],
                out_specs=VMEM,
                scratch_shapes=[pltpu.SemaphoreType.DMA((EARLY,))],
                name="early",
            )(state_hbm)
            far, own_toward, early = lax.optimization_barrier((far, own_toward, early))
        else:
            far, own_toward = lax.optimization_barrier((far, own_toward))
        sib_far = lax.ppermute(far, "gx", core)
        send = call(send_kernel, out_shape=shape(2, M, M), in_specs=[VMEM] * 3, out_specs=VMEM, name="send")(
            own_toward, far, sib_far
        )
        send, sib_far = lax.optimization_barrier((send, sib_far))
        h = lax.ppermute(send, both, side_y)
        q0 = call(same_kernel, out_shape=shape(2, M, M), in_specs=[VMEM] * 3, out_specs=VMEM, name="same")(
            own_level, far, sib_far
        )
        ranks.append(rank)
        if last:
            across = lax.ppermute(sib_far[ROWS // 2 :], "gx", side_x)
            column = call(
                column_kernel, out_shape=shape(height, 4 * NB, 128), in_specs=[VMEM] * 4, out_specs=VMEM, name="column"
            )(news, far, sib_far, across)
        if last:
            h, q0, column = lax.optimization_barrier((h, q0, column))
            gathered = lax.all_to_all(column, "gy", 0, 0, tiled=True)
        else:
            h, q0 = lax.optimization_barrier((h, q0))
        g = lax.ppermute(h, "gx", core)
        if not last:
            tail = k + 2 == NB
            edge_shape = (shape(ROWS // 2 + 8, 128), shape(8, 128)) if tail else pay_shapes[1:]
            z, pay, edge, *rest = call(
                functools.partial(step_kernel, k + 1),
                out_shape=(z_shape, pay_shapes[0]) + edge_shape,
                in_specs=[VMEM] * 4,
                out_specs=(VMEM,) * (4 if tail else 3),
                name="step",
            )(q0, h, g, z)
            if tail:
                news = rest[0]
    state = call(
        final_kernel,
        out_shape=shape(M, LEV, TX, TY),
        in_specs=[VMEM] * 5 + [HBM],
        out_specs=HBM,
        scratch_shapes=[
            pltpu.VMEM((SLABS - EARLY, M, SLAB, TY), F32), pltpu.VMEM((SLABS, M, SLAB, TY), F32),
            pltpu.SemaphoreType.DMA((SLABS - EARLY,)), pltpu.SemaphoreType.DMA((SLABS * SLAB // 8,)),
        ],
        cost_estimate=pl.CostEstimate(flops=6 * M * M * LEV * TX * TY, bytes_accessed=8 * M * LEV * TX * TY, transcendentals=0),
        name="final",
    )(q0, h, g, z, early, state_hbm)
    state, gathered = lax.optimization_barrier((state, gathered))
    innovation = call(
        place_kernel,
        out_shape=shape(NB, OBS),
        in_specs=[SMEM] + [VMEM] * 6,
        out_specs=VMEM,
        name="place",
    )(batch_order, obs_owner, gathered, *ranks)
    return state, innovation


def solution(mesh):
    placed = (P(None, None, "gx", "gy"), P(), P(), P(), P(), P(), P())
    return jax.shard_map(
        local,
        mesh=mesh,
        in_specs=placed,
        out_specs=(P(None, None, "gx", "gy"), P()),
        check_vma=False,
    )
```

```python
import functools

import jax
import jax.numpy as jnp
from jax import lax
from jax.experimental import pallas as pl
from jax.experimental.pallas import tpu as pltpu
from jax.sharding import PartitionSpec as P

M = 80
LEV = 4
NB = 4
TX = 32
TY = 256
CAP = 64
OBS = 2048
TILES = 128
EPS = 1e-05
F32 = jnp.float32
BF16 = jnp.bfloat16
SLAB = 16
PARTS = TX // SLAB
SLABS = LEV * PARTS
TURN = 2

ROW_A = M
ROW_C = M + 1
ROW_W = M + 2
ROW_N = M + 11
ROWS = 96
TAPER = (0.25, 0.5, 0.25, 0.5, 1.0, 0.5, 0.25, 0.5, 0.25)


def split2(x):
    high = x.astype(BF16)
    return high, (x - high.astype(F32)).astype(BF16)


def split3(x):
    high = x.astype(BF16)
    rest = x - high.astype(F32)
    mid = rest.astype(BF16)
    return high, mid, (rest - mid.astype(F32)).astype(BF16)


def iota(shape, dim):
    return lax.broadcasted_iota(jnp.int32, shape, dim)


def dot(a, b, **kw):
    return jnp.dot(a, b, preferred_element_type=F32, **kw)


def dot_t(a, b, **kw):
    return lax.dot_general(a, b, (((1,), (1,)), ((), ())), preferred_element_type=F32, **kw)


def dot3(a, b, product=dot):
    ah, al = split2(a)
    bh, bl = split2(b)
    return product(ah, bh) + (product(ah, bl) + product(al, bh))


def pack(rows):
    return jnp.concatenate([rows[: ROWS // 2], rows[ROWS // 2 :]], axis=1)


def unpack(packed):
    return jnp.concatenate([packed[:, :CAP], packed[:, CAP:]], axis=0)


def make_payload(prior, meta):
    valid = meta[0:1] > 0.5
    value = meta[1:2]
    variance = jnp.where(valid, meta[2:3], 1.0)
    center = jnp.sum(prior, axis=0, keepdims=True) / M
    deviation = prior - center
    spread = jnp.sum(deviation * deviation, axis=0, keepdims=True) / (M - 1)
    total = spread + variance
    miss = value - center
    normed = jnp.where(valid, miss / jnp.sqrt(total), 0.0)
    a = spread / total * miss
    c = jnp.sqrt(variance / total) - 1.0
    d = jnp.where(valid, 1.0 / ((M - 1) * (spread + EPS)), 0.0)
    rows = [deviation, a, c]
    for i in range(9):
        if i == 4:
            rows.append(d)
        else:
            at = 3 + (i if i < 4 else i - 1)
            rows.append(d * (meta[at : at + 1] * TAPER[i]))
    rows.append(jnp.zeros((ROWS - M - 11, CAP), F32))
    return pack(jnp.concatenate(rows, axis=0)), normed


def init_kernel(order_hbm, value_hbm, variance_hbm, owner_hbm, cell_hbm, reach_hbm, x_hbm, out,
                order, value, variance, owner, cell, reach, surface, sems):
    small = [
        pltpu.make_async_copy(source, target, sems.at[i])
        for i, (source, target) in enumerate([
            (order_hbm, order), (owner_hbm, owner), (cell_hbm, cell),
            (value_hbm, value), (variance_hbm, variance), (reach_hbm, reach),
        ])
    ]
    load = pltpu.make_async_copy(x_hbm.at[:, 0], surface, sems.at[6])
    for copy in small:
        copy.start()
    load.start()
    me = lax.axis_index("gx") * lax.axis_size("gy") + lax.axis_index("gy")
    small[0].wait()
    small[1].wait()
    owned = jnp.concatenate([owner[pl.ds(order[k], 1), :] for k in range(NB)], axis=0) == me
    ownf = jnp.where(owned, 1.0, 0.0)
    chunks = OBS // 128
    own64 = jnp.concatenate([ownf[:, 128 * c : 128 * c + 128] for c in range(chunks)], axis=0).astype(BF16)
    upper = jnp.where(iota((128, 128), 0) < iota((128, 128), 1), 1.0, 0.0).astype(BF16)
    rows = NB * chunks
    r0, r1 = iota((rows, rows), 0), iota((rows, rows), 1)
    before = jnp.where((r1 < r0) & (((r0 - r1) & (NB - 1)) == 0), 1.0, 0.0).astype(BF16)
    base = dot(dot(before, own64).astype(BF16), jnp.ones((128, 128), BF16))
    rank64 = dot(own64, upper) + base
    rank = jnp.concatenate([rank64[NB * c : NB * c + NB] for c in range(chunks)], axis=1)
    rank = jnp.where(owned, rank, -1.0)
    slots = iota((CAP, OBS), 0).astype(F32)
    for copy in small[2:]:
        copy.wait()
    metas = []
    for k in range(NB):
        b = order[k]
        hot = jnp.where(rank[k : k + 1] == slots, 1.0, 0.0).astype(BF16)
        where = cell[pl.ds(b, 1), :]
        vh, vm, vl = split3(value[pl.ds(b, 1), :])
        rh, rm, rl = split3(variance[pl.ds(b, 1), :])
        parts = [
            reach[b].astype(F32),
            lax.shift_right_logical(where, 8).astype(F32),
            (where & 255).astype(F32),
            vh.astype(F32), vm.astype(F32), vl.astype(F32),
            rh.astype(F32), rm.astype(F32), rl.astype(F32),
            jnp.ones((1, OBS), F32),
            jnp.zeros((15, OBS), F32),
        ]
        metas.append(dot_t(jnp.concatenate(parts, axis=0).astype(BF16), hot))
    got = jnp.concatenate(metas, axis=1)
    out[M:] = jnp.concatenate(
        [
            got[16:17],
            got[10:11] + got[11:12] + got[12:13],
            got[13:14] + got[14:15] + got[15:16],
            got[:8],
            jnp.zeros((5, NB * CAP), F32),
        ],
        axis=0,
    )
    hot_y = jnp.where(got[9:10] == iota((TY, NB * CAP), 0).astype(F32), 1.0, 0.0).astype(BF16)
    hot_x = jnp.where(got[8:9] == iota((TX, NB * CAP), 0).astype(F32), 1.0, 0.0)
    load.wait()
    group = 16
    for g in range(M // group):
        high, low = split2(surface[group * g : group * g + group].reshape(group * TX, TY))
        picked = dot(high, hot_y) + dot(low, hot_y)
        out[group * g : group * g + group] = jnp.sum(
            picked.reshape(group, TX, NB * CAP) * hot_x[None], axis=1
        )


def core_of():
    return lax.rem(lax.axis_index("gx"), 2)


def edge(index, count):
    return (index == 0) | (index == count - 1)


def upward(index):
    return lax.rem(index + core_of(), 2) == 0


def emit(k, z, z_out, pay_out, edge_out, news_out=None):
    pays = []
    at = slice(CAP * k, CAP * k + CAP)
    news = []
    for t in range(2):
        pay, normed = make_payload(z[t][:M, at], z[t][M:, at])
        pay_out[t] = pay
        z_out[t, ROW_N : ROW_N + 1, at] = normed
        pays.append(pay)
        news.append(normed)
    edge_out[: ROWS // 2] = jnp.where(upward(lax.axis_index("gx") // 2), pays[1], pays[0])
    if news_out is not None:
        rows = [
            jnp.concatenate([z[t][ROW_N : ROW_N + 1, CAP * i : CAP * i + CAP] for t in range(2)], axis=1) for i in range(k)
        ]
        rows.append(jnp.concatenate(news, axis=1))
        rows.append(jnp.zeros((8 - NB, 2 * CAP), F32))
        block = jnp.concatenate(rows, axis=0)
        edge_out[ROWS // 2 :] = block
        news_out[...] = block


def start_kernel(own, sib, z_out, pay_out, edge_out):
    first = core_of() == 0
    mine, other = own[...], sib[...]
    z = [jnp.where(first, mine, other), jnp.where(first, other, mine)]
    unit = jnp.where(iota((ROWS, 128), 0) == iota((ROWS, 128), 1), 1.0, 0.0)
    unit = jnp.where(iota((ROWS, 128), 0) < M, unit, 0.0)
    for t in range(2):
        z_out[t, :, : NB * CAP] = z[t]
        z_out[t, :, NB * CAP :] = unit
    emit(0, z, z_out, pay_out, edge_out)


def right_side(rows):
    return rows[ROW_A : ROW_A + 1] + rows[ROW_C : ROW_C + 1] * rows[:M]


def factor(rows, dx, dy):
    at = ROW_W + 3 * (dx + 1) + dy + 1
    return rows[at : at + 1]


def toward(rows, dx):
    return jnp.where(upward(lax.axis_index("gy")), factor(rows, dx, 1), factor(rows, dx, -1))


def level(rows, dx):
    return factor(rows, dx, 0)


def inner(pay, weight):
    blocks = [unpack(pay[t]) for t in range(2)]
    right = jnp.concatenate([right_side(b) for b in blocks], axis=1)
    return [
        dot3(right, jnp.concatenate([b[:M] * weight(b, t - i) for i, b in enumerate(blocks)], axis=1), dot_t)
        for t in range(2)
    ]


def outer(far, sib_far, weight):
    y, chips = lax.axis_index("gx") // 2, lax.axis_size("gx") // 2
    up = upward(y)
    first = core_of() == 0
    ends = edge(y, chips)
    far = jnp.where(ends & jnp.logical_not(first), 0.0, far[: ROWS // 2])
    sib_far = jnp.where(ends & first, 0.0, sib_far[: ROWS // 2])
    blocks = [unpack(jnp.where(up, sib_far, far)), unpack(jnp.where(up, far, sib_far))]
    return [dot3(right_side(b), b[:M] * weight(b, dx), dot_t) for b, dx in zip(blocks, (1, -1))]


def own_kernel(k, order, owner, pay, toward_out, level_out, rank_out):
    for t, value in enumerate(inner(pay, toward)):
        toward_out[t] = value
    for t, value in enumerate(inner(pay, level)):
        level_out[t] = value
    row = owner[pl.ds(order[k], 1), :]
    upper = jnp.where(iota((128, 128), 0) < iota((128, 128), 1), 1.0, 0.0).astype(BF16)
    tiles = iota((TILES, 128), 0)
    base = jnp.zeros((TILES, 1), F32)
    for c in range(OBS // 128):
        at = slice(128 * c, 128 * c + 128)
        hot = jnp.where(row[:, at] == tiles, 1.0, 0.0)
        rank = dot(hot.astype(BF16), upper) + base
        rank_out[:, at] = jnp.sum(hot * rank, axis=0, keepdims=True)
        base = base + jnp.sum(hot, axis=1, keepdims=True)


def send_kernel(own, far, sib_far, out):
    for t, value in enumerate(outer(far, sib_far, toward)):
        out[t] = own[t] + value


def same_kernel(own, far, sib_far, out):
    for t, value in enumerate(outer(far, sib_far, level)):
        out[t] = own[t] + value


def column_kernel(news, far, sib_far, across, out):
    first = core_of() == 0
    at = slice(ROWS // 2, ROWS // 2 + NB)
    mine, other = far[at], sib_far[at]
    column = jnp.concatenate(
        [news[:NB], jnp.where(first, mine, other), across[:NB], jnp.where(first, other, mine)], axis=0
    )
    out[...] = jnp.broadcast_to(column[None], out.shape)


def advance(z, gain):
    anomaly = z - jnp.sum(z, axis=0, keepdims=True) / M
    return z + dot3(gain, anomaly)


def whole_gain(t, q0, h, g):
    first = core_of() == 0
    ends = edge(lax.axis_index("gy"), lax.axis_size("gy"))
    return q0[t] + jnp.where(ends & jnp.logical_not(first), 0.0, h[t]) + jnp.where(ends & first, 0.0, g[t])


def step_kernel(k, q0, h, g, z, z_out, pay_out, edge_out, news_out=None):
    new = []
    for t in range(2):
        moved = advance(z[t, :M], whole_gain(t, q0, h, g))
        z_out[t, :M] = moved
        z_out[t, M:] = z[t, M:]
        new.append(jnp.concatenate([moved, z[t, M:]], axis=0))
    emit(k, new, z_out, pay_out, edge_out, news_out)


def part(ref, i):
    return ref.at[:, i // PARTS, pl.ds((i % PARTS) * SLAB, SLAB), :]


def turn(block, out, at):
    high, low = split2(jnp.swapaxes(block, 0, 1))
    out[at : at + 8, :M] = high
    out[at : at + 8, M:] = low


def turn_kernel(first, x, out, come, sems):
    loads = [pltpu.make_async_copy(part(x, first + i), come.at[i], sems.at[i]) for i in range(TURN)]
    for load in loads:
        load.start()
    for i in range(TURN):
        loads[i].wait()
        for j in range(0, SLAB, 8):
            turn(come[i, :, j : j + 8, :], out, SLAB * i + j)


def turn_away_kernel(first, x, out, come, turned, sems, out_sems):
    loads = [pltpu.make_async_copy(part(x, first + i), come.at[i], sems.at[i]) for i in range(TURN)]
    stores = [
        pltpu.make_async_copy(turned.at[pl.ds(SLAB * i, SLAB)], out.at[pl.ds(SLAB * i, SLAB)], out_sems.at[i])
        for i in range(TURN)
    ]
    for load in loads:
        load.start()
    for i in range(TURN):
        loads[i].wait()
        for j in range(0, SLAB, 8):
            turn(come[i, :, j : j + 8, :], turned, SLAB * i + j)
        stores[i].start()
    for store in stores:
        store.wait()


def final_kernel(q0, h, g, z, near, far0, far1, x, out, back, come, go, back_sems, come_sems, go_sems):
    loads = [
        pltpu.make_async_copy(
            (far0, far1)[i // TURN].at[pl.ds(SLAB * (i % TURN), SLAB)], back.at[pl.ds(SLAB * i, SLAB)], back_sems.at[i]
        )
        for i in range(2 * TURN)
    ]
    raw = 3 * TURN
    loads += [pltpu.make_async_copy(part(x, i), come.at[i - raw], come_sems.at[i - raw]) for i in range(raw, SLABS)]
    stores = [pltpu.make_async_copy(go.at[i], part(out, i), go_sems.at[i]) for i in range(SLABS)]
    for load in loads:
        load.start()
    c = core_of()
    t = advance(z[c, :M, NB * CAP :], whole_gain(c, q0, h, g))[:, :M]
    th, tl = split2(t)
    w = jnp.concatenate([th, th, tl], axis=1)
    for i in range(SLABS):
        if i >= TURN:
            loads[i - TURN].wait()
        for j in range(0, SLAB, 8):
            if i >= raw:
                turned = jnp.swapaxes(come[i - raw, :, j : j + 8, :], 0, 1)
            rows = []
            for r in range(8):
                if i >= raw:
                    xh, xl = split2(turned[r])
                    stack = [xh, xl, xh]
                else:
                    both = near[SLAB * i + j + r] if i < TURN else back[SLAB * (i - TURN) + j + r]
                    stack = [both, both[:M]]
                rows.append(dot(w, jnp.concatenate(stack, axis=0))[None])
            go[i, :, j : j + 8, :] = jnp.swapaxes(jnp.concatenate(rows, axis=0), 0, 1)
        stores[i].start()
    for store in stores:
        store.wait()


def place_kernel(order, owner, gathered, r0, r1, r2, r3, out):
    y = lax.axis_index("gx") // 2
    tiles = iota((TILES, OBS), 0)
    slots = iota((CAP, OBS), 0).astype(F32)
    rows = gathered.reshape(TILES // 2 * NB, 2 * CAP)
    for k, rank in enumerate((r0, r1, r2, r3)):
        b = order[k]
        tile = owner[pl.ds(b, 1), :]
        place = ((tile >> 4) & 1) * (TILES // 2) + (tile & 15) * 4 + ((tile >> 5) ^ y)
        turned = rows[pl.ds(k, TILES // 2, stride=NB), :].T
        table = jnp.concatenate([turned[:CAP], turned[CAP:]], axis=1)
        if k < NB // 2:
            chunks = [slice(at, at + 128) for at in range(0, OBS, 128)]
            got = jnp.concatenate([
                jnp.take_along_axis(table, jnp.broadcast_to(place[:, at], (CAP, 128)), axis=1) for at in chunks
            ], axis=1)
        else:
            hot = jnp.where(place == tiles, 1.0, 0.0).astype(BF16)
            both = dot(jnp.concatenate(split2(table), axis=0), hot)
            got = both[:CAP] + both[CAP:]
        out[pl.ds(b, 1), :] = jnp.sum(jnp.where(rank[...] == slots, got, 0.0), axis=0, keepdims=True)


VMEM = pl.BlockSpec(memory_space=pltpu.VMEM)
SMEM = pl.BlockSpec(memory_space=pltpu.SMEM)
HBM = pl.BlockSpec(memory_space=pltpu.HBM)


def shape(*dims):
    return jax.ShapeDtypeStruct(dims, F32)


def swaps(pairs):
    return pairs + [(high, low) for low, high in pairs]


def local(ensemble, obs_value, obs_variance, obs_owner, obs_cell, obs_reach, batch_order):
    params = pltpu.CompilerParams(vmem_limit_bytes=32 * 2**20)
    call = functools.partial(pl.pallas_call, compiler_params=params)
    width, height = lax.axis_size("gx"), lax.axis_size("gy")
    both = ("gx", "gy")
    core = swaps([(x, x + 1) for x in range(0, width, 2)])
    chips = width // 2
    side_x = swaps([(2 * y + c, 2 * ((y + 1) % chips) + c) for c in range(2) for y in range(c, chips, 2)])
    side_y = swaps([
        (x * height + k, x * height + k + 1) for x in range(width) for k in range(x % 2, height - 1, 2)
    ] + [(x * height + k, (x + 2) * height + k) for x in range(1, width, 4) for k in (0, height - 1)])
    pay_shapes = (shape(2, ROWS // 2, 128), shape(ROWS // 2, 128))
    z_shape = shape(2, ROWS, NB * CAP + 128)
    row = pltpu.VMEM((NB, OBS), F32)
    row_i = pltpu.VMEM((NB, OBS), jnp.int32)
    own = call(
        init_kernel,
        out_shape=shape(ROWS, NB * CAP),
        in_specs=[HBM] * 7,
        out_specs=VMEM,
        scratch_shapes=[
            pltpu.SMEM((NB,), jnp.int32), row, row, row_i, row_i,
            pltpu.VMEM((NB, 8, OBS), jnp.int32), pltpu.VMEM((M, TX, TY), F32), pltpu.SemaphoreType.DMA((7,)),
        ],
        name="init",
    )(*(
        pltpu.with_memory_space_constraint(value, pltpu.HBM)
        for value in (
            batch_order, obs_value, obs_variance, obs_owner, obs_cell, jnp.swapaxes(obs_reach, 1, 2), ensemble
        )
    ))
    z, pay, edge = call(
        start_kernel,
        out_shape=(z_shape,) + pay_shapes,
        in_specs=[VMEM] * 2,
        out_specs=(VMEM,) * 3,
        name="start",
    )(own, lax.ppermute(own, "gx", core))
    ranks, aways = [], []
    state_hbm = pltpu.with_memory_space_constraint(ensemble, pltpu.HBM)
    for k in range(NB):
        last = k + 1 == NB
        far = lax.ppermute(edge, "gx", side_x)
        own_toward, own_level, rank = call(
            functools.partial(own_kernel, k),
            out_shape=(shape(2, M, M), shape(2, M, M), shape(1, OBS)),
            in_specs=[SMEM, VMEM, VMEM],
            out_specs=(VMEM,) * 3,
            name="own",
        )(batch_order, obs_owner, pay)
        far, own_toward = lax.optimization_barrier((far, own_toward))
        sib_far = lax.ppermute(far, "gx", core)
        send = call(send_kernel, out_shape=shape(2, M, M), in_specs=[VMEM] * 3, out_specs=VMEM, name="send")(
            own_toward, far, sib_far
        )
        send, sib_far = lax.optimization_barrier((send, sib_far))
        h = lax.ppermute(send, both, side_y)
        q0 = call(same_kernel, out_shape=shape(2, M, M), in_specs=[VMEM] * 3, out_specs=VMEM, name="same")(
            own_level, far, sib_far
        )
        ranks.append(rank)
        if last:
            across = lax.ppermute(sib_far[ROWS // 2 :], "gx", side_x)
            column = call(
                column_kernel, out_shape=shape(height, 4 * NB, 128), in_specs=[VMEM] * 4, out_specs=VMEM, name="column"
            )(news, far, sib_far, across)
        if last:
            h, q0, column = lax.optimization_barrier((h, q0, column))
            gathered = lax.all_to_all(column, "gy", 0, 0, tiled=True)
        else:
            turned_shape = jax.ShapeDtypeStruct((TURN * SLAB, 2 * M, TY), BF16)
            come = pltpu.VMEM((TURN, M, SLAB, TY), F32)
            if k + 2 < NB:
                turned = call(
                    functools.partial(turn_away_kernel, TURN * (k + 1)),
                    out_shape=pltpu.HBM(turned_shape.shape, BF16),
                    in_specs=[HBM],
                    out_specs=HBM,
                    scratch_shapes=[
                        come, pltpu.VMEM((TURN * SLAB, 2 * M, TY), BF16),
                        pltpu.SemaphoreType.DMA((TURN,)), pltpu.SemaphoreType.DMA((TURN,)),
                    ],
                    name="turn",
                )(state_hbm)
                h, q0, turned = lax.optimization_barrier((h, q0, turned))
                aways.append(turned)
            else:
                near = call(
                    functools.partial(turn_kernel, 0),
                    out_shape=turned_shape,
                    in_specs=[HBM],
                    out_specs=VMEM,
                    scratch_shapes=[come, pltpu.SemaphoreType.DMA((TURN,))],
                    name="turn",
                )(state_hbm)
                h, q0, near = lax.optimization_barrier((h, q0, near))
        g = lax.ppermute(h, "gx", core)
        if not last:
            tail = k + 2 == NB
            edge_shape = (shape(ROWS // 2 + 8, 128), shape(8, 128)) if tail else pay_shapes[1:]
            z, pay, edge, *rest = call(
                functools.partial(step_kernel, k + 1),
                out_shape=(z_shape, pay_shapes[0]) + edge_shape,
                in_specs=[VMEM] * 4,
                out_specs=(VMEM,) * (4 if tail else 3),
                name="step",
            )(q0, h, g, z)
            if tail:
                news = rest[0]
    dma = lambda n: pltpu.SemaphoreType.DMA((n,))
    state = call(
        final_kernel,
        out_shape=shape(M, LEV, TX, TY),
        in_specs=[VMEM] * 5 + [HBM] * 3,
        out_specs=HBM,
        scratch_shapes=[
            pltpu.VMEM((2 * TURN * SLAB, 2 * M, TY), BF16),
            pltpu.VMEM((SLABS - 3 * TURN, M, SLAB, TY), F32),
            pltpu.VMEM((SLABS, M, SLAB, TY), F32),
            dma(2 * TURN), dma(SLABS - 3 * TURN), dma(SLABS),
        ],
        cost_estimate=pl.CostEstimate(flops=6 * M * M * LEV * TX * TY, bytes_accessed=8 * M * LEV * TX * TY, transcendentals=0),
        name="final",
    )(q0, h, g, z, near, *(pltpu.with_memory_space_constraint(value, pltpu.HBM) for value in aways), state_hbm)
    state, gathered = lax.optimization_barrier((state, gathered))
    innovation = call(
        place_kernel,
        out_shape=shape(NB, OBS),
        in_specs=[SMEM] + [VMEM] * 6,
        out_specs=VMEM,
        name="place",
    )(batch_order, obs_owner, gathered, *ranks)
    return state, innovation


def solution(mesh):
    placed = (P(None, None, "gx", "gy"), P(), P(), P(), P(), P(), P())
    return jax.shard_map(
        local,
        mesh=mesh,
        in_specs=placed,
        out_specs=(P(None, None, "gx", "gy"), P()),
        check_vma=False,
    )
```

```python
import functools

import jax
import jax.numpy as jnp
from jax import lax
from jax.experimental import pallas as pl
from jax.experimental.pallas import tpu as pltpu
from jax.sharding import PartitionSpec as P

M = 80
LEV = 4
NB = 4
TX = 32
TY = 256
CAP = 64
OBS = 2048
TILES = 128
EPS = 1e-05
F32 = jnp.float32
BF16 = jnp.bfloat16
SLAB = 16
PARTS = TX // SLAB
SLABS = LEV * PARTS
TURN = 2

ROW_A = M
ROW_C = M + 1
ROW_W = M + 2
ROW_N = M + 11
ROWS = 96
TAPER = (0.25, 0.5, 0.25, 0.5, 1.0, 0.5, 0.25, 0.5, 0.25)


def split2(x):
    high = x.astype(BF16)
    return high, (x - high.astype(F32)).astype(BF16)


def split3(x):
    high = x.astype(BF16)
    rest = x - high.astype(F32)
    mid = rest.astype(BF16)
    return high, mid, (rest - mid.astype(F32)).astype(BF16)


def iota(shape, dim):
    return lax.broadcasted_iota(jnp.int32, shape, dim)


def dot(a, b, **kw):
    return jnp.dot(a, b, preferred_element_type=F32, **kw)


def dot_t(a, b, **kw):
    return lax.dot_general(a, b, (((1,), (1,)), ((), ())), preferred_element_type=F32, **kw)


def dot3(a, b, product=dot):
    ah, al = split2(a)
    bh, bl = split2(b)
    return product(ah, bh) + (product(ah, bl) + product(al, bh))


def pack(rows):
    return jnp.concatenate([rows[: ROWS // 2], rows[ROWS // 2 :]], axis=1)


def unpack(packed):
    return jnp.concatenate([packed[:, :CAP], packed[:, CAP:]], axis=0)


def make_payload(prior, meta):
    valid = meta[0:1] > 0.5
    value = meta[1:2]
    variance = jnp.where(valid, meta[2:3], 1.0)
    center = jnp.sum(prior, axis=0, keepdims=True) / M
    deviation = prior - center
    spread = jnp.sum(deviation * deviation, axis=0, keepdims=True) / (M - 1)
    total = spread + variance
    miss = value - center
    normed = jnp.where(valid, miss / jnp.sqrt(total), 0.0)
    a = spread / total * miss
    c = jnp.sqrt(variance / total) - 1.0
    d = jnp.where(valid, 1.0 / ((M - 1) * (spread + EPS)), 0.0)
    rows = [deviation, a, c]
    for i in range(9):
        if i == 4:
            rows.append(d)
        else:
            at = 3 + (i if i < 4 else i - 1)
            rows.append(d * (meta[at : at + 1] * TAPER[i]))
    rows.append(jnp.zeros((ROWS - M - 11, CAP), F32))
    return pack(jnp.concatenate(rows, axis=0)), normed


def init_kernel(order_hbm, value_hbm, variance_hbm, owner_hbm, cell_hbm, reach_hbm, x_hbm, out,
                order, value, variance, owner, cell, reach, surface, sems):
    small = [
        pltpu.make_async_copy(source, target, sems.at[i])
        for i, (source, target) in enumerate([
            (order_hbm, order), (owner_hbm, owner), (cell_hbm, cell),
            (value_hbm, value), (variance_hbm, variance), (reach_hbm, reach),
        ])
    ]
    load = pltpu.make_async_copy(x_hbm.at[:, 0], surface, sems.at[6])
    for copy in small:
        copy.start()
    load.start()
    me = lax.axis_index("gx") * lax.axis_size("gy") + lax.axis_index("gy")
    small[0].wait()
    small[1].wait()
    owned = jnp.concatenate([owner[pl.ds(order[k], 1), :] for k in range(NB)], axis=0) == me
    ownf = jnp.where(owned, 1.0, 0.0)
    chunks = OBS // 128
    own64 = jnp.concatenate([ownf[:, 128 * c : 128 * c + 128] for c in range(chunks)], axis=0).astype(BF16)
    upper = jnp.where(iota((128, 128), 0) < iota((128, 128), 1), 1.0, 0.0).astype(BF16)
    rows = NB * chunks
    r0, r1 = iota((rows, rows), 0), iota((rows, rows), 1)
    before = jnp.where((r1 < r0) & (((r0 - r1) & (NB - 1)) == 0), 1.0, 0.0).astype(BF16)
    base = dot(dot(before, own64).astype(BF16), jnp.ones((128, 128), BF16))
    rank64 = dot(own64, upper) + base
    rank = jnp.concatenate([rank64[NB * c : NB * c + NB] for c in range(chunks)], axis=1)
    rank = jnp.where(owned, rank, -1.0)
    slots = iota((CAP, OBS), 0).astype(F32)
    for copy in small[2:]:
        copy.wait()
    metas = []
    for k in range(NB):
        b = order[k]
        hot = jnp.where(rank[k : k + 1] == slots, 1.0, 0.0).astype(BF16)
        where = cell[pl.ds(b, 1), :]
        vh, vm, vl = split3(value[pl.ds(b, 1), :])
        rh, rm, rl = split3(variance[pl.ds(b, 1), :])
        parts = [
            reach[b].astype(F32),
            lax.shift_right_logical(where, 8).astype(F32),
            (where & 255).astype(F32),
            vh.astype(F32), vm.astype(F32), vl.astype(F32),
            rh.astype(F32), rm.astype(F32), rl.astype(F32),
            jnp.ones((1, OBS), F32),
            jnp.zeros((15, OBS), F32),
        ]
        metas.append(dot_t(jnp.concatenate(parts, axis=0).astype(BF16), hot))
    got = jnp.concatenate(metas, axis=1)
    out[M:] = jnp.concatenate(
        [
            got[16:17],
            got[10:11] + got[11:12] + got[12:13],
            got[13:14] + got[14:15] + got[15:16],
            got[:8],
            jnp.zeros((5, NB * CAP), F32),
        ],
        axis=0,
    )
    hot_y = jnp.where(got[9:10] == iota((TY, NB * CAP), 0).astype(F32), 1.0, 0.0).astype(BF16)
    hot_x = jnp.where(got[8:9] == iota((TX, NB * CAP), 0).astype(F32), 1.0, 0.0)
    load.wait()
    group = 16
    for g in range(M // group):
        high, low = split2(surface[group * g : group * g + group].reshape(group * TX, TY))
        picked = dot(high, hot_y) + dot(low, hot_y)
        out[group * g : group * g + group] = jnp.sum(
            picked.reshape(group, TX, NB * CAP) * hot_x[None], axis=1
        )


def core_of():
    return lax.rem(lax.axis_index("gx"), 2)


def edge(index, count):
    return (index == 0) | (index == count - 1)


def upward(index):
    return lax.rem(index + core_of(), 2) == 0


def emit(k, z, z_out, pay_out, edge_out, news_out=None):
    pays = []
    at = slice(CAP * k, CAP * k + CAP)
    news = []
    for t in range(2):
        pay, normed = make_payload(z[t][:M, at], z[t][M:, at])
        pay_out[t] = pay
        z_out[t, ROW_N : ROW_N + 1, at] = normed
        pays.append(pay)
        news.append(normed)
    edge_out[: ROWS // 2] = jnp.where(upward(lax.axis_index("gx") // 2), pays[1], pays[0])
    if news_out is not None:
        rows = [
            jnp.concatenate([z[t][ROW_N : ROW_N + 1, CAP * i : CAP * i + CAP] for t in range(2)], axis=1) for i in range(k)
        ]
        rows.append(jnp.concatenate(news, axis=1))
        rows.append(jnp.zeros((8 - NB, 2 * CAP), F32))
        block = jnp.concatenate(rows, axis=0)
        edge_out[ROWS // 2 :] = block
        news_out[...] = block


def start_kernel(own, sib, z_out, pay_out, edge_out):
    first = core_of() == 0
    mine, other = own[...], sib[...]
    z = [jnp.where(first, mine, other), jnp.where(first, other, mine)]
    unit = jnp.where(iota((ROWS, 128), 0) == iota((ROWS, 128), 1), 1.0, 0.0)
    unit = jnp.where(iota((ROWS, 128), 0) < M, unit, 0.0)
    for t in range(2):
        z_out[t, :, : NB * CAP] = z[t]
        z_out[t, :, NB * CAP :] = unit
    emit(0, z, z_out, pay_out, edge_out)


def right_side(rows):
    return rows[ROW_A : ROW_A + 1] + rows[ROW_C : ROW_C + 1] * rows[:M]


def factor(rows, dx, dy):
    at = ROW_W + 3 * (dx + 1) + dy + 1
    return rows[at : at + 1]


def toward(rows, dx):
    return jnp.where(upward(lax.axis_index("gy")), factor(rows, dx, 1), factor(rows, dx, -1))


def level(rows, dx):
    return factor(rows, dx, 0)


def inner(pay, weight):
    blocks = [unpack(pay[t]) for t in range(2)]
    right = jnp.concatenate([right_side(b) for b in blocks], axis=1)
    return [
        dot3(right, jnp.concatenate([b[:M] * weight(b, t - i) for i, b in enumerate(blocks)], axis=1), dot_t)
        for t in range(2)
    ]


def outer(far, sib_far, weight):
    y, chips = lax.axis_index("gx") // 2, lax.axis_size("gx") // 2
    up = upward(y)
    first = core_of() == 0
    ends = edge(y, chips)
    far = jnp.where(ends & jnp.logical_not(first), 0.0, far[: ROWS // 2])
    sib_far = jnp.where(ends & first, 0.0, sib_far[: ROWS // 2])
    blocks = [unpack(jnp.where(up, sib_far, far)), unpack(jnp.where(up, far, sib_far))]
    return [dot3(right_side(b), b[:M] * weight(b, dx), dot_t) for b, dx in zip(blocks, (1, -1))]


def own_kernel(k, order, owner, pay, toward_out, level_out, rank_out):
    for t, value in enumerate(inner(pay, toward)):
        toward_out[t] = value
    for t, value in enumerate(inner(pay, level)):
        level_out[t] = value
    row = owner[pl.ds(order[k], 1), :]
    upper = jnp.where(iota((128, 128), 0) < iota((128, 128), 1), 1.0, 0.0).astype(BF16)
    tiles = iota((TILES, 128), 0)
    base = jnp.zeros((TILES, 1), F32)
    for c in range(OBS // 128):
        at = slice(128 * c, 128 * c + 128)
        hot = jnp.where(row[:, at] == tiles, 1.0, 0.0)
        rank = dot(hot.astype(BF16), upper) + base
        rank_out[:, at] = jnp.sum(hot * rank, axis=0, keepdims=True)
        base = base + jnp.sum(hot, axis=1, keepdims=True)


def send_kernel(own, far, sib_far, out):
    for t, value in enumerate(outer(far, sib_far, toward)):
        out[t] = own[t] + value


def same_kernel(own, far, sib_far, out):
    for t, value in enumerate(outer(far, sib_far, level)):
        out[t] = own[t] + value


def column_kernel(news, far, sib_far, across, out):
    first = core_of() == 0
    at = slice(ROWS // 2, ROWS // 2 + NB)
    mine, other = far[at], sib_far[at]
    column = jnp.concatenate(
        [news[:NB], jnp.where(first, mine, other), across[:NB], jnp.where(first, other, mine)], axis=0
    )
    out[...] = jnp.broadcast_to(column[None], out.shape)


def advance(z, gain):
    anomaly = z - jnp.sum(z, axis=0, keepdims=True) / M
    return z + dot3(gain, anomaly)


def whole_gain(t, q0, h, g):
    first = core_of() == 0
    ends = edge(lax.axis_index("gy"), lax.axis_size("gy"))
    return q0[t] + jnp.where(ends & jnp.logical_not(first), 0.0, h[t]) + jnp.where(ends & first, 0.0, g[t])


def step_kernel(k, q0, h, g, z, z_out, pay_out, edge_out, news_out=None):
    new = []
    for t in range(2):
        moved = advance(z[t, :M], whole_gain(t, q0, h, g))
        z_out[t, :M] = moved
        z_out[t, M:] = z[t, M:]
        new.append(jnp.concatenate([moved, z[t, M:]], axis=0))
    emit(k, new, z_out, pay_out, edge_out, news_out)


def part(ref, i):
    return ref.at[:, i // PARTS, pl.ds((i % PARTS) * SLAB, SLAB), :]


def turn(block, out, at):
    high, low = split2(jnp.swapaxes(block, 0, 1))
    out[at : at + 8, :M] = high
    out[at : at + 8, M:] = low


def turn_kernel(first, x, out, come, sems):
    loads = [pltpu.make_async_copy(part(x, first + i), come.at[i], sems.at[i]) for i in range(TURN)]
    for load in loads:
        load.start()
    for i in range(TURN):
        loads[i].wait()
        for j in range(0, SLAB, 8):
            turn(come[i, :, j : j + 8, :], out, SLAB * i + j)


def final_kernel(q0, h, g, z, x, out, mix, come, go, come_sems, go_sems):
    loads = [pltpu.make_async_copy(part(x, i), come.at[i], come_sems.at[i]) for i in range(SLABS - TURN)]
    stores = [pltpu.make_async_copy(go.at[i], part(out, i), go_sems.at[i]) for i in range(SLABS - TURN)]
    for load in loads:
        load.start()
    c = core_of()
    t = advance(z[c, :M, NB * CAP :], whole_gain(c, q0, h, g))[:, :M]
    th, tl = split2(t)
    w = jnp.concatenate([th, th, tl], axis=1)
    mix[...] = w
    for i in range(SLABS - TURN):
        loads[i].wait()
        for j in range(0, SLAB, 8):
            turned = jnp.swapaxes(come[i, :, j : j + 8, :], 0, 1)
            rows = []
            for r in range(8):
                xh, xl = split2(turned[r])
                rows.append(dot(w, jnp.concatenate([xh, xl, xh], axis=0))[None])
            go[i, :, j : j + 8, :] = jnp.swapaxes(jnp.concatenate(rows, axis=0), 0, 1)
        stores[i].start()
    for store in stores:
        store.wait()


def last_kernel(done, mix, near, order, owner, gathered, r0, r1, r2, r3, out, placed, go, go_sems):
    stores = [pltpu.make_async_copy(go.at[i], part(out, SLABS - TURN + i), go_sems.at[i]) for i in range(TURN)]
    w = mix[...]
    for i in range(TURN):
        for j in range(0, SLAB, 8):
            rows = []
            for r in range(8):
                both = near[SLAB * i + j + r]
                rows.append(dot(w, jnp.concatenate([both, both[:M]], axis=0))[None])
            go[i, :, j : j + 8, :] = jnp.swapaxes(jnp.concatenate(rows, axis=0), 0, 1)
        stores[i].start()
    place_kernel(order, owner, gathered, r0, r1, r2, r3, placed)
    for store in stores:
        store.wait()


def place_kernel(order, owner, gathered, r0, r1, r2, r3, out):
    y = lax.axis_index("gx") // 2
    tiles = iota((TILES, OBS), 0)
    slots = iota((CAP, OBS), 0).astype(F32)
    rows = gathered.reshape(TILES // 2 * NB, 2 * CAP)
    for k, rank in enumerate((r0, r1, r2, r3)):
        b = order[k]
        tile = owner[pl.ds(b, 1), :]
        place = ((tile >> 4) & 1) * (TILES // 2) + (tile & 15) * 4 + ((tile >> 5) ^ y)
        turned = rows[pl.ds(k, TILES // 2, stride=NB), :].T
        table = jnp.concatenate([turned[:CAP], turned[CAP:]], axis=1)
        if k < NB // 2:
            chunks = [slice(at, at + 128) for at in range(0, OBS, 128)]
            got = jnp.concatenate([
                jnp.take_along_axis(table, jnp.broadcast_to(place[:, at], (CAP, 128)), axis=1) for at in chunks
            ], axis=1)
        else:
            hot = jnp.where(place == tiles, 1.0, 0.0).astype(BF16)
            both = dot(jnp.concatenate(split2(table), axis=0), hot)
            got = both[:CAP] + both[CAP:]
        out[pl.ds(b, 1), :] = jnp.sum(jnp.where(rank[...] == slots, got, 0.0), axis=0, keepdims=True)


VMEM = pl.BlockSpec(memory_space=pltpu.VMEM)
SMEM = pl.BlockSpec(memory_space=pltpu.SMEM)
HBM = pl.BlockSpec(memory_space=pltpu.HBM)


def shape(*dims):
    return jax.ShapeDtypeStruct(dims, F32)


def swaps(pairs):
    return pairs + [(high, low) for low, high in pairs]


def local(ensemble, obs_value, obs_variance, obs_owner, obs_cell, obs_reach, batch_order):
    params = pltpu.CompilerParams(vmem_limit_bytes=32 * 2**20)
    call = functools.partial(pl.pallas_call, compiler_params=params)
    width, height = lax.axis_size("gx"), lax.axis_size("gy")
    both = ("gx", "gy")
    core = swaps([(x, x + 1) for x in range(0, width, 2)])
    chips = width // 2
    side_x = swaps([(2 * y + c, 2 * ((y + 1) % chips) + c) for c in range(2) for y in range(c, chips, 2)])
    side_y = swaps([
        (x * height + k, x * height + k + 1) for x in range(width) for k in range(x % 2, height - 1, 2)
    ] + [(x * height + k, (x + 2) * height + k) for x in range(1, width, 4) for k in (0, height - 1)])
    pay_shapes = (shape(2, ROWS // 2, 128), shape(ROWS // 2, 128))
    z_shape = shape(2, ROWS, NB * CAP + 128)
    row = pltpu.VMEM((NB, OBS), F32)
    row_i = pltpu.VMEM((NB, OBS), jnp.int32)
    own = call(
        init_kernel,
        out_shape=shape(ROWS, NB * CAP),
        in_specs=[HBM] * 7,
        out_specs=VMEM,
        scratch_shapes=[
            pltpu.SMEM((NB,), jnp.int32), row, row, row_i, row_i,
            pltpu.VMEM((NB, 8, OBS), jnp.int32), pltpu.VMEM((M, TX, TY), F32), pltpu.SemaphoreType.DMA((7,)),
        ],
        name="init",
    )(*(
        pltpu.with_memory_space_constraint(value, pltpu.HBM)
        for value in (
            batch_order, obs_value, obs_variance, obs_owner, obs_cell, jnp.swapaxes(obs_reach, 1, 2), ensemble
        )
    ))
    z, pay, edge = call(
        start_kernel,
        out_shape=(z_shape,) + pay_shapes,
        in_specs=[VMEM] * 2,
        out_specs=(VMEM,) * 3,
        name="start",
    )(own, lax.ppermute(own, "gx", core))
    ranks = []
    state_hbm = pltpu.with_memory_space_constraint(ensemble, pltpu.HBM)
    for k in range(NB):
        last = k + 1 == NB
        far = lax.ppermute(edge, "gx", side_x)
        own_toward, own_level, rank = call(
            functools.partial(own_kernel, k),
            out_shape=(shape(2, M, M), shape(2, M, M), shape(1, OBS)),
            in_specs=[SMEM, VMEM, VMEM],
            out_specs=(VMEM,) * 3,
            name="own",
        )(batch_order, obs_owner, pay)
        far, own_toward = lax.optimization_barrier((far, own_toward))
        sib_far = lax.ppermute(far, "gx", core)
        send = call(send_kernel, out_shape=shape(2, M, M), in_specs=[VMEM] * 3, out_specs=VMEM, name="send")(
            own_toward, far, sib_far
        )
        send, sib_far = lax.optimization_barrier((send, sib_far))
        h = lax.ppermute(send, both, side_y)
        q0 = call(same_kernel, out_shape=shape(2, M, M), in_specs=[VMEM] * 3, out_specs=VMEM, name="same")(
            own_level, far, sib_far
        )
        ranks.append(rank)
        if last:
            across = lax.ppermute(sib_far[ROWS // 2 :], "gx", side_x)
            column = call(
                column_kernel, out_shape=shape(height, 4 * NB, 128), in_specs=[VMEM] * 4, out_specs=VMEM, name="column"
            )(news, far, sib_far, across)
        if last:
            h, q0, column = lax.optimization_barrier((h, q0, column))
            gathered = lax.all_to_all(column, "gy", 0, 0, tiled=True)
        else:
            turned_shape = jax.ShapeDtypeStruct((TURN * SLAB, 2 * M, TY), BF16)
            come = pltpu.VMEM((TURN, M, SLAB, TY), F32)
            if k + 2 < NB:
                h, q0 = lax.optimization_barrier((h, q0))
            else:
                near = call(
                    functools.partial(turn_kernel, SLABS - TURN),
                    out_shape=turned_shape,
                    in_specs=[HBM],
                    out_specs=VMEM,
                    scratch_shapes=[come, pltpu.SemaphoreType.DMA((TURN,))],
                    name="turn",
                )(state_hbm)
                h, q0, near = lax.optimization_barrier((h, q0, near))
        g = lax.ppermute(h, "gx", core)
        if not last:
            tail = k + 2 == NB
            edge_shape = (shape(ROWS // 2 + 8, 128), shape(8, 128)) if tail else pay_shapes[1:]
            z, pay, edge, *rest = call(
                functools.partial(step_kernel, k + 1),
                out_shape=(z_shape, pay_shapes[0]) + edge_shape,
                in_specs=[VMEM] * 4,
                out_specs=(VMEM,) * (4 if tail else 3),
                name="step",
            )(q0, h, g, z)
            if tail:
                news = rest[0]
    dma = lambda n: pltpu.SemaphoreType.DMA((n,))
    state, mix = call(
        final_kernel,
        out_shape=(shape(M, LEV, TX, TY), jax.ShapeDtypeStruct((M, 3 * M), BF16)),
        in_specs=[VMEM] * 4 + [HBM],
        out_specs=(HBM, VMEM),
        scratch_shapes=[
            pltpu.VMEM((SLABS - TURN, M, SLAB, TY), F32),
            pltpu.VMEM((SLABS - TURN, M, SLAB, TY), F32),
            dma(SLABS - TURN), dma(SLABS - TURN),
        ],
        cost_estimate=pl.CostEstimate(flops=6 * M * M * LEV * TX * TY, bytes_accessed=8 * M * LEV * TX * TY, transcendentals=0),
        name="final",
    )(q0, h, g, z, state_hbm)
    mix, gathered = lax.optimization_barrier((mix, gathered))
    state, innovation = call(
        last_kernel,
        out_shape=(shape(M, LEV, TX, TY), shape(NB, OBS)),
        in_specs=[HBM, VMEM, VMEM, SMEM] + [VMEM] * 6,
        out_specs=(HBM, VMEM),
        scratch_shapes=[pltpu.VMEM((TURN, M, SLAB, TY), F32), dma(TURN)],
        input_output_aliases={0: 0},
        name="last",
    )(state, mix, near, batch_order, obs_owner, gathered, *ranks)
    return state, innovation


def solution(mesh):
    placed = (P(None, None, "gx", "gy"), P(), P(), P(), P(), P(), P())
    return jax.shard_map(
        local,
        mesh=mesh,
        in_specs=placed,
        out_specs=(P(None, None, "gx", "gy"), P()),
        check_vma=False,
    )
```

```python
import functools

import jax
import jax.numpy as jnp
from jax import lax
from jax.experimental import pallas as pl
from jax.experimental.pallas import tpu as pltpu
from jax.sharding import PartitionSpec as P

M = 80
LEV = 4
NB = 4
TX = 32
TY = 256
CAP = 64
OBS = 2048
TILES = 128
EPS = 1e-05
F32 = jnp.float32
BF16 = jnp.bfloat16
SLAB = 16
PARTS = TX // SLAB
SLABS = LEV * PARTS
TURN = 2

ROW_A = M
ROW_C = M + 1
ROW_W = M + 2
ROW_N = M + 11
ROWS = 96
TAPER = (0.25, 0.5, 0.25, 0.5, 1.0, 0.5, 0.25, 0.5, 0.25)


def split2(x):
    high = x.astype(BF16)
    return high, (x - high.astype(F32)).astype(BF16)


def split3(x):
    high = x.astype(BF16)
    rest = x - high.astype(F32)
    mid = rest.astype(BF16)
    return high, mid, (rest - mid.astype(F32)).astype(BF16)


def iota(shape, dim):
    return lax.broadcasted_iota(jnp.int32, shape, dim)


def dot(a, b, **kw):
    return jnp.dot(a, b, preferred_element_type=F32, **kw)


def dot_t(a, b, **kw):
    return lax.dot_general(a, b, (((1,), (1,)), ((), ())), preferred_element_type=F32, **kw)


def dot3(a, b, product=dot):
    ah, al = split2(a)
    bh, bl = split2(b)
    return product(ah, bh) + (product(ah, bl) + product(al, bh))


def pack(rows):
    return jnp.concatenate([rows[: ROWS // 2], rows[ROWS // 2 :]], axis=1)


def unpack(packed):
    return jnp.concatenate([packed[:, :CAP], packed[:, CAP:]], axis=0)


def make_payload(prior, meta):
    valid = meta[0:1] > 0.5
    value = meta[1:2]
    variance = jnp.where(valid, meta[2:3], 1.0)
    center = jnp.sum(prior, axis=0, keepdims=True) / M
    deviation = prior - center
    spread = jnp.sum(deviation * deviation, axis=0, keepdims=True) / (M - 1)
    total = spread + variance
    miss = value - center
    normed = jnp.where(valid, miss / jnp.sqrt(total), 0.0)
    a = spread / total * miss
    c = jnp.sqrt(variance / total) - 1.0
    d = jnp.where(valid, 1.0 / ((M - 1) * (spread + EPS)), 0.0)
    rows = [deviation, a, c]
    for i in range(9):
        if i == 4:
            rows.append(d)
        else:
            at = 3 + (i if i < 4 else i - 1)
            rows.append(d * (meta[at : at + 1] * TAPER[i]))
    rows.append(jnp.zeros((ROWS - M - 11, CAP), F32))
    return pack(jnp.concatenate(rows, axis=0)), normed


def init_kernel(order_hbm, value_hbm, variance_hbm, owner_hbm, cell_hbm, reach_hbm, x_hbm, out,
                order, value, variance, owner, cell, reach, surface, sems):
    small = [
        pltpu.make_async_copy(source, target, sems.at[i])
        for i, (source, target) in enumerate([
            (order_hbm, order), (owner_hbm, owner), (cell_hbm, cell),
            (value_hbm, value), (variance_hbm, variance), (reach_hbm, reach),
        ])
    ]
    load = pltpu.make_async_copy(x_hbm.at[:, 0], surface, sems.at[6])
    for copy in small:
        copy.start()
    load.start()
    me = lax.axis_index("gx") * lax.axis_size("gy") + lax.axis_index("gy")
    small[0].wait()
    small[1].wait()
    owned = jnp.concatenate([owner[pl.ds(order[k], 1), :] for k in range(NB)], axis=0) == me
    ownf = jnp.where(owned, 1.0, 0.0)
    chunks = OBS // 128
    own64 = jnp.concatenate([ownf[:, 128 * c : 128 * c + 128] for c in range(chunks)], axis=0).astype(BF16)
    upper = jnp.where(iota((128, 128), 0) < iota((128, 128), 1), 1.0, 0.0).astype(BF16)
    rows = NB * chunks
    r0, r1 = iota((rows, rows), 0), iota((rows, rows), 1)
    before = jnp.where((r1 < r0) & (((r0 - r1) & (NB - 1)) == 0), 1.0, 0.0).astype(BF16)
    base = dot(dot(before, own64).astype(BF16), jnp.ones((128, 128), BF16))
    rank64 = dot(own64, upper) + base
    rank = jnp.concatenate([rank64[NB * c : NB * c + NB] for c in range(chunks)], axis=1)
    rank = jnp.where(owned, rank, -1.0)
    slots = iota((CAP, OBS), 0).astype(F32)
    for copy in small[2:]:
        copy.wait()
    metas = []
    for k in range(NB):
        b = order[k]
        hot = jnp.where(rank[k : k + 1] == slots, 1.0, 0.0).astype(BF16)
        where = cell[pl.ds(b, 1), :]
        vh, vm, vl = split3(value[pl.ds(b, 1), :])
        rh, rm, rl = split3(variance[pl.ds(b, 1), :])
        parts = [
            reach[b].astype(F32),
            lax.shift_right_logical(where, 8).astype(F32),
            (where & 255).astype(F32),
            vh.astype(F32), vm.astype(F32), vl.astype(F32),
            rh.astype(F32), rm.astype(F32), rl.astype(F32),
            jnp.ones((1, OBS), F32),
            jnp.zeros((15, OBS), F32),
        ]
        metas.append(dot_t(jnp.concatenate(parts, axis=0).astype(BF16), hot))
    got = jnp.concatenate(metas, axis=1)
    out[M:] = jnp.concatenate(
        [
            got[16:17],
            got[10:11] + got[11:12] + got[12:13],
            got[13:14] + got[14:15] + got[15:16],
            got[:8],
            jnp.zeros((5, NB * CAP), F32),
        ],
        axis=0,
    )
    hot_y = jnp.where(got[9:10] == iota((TY, NB * CAP), 0).astype(F32), 1.0, 0.0).astype(BF16)
    hot_x = jnp.where(got[8:9] == iota((TX, NB * CAP), 0).astype(F32), 1.0, 0.0)
    load.wait()
    group = 16
    for g in range(M // group):
        high, low = split2(surface[group * g : group * g + group].reshape(group * TX, TY))
        picked = dot(high, hot_y) + dot(low, hot_y)
        out[group * g : group * g + group] = jnp.sum(
            picked.reshape(group, TX, NB * CAP) * hot_x[None], axis=1
        )


def core_of():
    return lax.rem(lax.axis_index("gx"), 2)


def edge(index, count):
    return (index == 0) | (index == count - 1)


def upward(index):
    return lax.rem(index + core_of(), 2) == 0


def emit(k, z, z_out, pay_out, edge_out, news_out=None):
    pays = []
    at = slice(CAP * k, CAP * k + CAP)
    news = []
    for t in range(2):
        pay, normed = make_payload(z[t][:M, at], z[t][M:, at])
        pay_out[t] = pay
        z_out[t, ROW_N : ROW_N + 1, at] = normed
        pays.append(pay)
        news.append(normed)
    edge_out[: ROWS // 2] = jnp.where(upward(lax.axis_index("gx") // 2), pays[1], pays[0])
    if news_out is not None:
        rows = [
            jnp.concatenate([z[t][ROW_N : ROW_N + 1, CAP * i : CAP * i + CAP] for t in range(2)], axis=1) for i in range(k)
        ]
        rows.append(jnp.concatenate(news, axis=1))
        rows.append(jnp.zeros((8 - NB, 2 * CAP), F32))
        block = jnp.concatenate(rows, axis=0)
        edge_out[ROWS // 2 :] = block
        news_out[...] = block


def start_kernel(own, sib, z_out, pay_out, edge_out):
    first = core_of() == 0
    mine, other = own[...], sib[...]
    z = [jnp.where(first, mine, other), jnp.where(first, other, mine)]
    unit = jnp.where(iota((ROWS, 128), 0) == iota((ROWS, 128), 1), 1.0, 0.0)
    unit = jnp.where(iota((ROWS, 128), 0) < M, unit, 0.0)
    for t in range(2):
        z_out[t, :, : NB * CAP] = z[t]
        z_out[t, :, NB * CAP :] = unit
    emit(0, z, z_out, pay_out, edge_out)


def right_side(rows):
    return rows[ROW_A : ROW_A + 1] + rows[ROW_C : ROW_C + 1] * rows[:M]


def factor(rows, dx, dy):
    at = ROW_W + 3 * (dx + 1) + dy + 1
    return rows[at : at + 1]


def toward(rows, dx):
    return jnp.where(upward(lax.axis_index("gy")), factor(rows, dx, 1), factor(rows, dx, -1))


def level(rows, dx):
    return factor(rows, dx, 0)


def inner(pay, weight):
    blocks = [unpack(pay[t]) for t in range(2)]
    right = jnp.concatenate([right_side(b) for b in blocks], axis=1)
    return [
        dot3(right, jnp.concatenate([b[:M] * weight(b, t - i) for i, b in enumerate(blocks)], axis=1), dot_t)
        for t in range(2)
    ]


def outer(far, sib_far, weight):
    y, chips = lax.axis_index("gx") // 2, lax.axis_size("gx") // 2
    up = upward(y)
    first = core_of() == 0
    ends = edge(y, chips)
    far = jnp.where(ends & jnp.logical_not(first), 0.0, far[: ROWS // 2])
    sib_far = jnp.where(ends & first, 0.0, sib_far[: ROWS // 2])
    blocks = [unpack(jnp.where(up, sib_far, far)), unpack(jnp.where(up, far, sib_far))]
    return [dot3(right_side(b), b[:M] * weight(b, dx), dot_t) for b, dx in zip(blocks, (1, -1))]


def own_kernel(k, order, owner, pay, toward_out, level_out, rank_out):
    for t, value in enumerate(inner(pay, toward)):
        toward_out[t] = value
    for t, value in enumerate(inner(pay, level)):
        level_out[t] = value
    row = owner[pl.ds(order[k], 1), :]
    upper = jnp.where(iota((128, 128), 0) < iota((128, 128), 1), 1.0, 0.0).astype(BF16)
    tiles = iota((TILES, 128), 0)
    base = jnp.zeros((TILES, 1), F32)
    for c in range(OBS // 128):
        at = slice(128 * c, 128 * c + 128)
        hot = jnp.where(row[:, at] == tiles, 1.0, 0.0)
        rank = dot(hot.astype(BF16), upper) + base
        rank_out[:, at] = jnp.sum(hot * rank, axis=0, keepdims=True)
        base = base + jnp.sum(hot, axis=1, keepdims=True)


def send_kernel(own, far, sib_far, out):
    for t, value in enumerate(outer(far, sib_far, toward)):
        out[t] = own[t] + value


def same_kernel(own, far, sib_far, out):
    for t, value in enumerate(outer(far, sib_far, level)):
        out[t] = own[t] + value


def column_kernel(news, far, sib_far, across, out):
    first = core_of() == 0
    at = slice(ROWS // 2, ROWS // 2 + NB)
    mine, other = far[at], sib_far[at]
    column = jnp.concatenate(
        [news[:NB], jnp.where(first, mine, other), across[:NB], jnp.where(first, other, mine)], axis=0
    )
    out[...] = jnp.broadcast_to(column[None], out.shape)


def advance(z, gain):
    anomaly = z - jnp.sum(z, axis=0, keepdims=True) / M
    return z + dot3(gain, anomaly)


def whole_gain(t, q0, h, g):
    first = core_of() == 0
    ends = edge(lax.axis_index("gy"), lax.axis_size("gy"))
    return q0[t] + jnp.where(ends & jnp.logical_not(first), 0.0, h[t]) + jnp.where(ends & first, 0.0, g[t])


def step_kernel(k, q0, h, g, z, z_out, pay_out, edge_out, news_out=None):
    new = []
    for t in range(2):
        moved = advance(z[t, :M], whole_gain(t, q0, h, g))
        z_out[t, :M] = moved
        z_out[t, M:] = z[t, M:]
        new.append(jnp.concatenate([moved, z[t, M:]], axis=0))
    emit(k, new, z_out, pay_out, edge_out, news_out)


def part(ref, i):
    return ref.at[:, i // PARTS, pl.ds((i % PARTS) * SLAB, SLAB), :]


def turn(block, out, at):
    high, low = split2(jnp.swapaxes(block, 0, 1))
    out[at : at + 8, :M] = high
    out[at : at + 8, M:] = low


def turn_kernel(first, x, out, come, sems):
    loads = [pltpu.make_async_copy(part(x, first + i), come.at[i], sems.at[i]) for i in range(TURN)]
    for load in loads:
        load.start()
    for i in range(TURN):
        loads[i].wait()
        for j in range(0, SLAB, 8):
            turn(come[i, :, j : j + 8, :], out, SLAB * i + j)


def final_kernel(q0, h, g, z, near, x, out, come, go, come_sems, go_sems):
    loads = [pltpu.make_async_copy(part(x, i), come.at[i - TURN], come_sems.at[i - TURN]) for i in range(TURN, SLABS)]
    stores = [pltpu.make_async_copy(go.at[i], part(out, i), go_sems.at[i]) for i in range(SLABS)]
    for load in loads:
        load.start()
    c = core_of()
    t = advance(z[c, :M, NB * CAP :], whole_gain(c, q0, h, g))[:, :M]
    th, tl = split2(t)
    w = jnp.concatenate([th, th, tl], axis=1)
    for i in range(SLABS):
        if i >= TURN:
            loads[i - TURN].wait()
        for j in range(0, SLAB, 8):
            if i >= TURN:
                turned = jnp.swapaxes(come[i - TURN, :, j : j + 8, :], 0, 1)
            rows = []
            for r in range(8):
                if i >= TURN:
                    xh, xl = split2(turned[r])
                    stack = [xh, xl, xh]
                else:
                    both = near[SLAB * i + j + r]
                    stack = [both, both[:M]]
                rows.append(dot(w, jnp.concatenate(stack, axis=0))[None])
            go[i, :, j : j + 8, :] = jnp.swapaxes(jnp.concatenate(rows, axis=0), 0, 1)
        stores[i].start()
    for store in stores:
        store.wait()


def place_kernel(order, owner, gathered, r0, r1, r2, r3, out):
    y = lax.axis_index("gx") // 2
    tiles = iota((TILES, OBS), 0)
    slots = iota((CAP, OBS), 0).astype(F32)
    rows = gathered.reshape(TILES // 2 * NB, 2 * CAP)
    for k, rank in enumerate((r0, r1, r2, r3)):
        b = order[k]
        tile = owner[pl.ds(b, 1), :]
        place = ((tile >> 4) & 1) * (TILES // 2) + (tile & 15) * 4 + ((tile >> 5) ^ y)
        turned = rows[pl.ds(k, TILES // 2, stride=NB), :].T
        table = jnp.concatenate([turned[:CAP], turned[CAP:]], axis=1)
        if k < NB // 2:
            chunks = [slice(at, at + 128) for at in range(0, OBS, 128)]
            got = jnp.concatenate([
                jnp.take_along_axis(table, jnp.broadcast_to(place[:, at], (CAP, 128)), axis=1) for at in chunks
            ], axis=1)
        else:
            hot = jnp.where(place == tiles, 1.0, 0.0).astype(BF16)
            both = dot(jnp.concatenate(split2(table), axis=0), hot)
            got = both[:CAP] + both[CAP:]
        out[pl.ds(b, 1), :] = jnp.sum(jnp.where(rank[...] == slots, got, 0.0), axis=0, keepdims=True)


VMEM = pl.BlockSpec(memory_space=pltpu.VMEM)
SMEM = pl.BlockSpec(memory_space=pltpu.SMEM)
HBM = pl.BlockSpec(memory_space=pltpu.HBM)


def shape(*dims):
    return jax.ShapeDtypeStruct(dims, F32)


def swaps(pairs):
    return pairs + [(high, low) for low, high in pairs]


def local(ensemble, obs_value, obs_variance, obs_owner, obs_cell, obs_reach, batch_order):
    params = pltpu.CompilerParams(vmem_limit_bytes=32 * 2**20)
    call = functools.partial(pl.pallas_call, compiler_params=params)
    width, height = lax.axis_size("gx"), lax.axis_size("gy")
    both = ("gx", "gy")
    core = swaps([(x, x + 1) for x in range(0, width, 2)])
    chips = width // 2
    side_x = swaps([(2 * y + c, 2 * ((y + 1) % chips) + c) for c in range(2) for y in range(c, chips, 2)])
    side_y = swaps([
        (x * height + k, x * height + k + 1) for x in range(width) for k in range(x % 2, height - 1, 2)
    ] + [(x * height + k, (x + 2) * height + k) for x in range(1, width, 4) for k in (0, height - 1)])
    pay_shapes = (shape(2, ROWS // 2, 128), shape(ROWS // 2, 128))
    z_shape = shape(2, ROWS, NB * CAP + 128)
    row = pltpu.VMEM((NB, OBS), F32)
    row_i = pltpu.VMEM((NB, OBS), jnp.int32)
    own = call(
        init_kernel,
        out_shape=shape(ROWS, NB * CAP),
        in_specs=[HBM] * 7,
        out_specs=VMEM,
        scratch_shapes=[
            pltpu.SMEM((NB,), jnp.int32), row, row, row_i, row_i,
            pltpu.VMEM((NB, 8, OBS), jnp.int32), pltpu.VMEM((M, TX, TY), F32), pltpu.SemaphoreType.DMA((7,)),
        ],
        name="init",
    )(*(
        pltpu.with_memory_space_constraint(value, pltpu.HBM)
        for value in (
            batch_order, obs_value, obs_variance, obs_owner, obs_cell, jnp.swapaxes(obs_reach, 1, 2), ensemble
        )
    ))
    z, pay, edge = call(
        start_kernel,
        out_shape=(z_shape,) + pay_shapes,
        in_specs=[VMEM] * 2,
        out_specs=(VMEM,) * 3,
        name="start",
    )(own, lax.ppermute(own, "gx", core))
    ranks = []
    state_hbm = pltpu.with_memory_space_constraint(ensemble, pltpu.HBM)
    for k in range(NB):
        last = k + 1 == NB
        far = lax.ppermute(edge, "gx", side_x)
        own_toward, own_level, rank = call(
            functools.partial(own_kernel, k),
            out_shape=(shape(2, M, M), shape(2, M, M), shape(1, OBS)),
            in_specs=[SMEM, VMEM, VMEM],
            out_specs=(VMEM,) * 3,
            name="own",
        )(batch_order, obs_owner, pay)
        far, own_toward = lax.optimization_barrier((far, own_toward))
        sib_far = lax.ppermute(far, "gx", core)
        send = call(send_kernel, out_shape=shape(2, M, M), in_specs=[VMEM] * 3, out_specs=VMEM, name="send")(
            own_toward, far, sib_far
        )
        send, sib_far = lax.optimization_barrier((send, sib_far))
        h = lax.ppermute(send, both, side_y)
        q0 = call(same_kernel, out_shape=shape(2, M, M), in_specs=[VMEM] * 3, out_specs=VMEM, name="same")(
            own_level, far, sib_far
        )
        ranks.append(rank)
        if last:
            across = lax.ppermute(sib_far[ROWS // 2 :], "gx", side_x)
            column = call(
                column_kernel, out_shape=shape(height, 4 * NB, 128), in_specs=[VMEM] * 4, out_specs=VMEM, name="column"
            )(news, far, sib_far, across)
        if last:
            h, q0, column = lax.optimization_barrier((h, q0, column))
            gathered = lax.all_to_all(column, "gy", 0, 0, tiled=True)
        else:
            turned_shape = jax.ShapeDtypeStruct((TURN * SLAB, 2 * M, TY), BF16)
            come = pltpu.VMEM((TURN, M, SLAB, TY), F32)
            if k + 2 < NB:
                h, q0 = lax.optimization_barrier((h, q0))
            else:
                near = call(
                    functools.partial(turn_kernel, 0),
                    out_shape=turned_shape,
                    in_specs=[HBM],
                    out_specs=VMEM,
                    scratch_shapes=[come, pltpu.SemaphoreType.DMA((TURN,))],
                    name="turn",
                )(state_hbm)
                h, q0, near = lax.optimization_barrier((h, q0, near))
        g = lax.ppermute(h, "gx", core)
        if not last:
            tail = k + 2 == NB
            edge_shape = (shape(ROWS // 2 + 8, 128), shape(8, 128)) if tail else pay_shapes[1:]
            z, pay, edge, *rest = call(
                functools.partial(step_kernel, k + 1),
                out_shape=(z_shape, pay_shapes[0]) + edge_shape,
                in_specs=[VMEM] * 4,
                out_specs=(VMEM,) * (4 if tail else 3),
                name="step",
            )(q0, h, g, z)
            if tail:
                news = rest[0]
    dma = lambda n: pltpu.SemaphoreType.DMA((n,))
    state = call(
        final_kernel,
        out_shape=shape(M, LEV, TX, TY),
        in_specs=[VMEM] * 5 + [HBM],
        out_specs=HBM,
        scratch_shapes=[
            pltpu.VMEM((SLABS - TURN, M, SLAB, TY), F32), pltpu.VMEM((SLABS, M, SLAB, TY), F32),
            dma(SLABS - TURN), dma(SLABS),
        ],
        cost_estimate=pl.CostEstimate(flops=6 * M * M * LEV * TX * TY, bytes_accessed=8 * M * LEV * TX * TY, transcendentals=0),
        name="final",
    )(q0, h, g, z, near, state_hbm)
    state, gathered = lax.optimization_barrier((state, gathered))
    innovation = call(
        place_kernel,
        out_shape=shape(NB, OBS),
        in_specs=[SMEM] + [VMEM] * 6,
        out_specs=VMEM,
        name="place",
    )(batch_order, obs_owner, gathered, *ranks)
    return state, innovation


def solution(mesh):
    placed = (P(None, None, "gx", "gy"), P(), P(), P(), P(), P(), P())
    return jax.shard_map(
        local,
        mesh=mesh,
        in_specs=placed,
        out_specs=(P(None, None, "gx", "gy"), P()),
        check_vma=False,
    )
```

```python
import functools

import jax
import jax.numpy as jnp
from jax import lax
from jax.experimental import pallas as pl
from jax.experimental.pallas import tpu as pltpu
from jax.sharding import PartitionSpec as P

M = 80
LEV = 4
NB = 4
TX = 32
TY = 256
CAP = 64
OBS = 2048
TILES = 128
EPS = 1e-05
F32 = jnp.float32
BF16 = jnp.bfloat16
SLAB = 16
PARTS = TX // SLAB
SLABS = LEV * PARTS
TURN = 2

ROW_A = M
ROW_C = M + 1
ROW_W = M + 2
ROW_N = M + 11
ROWS = 96
TAPER = (0.25, 0.5, 0.25, 0.5, 1.0, 0.5, 0.25, 0.5, 0.25)


def split2(x):
    high = x.astype(BF16)
    return high, (x - high.astype(F32)).astype(BF16)


def split3(x):
    high = x.astype(BF16)
    rest = x - high.astype(F32)
    mid = rest.astype(BF16)
    return high, mid, (rest - mid.astype(F32)).astype(BF16)


def iota(shape, dim):
    return lax.broadcasted_iota(jnp.int32, shape, dim)


def dot(a, b, **kw):
    return jnp.dot(a, b, preferred_element_type=F32, **kw)


def dot_t(a, b, **kw):
    return lax.dot_general(a, b, (((1,), (1,)), ((), ())), preferred_element_type=F32, **kw)


def dot3(a, b, product=dot):
    ah, al = split2(a)
    bh, bl = split2(b)
    return product(ah, bh) + (product(ah, bl) + product(al, bh))


def pack(rows):
    return jnp.concatenate([rows[: ROWS // 2], rows[ROWS // 2 :]], axis=1)


def unpack(packed):
    return jnp.concatenate([packed[:, :CAP], packed[:, CAP:]], axis=0)


def make_payload(prior, meta):
    valid = meta[0:1] > 0.5
    value = meta[1:2]
    variance = jnp.where(valid, meta[2:3], 1.0)
    center = jnp.sum(prior, axis=0, keepdims=True) / M
    deviation = prior - center
    spread = jnp.sum(deviation * deviation, axis=0, keepdims=True) / (M - 1)
    total = spread + variance
    miss = value - center
    normed = jnp.where(valid, miss / jnp.sqrt(total), 0.0)
    a = spread / total * miss
    c = jnp.sqrt(variance / total) - 1.0
    d = jnp.where(valid, 1.0 / ((M - 1) * (spread + EPS)), 0.0)
    rows = [deviation, a, c]
    for i in range(9):
        if i == 4:
            rows.append(d)
        else:
            at = 3 + (i if i < 4 else i - 1)
            rows.append(d * (meta[at : at + 1] * TAPER[i]))
    rows.append(jnp.zeros((ROWS - M - 11, CAP), F32))
    return pack(jnp.concatenate(rows, axis=0)), normed


def init_kernel(order_hbm, value_hbm, variance_hbm, owner_hbm, cell_hbm, reach_hbm, x_hbm, out,
                order, value, variance, owner, cell, reach, surface, sems):
    small = [
        pltpu.make_async_copy(source, target, sems.at[i])
        for i, (source, target) in enumerate([
            (order_hbm, order), (owner_hbm, owner), (cell_hbm, cell),
            (value_hbm, value), (variance_hbm, variance), (reach_hbm, reach),
        ])
    ]
    load = pltpu.make_async_copy(x_hbm.at[:, 0], surface, sems.at[6])
    for copy in small:
        copy.start()
    load.start()
    me = lax.axis_index("gx") * lax.axis_size("gy") + lax.axis_index("gy")
    small[0].wait()
    small[1].wait()
    owned = jnp.concatenate([owner[pl.ds(order[k], 1), :] for k in range(NB)], axis=0) == me
    ownf = jnp.where(owned, 1.0, 0.0)
    chunks = OBS // 128
    own64 = jnp.concatenate([ownf[:, 128 * c : 128 * c + 128] for c in range(chunks)], axis=0).astype(BF16)
    upper = jnp.where(iota((128, 128), 0) < iota((128, 128), 1), 1.0, 0.0).astype(BF16)
    rows = NB * chunks
    r0, r1 = iota((rows, rows), 0), iota((rows, rows), 1)
    before = jnp.where((r1 < r0) & (((r0 - r1) & (NB - 1)) == 0), 1.0, 0.0).astype(BF16)
    base = dot(dot(before, own64).astype(BF16), jnp.ones((128, 128), BF16))
    rank64 = dot(own64, upper) + base
    rank = jnp.concatenate([rank64[NB * c : NB * c + NB] for c in range(chunks)], axis=1)
    rank = jnp.where(owned, rank, -1.0)
    slots = iota((CAP, OBS), 0).astype(F32)
    for copy in small[2:]:
        copy.wait()
    metas = []
    for k in range(NB):
        b = order[k]
        hot = jnp.where(rank[k : k + 1] == slots, 1.0, 0.0).astype(BF16)
        where = cell[pl.ds(b, 1), :]
        vh, vm, vl = split3(value[pl.ds(b, 1), :])
        rh, rm, rl = split3(variance[pl.ds(b, 1), :])
        parts = [
            reach[b].astype(F32),
            lax.shift_right_logical(where, 8).astype(F32),
            (where & 255).astype(F32),
            vh.astype(F32), vm.astype(F32), vl.astype(F32),
            rh.astype(F32), rm.astype(F32), rl.astype(F32),
            jnp.ones((1, OBS), F32),
            jnp.zeros((15, OBS), F32),
        ]
        metas.append(dot_t(jnp.concatenate(parts, axis=0).astype(BF16), hot))
    got = jnp.concatenate(metas, axis=1)
    out[M:] = jnp.concatenate(
        [
            got[16:17],
            got[10:11] + got[11:12] + got[12:13],
            got[13:14] + got[14:15] + got[15:16],
            got[:8],
            jnp.zeros((5, NB * CAP), F32),
        ],
        axis=0,
    )
    hot_y = jnp.where(got[9:10] == iota((TY, NB * CAP), 0).astype(F32), 1.0, 0.0).astype(BF16)
    hot_x = jnp.where(got[8:9] == iota((TX, NB * CAP), 0).astype(F32), 1.0, 0.0)
    load.wait()
    group = 16
    for g in range(M // group):
        high, low = split2(surface[group * g : group * g + group].reshape(group * TX, TY))
        picked = dot(high, hot_y) + dot(low, hot_y)
        out[group * g : group * g + group] = jnp.sum(
            picked.reshape(group, TX, NB * CAP) * hot_x[None], axis=1
        )


def core_of():
    return lax.rem(lax.axis_index("gx"), 2)


def edge(index, count):
    return (index == 0) | (index == count - 1)


def upward(index):
    return lax.rem(index + core_of(), 2) == 0


def emit(k, z, z_out, pay_out, edge_out, news_out=None):
    pays = []
    at = slice(CAP * k, CAP * k + CAP)
    news = []
    for t in range(2):
        pay, normed = make_payload(z[t][:M, at], z[t][M:, at])
        pay_out[t] = pay
        z_out[t, ROW_N : ROW_N + 1, at] = normed
        pays.append(pay)
        news.append(normed)
    edge_out[: ROWS // 2] = jnp.where(upward(lax.axis_index("gx") // 2), pays[1], pays[0])
    if news_out is not None:
        rows = [
            jnp.concatenate([z[t][ROW_N : ROW_N + 1, CAP * i : CAP * i + CAP] for t in range(2)], axis=1) for i in range(k)
        ]
        rows.append(jnp.concatenate(news, axis=1))
        rows.append(jnp.zeros((8 - NB, 2 * CAP), F32))
        block = jnp.concatenate(rows, axis=0)
        edge_out[ROWS // 2 :] = block
        news_out[...] = block


def start_kernel(own, sib, z_out, pay_out, edge_out):
    first = core_of() == 0
    mine, other = own[...], sib[...]
    z = [jnp.where(first, mine, other), jnp.where(first, other, mine)]
    unit = jnp.where(iota((ROWS, 128), 0) == iota((ROWS, 128), 1), 1.0, 0.0)
    unit = jnp.where(iota((ROWS, 128), 0) < M, unit, 0.0)
    for t in range(2):
        z_out[t, :, : NB * CAP] = z[t]
        z_out[t, :, NB * CAP :] = unit
    emit(0, z, z_out, pay_out, edge_out)


def right_side(rows):
    return rows[ROW_A : ROW_A + 1] + rows[ROW_C : ROW_C + 1] * rows[:M]


def factor(rows, dx, dy):
    at = ROW_W + 3 * (dx + 1) + dy + 1
    return rows[at : at + 1]


def toward(rows, dx):
    return jnp.where(upward(lax.axis_index("gy")), factor(rows, dx, 1), factor(rows, dx, -1))


def level(rows, dx):
    return factor(rows, dx, 0)


def inner(pay, weight):
    blocks = [unpack(pay[t]) for t in range(2)]
    right = jnp.concatenate([right_side(b) for b in blocks], axis=1)
    return [
        dot3(right, jnp.concatenate([b[:M] * weight(b, t - i) for i, b in enumerate(blocks)], axis=1), dot_t)
        for t in range(2)
    ]


def outer(far, sib_far, weight):
    y, chips = lax.axis_index("gx") // 2, lax.axis_size("gx") // 2
    up = upward(y)
    first = core_of() == 0
    ends = edge(y, chips)
    far = jnp.where(ends & jnp.logical_not(first), 0.0, far[: ROWS // 2])
    sib_far = jnp.where(ends & first, 0.0, sib_far[: ROWS // 2])
    blocks = [unpack(jnp.where(up, sib_far, far)), unpack(jnp.where(up, far, sib_far))]
    return [dot3(right_side(b), b[:M] * weight(b, dx), dot_t) for b, dx in zip(blocks, (1, -1))]


def own_kernel(k, order, owner, pay, toward_out, level_out, rank_out):
    for t, value in enumerate(inner(pay, toward)):
        toward_out[t] = value
    for t, value in enumerate(inner(pay, level)):
        level_out[t] = value
    row = owner[pl.ds(order[k], 1), :]
    upper = jnp.where(iota((128, 128), 0) < iota((128, 128), 1), 1.0, 0.0).astype(BF16)
    tiles = iota((TILES, 128), 0)
    base = jnp.zeros((TILES, 1), F32)
    for c in range(OBS // 128):
        at = slice(128 * c, 128 * c + 128)
        hot = jnp.where(row[:, at] == tiles, 1.0, 0.0)
        rank = dot(hot.astype(BF16), upper) + base
        rank_out[:, at] = jnp.sum(hot * rank, axis=0, keepdims=True)
        base = base + jnp.sum(hot, axis=1, keepdims=True)


def send_kernel(own, far, sib_far, out):
    for t, value in enumerate(outer(far, sib_far, toward)):
        out[t] = own[t] + value


def same_kernel(own, far, sib_far, out):
    for t, value in enumerate(outer(far, sib_far, level)):
        out[t] = own[t] + value


def column_kernel(news, far, sib_far, across, out):
    first = core_of() == 0
    at = slice(ROWS // 2, ROWS // 2 + NB)
    mine, other = far[at], sib_far[at]
    column = jnp.concatenate(
        [news[:NB], jnp.where(first, mine, other), across[:NB], jnp.where(first, other, mine)], axis=0
    )
    out[...] = jnp.broadcast_to(column[None], out.shape)


def advance(z, gain):
    anomaly = z - jnp.sum(z, axis=0, keepdims=True) / M
    return z + dot3(gain, anomaly)


def whole_gain(t, q0, h, g):
    first = core_of() == 0
    ends = edge(lax.axis_index("gy"), lax.axis_size("gy"))
    return q0[t] + jnp.where(ends & jnp.logical_not(first), 0.0, h[t]) + jnp.where(ends & first, 0.0, g[t])


def step_kernel(k, q0, h, g, z, z_out, pay_out, edge_out, news_out=None):
    new = []
    for t in range(2):
        moved = advance(z[t, :M], whole_gain(t, q0, h, g))
        z_out[t, :M] = moved
        z_out[t, M:] = z[t, M:]
        new.append(jnp.concatenate([moved, z[t, M:]], axis=0))
    emit(k, new, z_out, pay_out, edge_out, news_out)


def part(ref, i, at=0, rows=SLAB):
    return ref.at[:, i // PARTS, pl.ds((i % PARTS) * SLAB + at, rows), :]


def turn(block, out, at):
    high, low = split2(jnp.swapaxes(block, 0, 1))
    out[at : at + 8, :M] = high
    out[at : at + 8, M:] = low


def turn_kernel(first, x, out, come, sems):
    loads = [pltpu.make_async_copy(part(x, first + i), come.at[i], sems.at[i]) for i in range(TURN)]
    for load in loads:
        load.start()
    for i in range(TURN):
        loads[i].wait()
        for j in range(0, SLAB, 8):
            turn(come[i, :, j : j + 8, :], out, SLAB * i + j)


def final_kernel(q0, h, g, z, near, x, out, come, go, come_sems, go_sems):
    loads = [pltpu.make_async_copy(part(x, i), come.at[i - TURN], come_sems.at[i - TURN]) for i in range(TURN, SLABS)]
    stores = []
    for load in loads:
        load.start()
    c = core_of()
    t = advance(z[c, :M, NB * CAP :], whole_gain(c, q0, h, g))[:, :M]
    th, tl = split2(t)
    w = jnp.concatenate([th, th, tl], axis=1)
    for i in range(SLABS):
        if i >= TURN:
            loads[i - TURN].wait()
        for j in range(0, SLAB, 8):
            if i >= TURN:
                turned = jnp.swapaxes(come[i - TURN, :, j : j + 8, :], 0, 1)
            rows = []
            for r in range(8):
                if i >= TURN:
                    xh, xl = split2(turned[r])
                    stack = [xh, xl, xh]
                else:
                    both = near[SLAB * i + j + r]
                    stack = [both, both[:M]]
                rows.append(dot(w, jnp.concatenate(stack, axis=0))[None])
            go[i, :, j : j + 8, :] = jnp.swapaxes(jnp.concatenate(rows, axis=0), 0, 1)
            sem = go_sems.at[(SLAB * i + j) // 8]
            stores.append(pltpu.make_async_copy(go.at[i, :, pl.ds(j, 8), :], part(out, i, j, 8), sem))
            stores[-1].start()
    for store in stores:
        store.wait()


def place_kernel(order, owner, gathered, r0, r1, r2, r3, out):
    y = lax.axis_index("gx") // 2
    tiles = iota((TILES, OBS), 0)
    slots = iota((CAP, OBS), 0).astype(F32)
    rows = gathered.reshape(TILES // 2 * NB, 2 * CAP)
    for k, rank in enumerate((r0, r1, r2, r3)):
        b = order[k]
        tile = owner[pl.ds(b, 1), :]
        place = ((tile >> 4) & 1) * (TILES // 2) + (tile & 15) * 4 + ((tile >> 5) ^ y)
        turned = rows[pl.ds(k, TILES // 2, stride=NB), :].T
        table = jnp.concatenate([turned[:CAP], turned[CAP:]], axis=1)
        if k < NB // 2:
            chunks = [slice(at, at + 128) for at in range(0, OBS, 128)]
            got = jnp.concatenate([
                jnp.take_along_axis(table, jnp.broadcast_to(place[:, at], (CAP, 128)), axis=1) for at in chunks
            ], axis=1)
        else:
            hot = jnp.where(place == tiles, 1.0, 0.0).astype(BF16)
            both = dot(jnp.concatenate(split2(table), axis=0), hot)
            got = both[:CAP] + both[CAP:]
        out[pl.ds(b, 1), :] = jnp.sum(jnp.where(rank[...] == slots, got, 0.0), axis=0, keepdims=True)


VMEM = pl.BlockSpec(memory_space=pltpu.VMEM)
SMEM = pl.BlockSpec(memory_space=pltpu.SMEM)
HBM = pl.BlockSpec(memory_space=pltpu.HBM)


def shape(*dims):
    return jax.ShapeDtypeStruct(dims, F32)


def swaps(pairs):
    return pairs + [(high, low) for low, high in pairs]


def local(ensemble, obs_value, obs_variance, obs_owner, obs_cell, obs_reach, batch_order):
    params = pltpu.CompilerParams(vmem_limit_bytes=32 * 2**20)
    call = functools.partial(pl.pallas_call, compiler_params=params)
    width, height = lax.axis_size("gx"), lax.axis_size("gy")
    both = ("gx", "gy")
    core = swaps([(x, x + 1) for x in range(0, width, 2)])
    chips = width // 2
    side_x = swaps([(2 * y + c, 2 * ((y + 1) % chips) + c) for c in range(2) for y in range(c, chips, 2)])
    side_y = swaps([
        (x * height + k, x * height + k + 1) for x in range(width) for k in range(x % 2, height - 1, 2)
    ] + [(x * height + k, (x + 2) * height + k) for x in range(1, width, 4) for k in (0, height - 1)])
    pay_shapes = (shape(2, ROWS // 2, 128), shape(ROWS // 2, 128))
    z_shape = shape(2, ROWS, NB * CAP + 128)
    row = pltpu.VMEM((NB, OBS), F32)
    row_i = pltpu.VMEM((NB, OBS), jnp.int32)
    own = call(
        init_kernel,
        out_shape=shape(ROWS, NB * CAP),
        in_specs=[HBM] * 7,
        out_specs=VMEM,
        scratch_shapes=[
            pltpu.SMEM((NB,), jnp.int32), row, row, row_i, row_i,
            pltpu.VMEM((NB, 8, OBS), jnp.int32), pltpu.VMEM((M, TX, TY), F32), pltpu.SemaphoreType.DMA((7,)),
        ],
        name="init",
    )(*(
        pltpu.with_memory_space_constraint(value, pltpu.HBM)
        for value in (
            batch_order, obs_value, obs_variance, obs_owner, obs_cell, jnp.swapaxes(obs_reach, 1, 2), ensemble
        )
    ))
    z, pay, edge = call(
        start_kernel,
        out_shape=(z_shape,) + pay_shapes,
        in_specs=[VMEM] * 2,
        out_specs=(VMEM,) * 3,
        name="start",
    )(own, lax.ppermute(own, "gx", core))
    ranks = []
    state_hbm = pltpu.with_memory_space_constraint(ensemble, pltpu.HBM)
    for k in range(NB):
        last = k + 1 == NB
        far = lax.ppermute(edge, "gx", side_x)
        own_toward, own_level, rank = call(
            functools.partial(own_kernel, k),
            out_shape=(shape(2, M, M), shape(2, M, M), shape(1, OBS)),
            in_specs=[SMEM, VMEM, VMEM],
            out_specs=(VMEM,) * 3,
            name="own",
        )(batch_order, obs_owner, pay)
        far, own_toward = lax.optimization_barrier((far, own_toward))
        sib_far = lax.ppermute(far, "gx", core)
        send = call(send_kernel, out_shape=shape(2, M, M), in_specs=[VMEM] * 3, out_specs=VMEM, name="send")(
            own_toward, far, sib_far
        )
        send, sib_far = lax.optimization_barrier((send, sib_far))
        h = lax.ppermute(send, both, side_y)
        q0 = call(same_kernel, out_shape=shape(2, M, M), in_specs=[VMEM] * 3, out_specs=VMEM, name="same")(
            own_level, far, sib_far
        )
        ranks.append(rank)
        if last:
            across = lax.ppermute(sib_far[ROWS // 2 :], "gx", side_x)
            column = call(
                column_kernel, out_shape=shape(height, 4 * NB, 128), in_specs=[VMEM] * 4, out_specs=VMEM, name="column"
            )(news, far, sib_far, across)
        if last:
            h, q0, column = lax.optimization_barrier((h, q0, column))
            gathered = lax.all_to_all(column, "gy", 0, 0, tiled=True)
        else:
            turned_shape = jax.ShapeDtypeStruct((TURN * SLAB, 2 * M, TY), BF16)
            come = pltpu.VMEM((TURN, M, SLAB, TY), F32)
            if k + 2 < NB:
                h, q0 = lax.optimization_barrier((h, q0))
            else:
                near = call(
                    functools.partial(turn_kernel, 0),
                    out_shape=turned_shape,
                    in_specs=[HBM],
                    out_specs=VMEM,
                    scratch_shapes=[come, pltpu.SemaphoreType.DMA((TURN,))],
                    name="turn",
                )(state_hbm)
                h, q0, near = lax.optimization_barrier((h, q0, near))
        g = lax.ppermute(h, "gx", core)
        if not last:
            tail = k + 2 == NB
            edge_shape = (shape(ROWS // 2 + 8, 128), shape(8, 128)) if tail else pay_shapes[1:]
            z, pay, edge, *rest = call(
                functools.partial(step_kernel, k + 1),
                out_shape=(z_shape, pay_shapes[0]) + edge_shape,
                in_specs=[VMEM] * 4,
                out_specs=(VMEM,) * (4 if tail else 3),
                name="step",
            )(q0, h, g, z)
            if tail:
                news = rest[0]
    dma = lambda n: pltpu.SemaphoreType.DMA((n,))
    state = call(
        final_kernel,
        out_shape=shape(M, LEV, TX, TY),
        in_specs=[VMEM] * 5 + [HBM],
        out_specs=HBM,
        scratch_shapes=[
            pltpu.VMEM((SLABS - TURN, M, SLAB, TY), F32), pltpu.VMEM((SLABS, M, SLAB, TY), F32),
            dma(SLABS - TURN), dma(SLABS * SLAB // 8),
        ],
        cost_estimate=pl.CostEstimate(flops=6 * M * M * LEV * TX * TY, bytes_accessed=8 * M * LEV * TX * TY, transcendentals=0),
        name="final",
    )(q0, h, g, z, near, state_hbm)
    state, gathered = lax.optimization_barrier((state, gathered))
    innovation = call(
        place_kernel,
        out_shape=shape(NB, OBS),
        in_specs=[SMEM] + [VMEM] * 6,
        out_specs=VMEM,
        name="place",
    )(batch_order, obs_owner, gathered, *ranks)
    return state, innovation


def solution(mesh):
    placed = (P(None, None, "gx", "gy"), P(), P(), P(), P(), P(), P())
    return jax.shard_map(
        local,
        mesh=mesh,
        in_specs=placed,
        out_specs=(P(None, None, "gx", "gy"), P()),
        check_vma=False,
    )
```

```python
import functools

import jax
import jax.numpy as jnp
from jax import lax
from jax.experimental import pallas as pl
from jax.experimental.pallas import tpu as pltpu
from jax.sharding import PartitionSpec as P

M = 80
LEV = 4
NB = 4
TX = 32
TY = 256
CAP = 64
OBS = 2048
TILES = 128
EPS = 1e-05
F32 = jnp.float32
BF16 = jnp.bfloat16
SLAB = 16
PARTS = TX // SLAB
SLABS = LEV * PARTS
TURN = 2

ROW_A = M
ROW_C = M + 1
ROW_W = M + 2
ROW_N = M + 11
ROWS = 96
TAPER = (0.25, 0.5, 0.25, 0.5, 1.0, 0.5, 0.25, 0.5, 0.25)


def split2(x):
    high = x.astype(BF16)
    return high, (x - high.astype(F32)).astype(BF16)


def split3(x):
    high = x.astype(BF16)
    rest = x - high.astype(F32)
    mid = rest.astype(BF16)
    return high, mid, (rest - mid.astype(F32)).astype(BF16)


def iota(shape, dim):
    return lax.broadcasted_iota(jnp.int32, shape, dim)


def dot(a, b, **kw):
    return jnp.dot(a, b, preferred_element_type=F32, **kw)


def dot_t(a, b, **kw):
    return lax.dot_general(a, b, (((1,), (1,)), ((), ())), preferred_element_type=F32, **kw)


def dot3(a, b, product=dot):
    ah, al = split2(a)
    bh, bl = split2(b)
    return product(ah, bh) + (product(ah, bl) + product(al, bh))


def pack(rows):
    return jnp.concatenate([rows[: ROWS // 2], rows[ROWS // 2 :]], axis=1)


def unpack(packed):
    return jnp.concatenate([packed[:, :CAP], packed[:, CAP:]], axis=0)


def make_payload(prior, meta):
    valid = meta[0:1] > 0.5
    value = meta[1:2]
    variance = jnp.where(valid, meta[2:3], 1.0)
    center = jnp.sum(prior, axis=0, keepdims=True) / M
    deviation = prior - center
    spread = jnp.sum(deviation * deviation, axis=0, keepdims=True) / (M - 1)
    total = spread + variance
    miss = value - center
    normed = jnp.where(valid, miss / jnp.sqrt(total), 0.0)
    a = spread / total * miss
    c = jnp.sqrt(variance / total) - 1.0
    d = jnp.where(valid, 1.0 / ((M - 1) * (spread + EPS)), 0.0)
    rows = [deviation, a, c]
    for i in range(9):
        if i == 4:
            rows.append(d)
        else:
            at = 3 + (i if i < 4 else i - 1)
            rows.append(d * (meta[at : at + 1] * TAPER[i]))
    rows.append(jnp.zeros((ROWS - M - 11, CAP), F32))
    return pack(jnp.concatenate(rows, axis=0)), normed


def init_kernel(order_hbm, value_hbm, variance_hbm, owner_hbm, cell_hbm, reach_hbm, x_hbm, out,
                order, value, variance, owner, cell, reach, surface, sems):
    small = [
        pltpu.make_async_copy(source, target, sems.at[i])
        for i, (source, target) in enumerate([
            (order_hbm, order), (owner_hbm, owner), (cell_hbm, cell),
            (value_hbm, value), (variance_hbm, variance), (reach_hbm, reach),
        ])
    ]
    load = pltpu.make_async_copy(x_hbm.at[:, 0], surface, sems.at[6])
    for copy in small:
        copy.start()
    load.start()
    me = lax.axis_index("gx") * lax.axis_size("gy") + lax.axis_index("gy")
    small[0].wait()
    small[1].wait()
    owned = jnp.concatenate([owner[pl.ds(order[k], 1), :] for k in range(NB)], axis=0) == me
    ownf = jnp.where(owned, 1.0, 0.0)
    chunks = OBS // 128
    own64 = jnp.concatenate([ownf[:, 128 * c : 128 * c + 128] for c in range(chunks)], axis=0).astype(BF16)
    upper = jnp.where(iota((128, 128), 0) < iota((128, 128), 1), 1.0, 0.0).astype(BF16)
    rows = NB * chunks
    r0, r1 = iota((rows, rows), 0), iota((rows, rows), 1)
    before = jnp.where((r1 < r0) & (((r0 - r1) & (NB - 1)) == 0), 1.0, 0.0).astype(BF16)
    base = dot(dot(before, own64).astype(BF16), jnp.ones((128, 128), BF16))
    rank64 = dot(own64, upper) + base
    rank = jnp.concatenate([rank64[NB * c : NB * c + NB] for c in range(chunks)], axis=1)
    rank = jnp.where(owned, rank, -1.0)
    slots = iota((CAP, OBS), 0).astype(F32)
    for copy in small[2:]:
        copy.wait()
    metas = []
    for k in range(NB):
        b = order[k]
        hot = jnp.where(rank[k : k + 1] == slots, 1.0, 0.0).astype(BF16)
        where = cell[pl.ds(b, 1), :]
        vh, vm, vl = split3(value[pl.ds(b, 1), :])
        rh, rm, rl = split3(variance[pl.ds(b, 1), :])
        parts = [
            reach[b].astype(F32),
            lax.shift_right_logical(where, 8).astype(F32),
            (where & 255).astype(F32),
            vh.astype(F32), vm.astype(F32), vl.astype(F32),
            rh.astype(F32), rm.astype(F32), rl.astype(F32),
            jnp.ones((1, OBS), F32),
            jnp.zeros((15, OBS), F32),
        ]
        metas.append(dot_t(jnp.concatenate(parts, axis=0).astype(BF16), hot))
    got = jnp.concatenate(metas, axis=1)
    out[M:] = jnp.concatenate(
        [
            got[16:17],
            got[10:11] + got[11:12] + got[12:13],
            got[13:14] + got[14:15] + got[15:16],
            got[:8],
            jnp.zeros((5, NB * CAP), F32),
        ],
        axis=0,
    )
    hot_y = jnp.where(got[9:10] == iota((TY, NB * CAP), 0).astype(F32), 1.0, 0.0).astype(BF16)
    hot_x = jnp.where(got[8:9] == iota((TX, NB * CAP), 0).astype(F32), 1.0, 0.0)
    load.wait()
    group = 16
    for g in range(M // group):
        high, low = split2(surface[group * g : group * g + group].reshape(group * TX, TY))
        picked = dot(high, hot_y) + dot(low, hot_y)
        out[group * g : group * g + group] = jnp.sum(
            picked.reshape(group, TX, NB * CAP) * hot_x[None], axis=1
        )


def core_of():
    return lax.rem(lax.axis_index("gx"), 2)


def edge(index, count):
    return (index == 0) | (index == count - 1)


def upward(index):
    return lax.rem(index + core_of(), 2) == 0


def emit(k, z, z_out, pay_out, edge_out, news_out=None):
    pays = []
    at = slice(CAP * k, CAP * k + CAP)
    news = []
    for t in range(2):
        pay, normed = make_payload(z[t][:M, at], z[t][M:, at])
        pay_out[t] = pay
        z_out[t, ROW_N : ROW_N + 1, at] = normed
        pays.append(pay)
        news.append(normed)
    edge_out[: ROWS // 2] = jnp.where(upward(lax.axis_index("gx") // 2), pays[1], pays[0])
    if news_out is not None:
        rows = [
            jnp.concatenate([z[t][ROW_N : ROW_N + 1, CAP * i : CAP * i + CAP] for t in range(2)], axis=1) for i in range(k)
        ]
        rows.append(jnp.concatenate(news, axis=1))
        rows.append(jnp.zeros((8 - NB, 2 * CAP), F32))
        block = jnp.concatenate(rows, axis=0)
        edge_out[ROWS // 2 :] = block
        news_out[...] = block


def start_kernel(own, sib, z_out, pay_out, edge_out):
    first = core_of() == 0
    mine, other = own[...], sib[...]
    z = [jnp.where(first, mine, other), jnp.where(first, other, mine)]
    unit = jnp.where(iota((ROWS, 128), 0) == iota((ROWS, 128), 1), 1.0, 0.0)
    unit = jnp.where(iota((ROWS, 128), 0) < M, unit, 0.0)
    for t in range(2):
        z_out[t, :, : NB * CAP] = z[t]
        z_out[t, :, NB * CAP :] = unit
    emit(0, z, z_out, pay_out, edge_out)


def right_side(rows):
    return rows[ROW_A : ROW_A + 1] + rows[ROW_C : ROW_C + 1] * rows[:M]


def factor(rows, dx, dy):
    at = ROW_W + 3 * (dx + 1) + dy + 1
    return rows[at : at + 1]


def toward(rows, dx):
    return jnp.where(upward(lax.axis_index("gy")), factor(rows, dx, 1), factor(rows, dx, -1))


def level(rows, dx):
    return factor(rows, dx, 0)


def inner(pay, weight):
    blocks = [unpack(pay[t]) for t in range(2)]
    right = jnp.concatenate([right_side(b) for b in blocks], axis=1)
    return [
        dot3(right, jnp.concatenate([b[:M] * weight(b, t - i) for i, b in enumerate(blocks)], axis=1), dot_t)
        for t in range(2)
    ]


def outer(far, sib_far, weight):
    y, chips = lax.axis_index("gx") // 2, lax.axis_size("gx") // 2
    up = upward(y)
    first = core_of() == 0
    ends = edge(y, chips)
    far = jnp.where(ends & jnp.logical_not(first), 0.0, far[: ROWS // 2])
    sib_far = jnp.where(ends & first, 0.0, sib_far[: ROWS // 2])
    blocks = [unpack(jnp.where(up, sib_far, far)), unpack(jnp.where(up, far, sib_far))]
    return [dot3(right_side(b), b[:M] * weight(b, dx), dot_t) for b, dx in zip(blocks, (1, -1))]


def own_kernel(k, order, owner, pay, toward_out, level_out, rank_out):
    for t, value in enumerate(inner(pay, toward)):
        toward_out[t] = value
    for t, value in enumerate(inner(pay, level)):
        level_out[t] = value
    row = owner[pl.ds(order[k], 1), :]
    upper = jnp.where(iota((128, 128), 0) < iota((128, 128), 1), 1.0, 0.0).astype(BF16)
    tiles = iota((TILES, 128), 0)
    base = jnp.zeros((TILES, 1), F32)
    for c in range(OBS // 128):
        at = slice(128 * c, 128 * c + 128)
        hot = jnp.where(row[:, at] == tiles, 1.0, 0.0)
        rank = dot(hot.astype(BF16), upper) + base
        rank_out[:, at] = jnp.sum(hot * rank, axis=0, keepdims=True)
        base = base + jnp.sum(hot, axis=1, keepdims=True)


def send_kernel(own, far, sib_far, out):
    for t, value in enumerate(outer(far, sib_far, toward)):
        out[t] = own[t] + value


def same_kernel(own, far, sib_far, out):
    for t, value in enumerate(outer(far, sib_far, level)):
        out[t] = own[t] + value


def column_kernel(news, far, sib_far, across, out):
    first = core_of() == 0
    at = slice(ROWS // 2, ROWS // 2 + NB)
    mine, other = far[at], sib_far[at]
    column = jnp.concatenate(
        [news[:NB], jnp.where(first, mine, other), across[:NB], jnp.where(first, other, mine)], axis=0
    )
    out[...] = jnp.broadcast_to(column[None], out.shape)


def advance(z, gain):
    anomaly = z - jnp.sum(z, axis=0, keepdims=True) / M
    return z + dot3(gain, anomaly)


def whole_gain(t, q0, h, g):
    first = core_of() == 0
    ends = edge(lax.axis_index("gy"), lax.axis_size("gy"))
    return q0[t] + jnp.where(ends & jnp.logical_not(first), 0.0, h[t]) + jnp.where(ends & first, 0.0, g[t])


def step_kernel(k, q0, h, g, z, z_out, pay_out, edge_out, news_out=None):
    new = []
    for t in range(2):
        moved = advance(z[t, :M], whole_gain(t, q0, h, g))
        z_out[t, :M] = moved
        z_out[t, M:] = z[t, M:]
        new.append(jnp.concatenate([moved, z[t, M:]], axis=0))
    emit(k, new, z_out, pay_out, edge_out, news_out)


def part(ref, i, at=0, rows=SLAB):
    return ref.at[:, i // PARTS, pl.ds((i % PARTS) * SLAB + at, rows), :]


def turn(block, out, at):
    high, low = split2(jnp.swapaxes(block, 0, 1))
    out[at : at + 8, :M] = high
    out[at : at + 8, M:] = low


def turn_kernel(first, x, out, come, sems):
    loads = [pltpu.make_async_copy(part(x, first + i), come.at[i], sems.at[i]) for i in range(TURN)]
    for load in loads:
        load.start()
    for i in range(TURN):
        loads[i].wait()
        for j in range(0, SLAB, 8):
            turn(come[i, :, j : j + 8, :], out, SLAB * i + j)


def final_kernel(q0, h, g, z, near, x, out, come, go, come_sems, go_sems):
    loads = [pltpu.make_async_copy(part(x, i), come.at[i - TURN], come_sems.at[i - TURN]) for i in range(TURN, SLABS)]
    stores = []
    for load in loads:
        load.start()
    c = core_of()
    t = advance(z[c, :M, NB * CAP :], whole_gain(c, q0, h, g))[:, :M]
    th, tl = split2(t)
    w = jnp.concatenate([th, th, tl], axis=1)
    for i in (0, *range(TURN, SLABS), *range(1, TURN)):
        if i >= TURN:
            loads[i - TURN].wait()
        for j in range(0, SLAB, 8):
            if i >= TURN:
                turned = jnp.swapaxes(come[i - TURN, :, j : j + 8, :], 0, 1)
            rows = []
            for r in range(8):
                if i >= TURN:
                    xh, xl = split2(turned[r])
                    stack = [xh, xl, xh]
                else:
                    both = near[SLAB * i + j + r]
                    stack = [both, both[:M]]
                rows.append(dot(w, jnp.concatenate(stack, axis=0))[None])
            go[i, :, j : j + 8, :] = jnp.swapaxes(jnp.concatenate(rows, axis=0), 0, 1)
            sem = go_sems.at[(SLAB * i + j) // 8]
            stores.append(pltpu.make_async_copy(go.at[i, :, pl.ds(j, 8), :], part(out, i, j, 8), sem))
            stores[-1].start()
    for store in stores:
        store.wait()


def place_kernel(order, owner, gathered, r0, r1, r2, r3, out):
    y = lax.axis_index("gx") // 2
    tiles = iota((TILES, OBS), 0)
    slots = iota((CAP, OBS), 0).astype(F32)
    rows = gathered.reshape(TILES // 2 * NB, 2 * CAP)
    for k, rank in enumerate((r0, r1, r2, r3)):
        b = order[k]
        tile = owner[pl.ds(b, 1), :]
        place = ((tile >> 4) & 1) * (TILES // 2) + (tile & 15) * 4 + ((tile >> 5) ^ y)
        turned = rows[pl.ds(k, TILES // 2, stride=NB), :].T
        table = jnp.concatenate([turned[:CAP], turned[CAP:]], axis=1)
        if k < NB // 2:
            chunks = [slice(at, at + 128) for at in range(0, OBS, 128)]
            got = jnp.concatenate([
                jnp.take_along_axis(table, jnp.broadcast_to(place[:, at], (CAP, 128)), axis=1) for at in chunks
            ], axis=1)
        else:
            hot = jnp.where(place == tiles, 1.0, 0.0).astype(BF16)
            both = dot(jnp.concatenate(split2(table), axis=0), hot)
            got = both[:CAP] + both[CAP:]
        out[pl.ds(b, 1), :] = jnp.sum(jnp.where(rank[...] == slots, got, 0.0), axis=0, keepdims=True)


VMEM = pl.BlockSpec(memory_space=pltpu.VMEM)
SMEM = pl.BlockSpec(memory_space=pltpu.SMEM)
HBM = pl.BlockSpec(memory_space=pltpu.HBM)


def shape(*dims):
    return jax.ShapeDtypeStruct(dims, F32)


def swaps(pairs):
    return pairs + [(high, low) for low, high in pairs]


def local(ensemble, obs_value, obs_variance, obs_owner, obs_cell, obs_reach, batch_order):
    params = pltpu.CompilerParams(vmem_limit_bytes=32 * 2**20)
    call = functools.partial(pl.pallas_call, compiler_params=params)
    width, height = lax.axis_size("gx"), lax.axis_size("gy")
    both = ("gx", "gy")
    core = swaps([(x, x + 1) for x in range(0, width, 2)])
    chips = width // 2
    side_x = swaps([(2 * y + c, 2 * ((y + 1) % chips) + c) for c in range(2) for y in range(c, chips, 2)])
    side_y = swaps([
        (x * height + k, x * height + k + 1) for x in range(width) for k in range(x % 2, height - 1, 2)
    ] + [(x * height + k, (x + 2) * height + k) for x in range(1, width, 4) for k in (0, height - 1)])
    pay_shapes = (shape(2, ROWS // 2, 128), shape(ROWS // 2, 128))
    z_shape = shape(2, ROWS, NB * CAP + 128)
    row = pltpu.VMEM((NB, OBS), F32)
    row_i = pltpu.VMEM((NB, OBS), jnp.int32)
    own = call(
        init_kernel,
        out_shape=shape(ROWS, NB * CAP),
        in_specs=[HBM] * 7,
        out_specs=VMEM,
        scratch_shapes=[
            pltpu.SMEM((NB,), jnp.int32), row, row, row_i, row_i,
            pltpu.VMEM((NB, 8, OBS), jnp.int32), pltpu.VMEM((M, TX, TY), F32), pltpu.SemaphoreType.DMA((7,)),
        ],
        name="init",
    )(*(
        pltpu.with_memory_space_constraint(value, pltpu.HBM)
        for value in (
            batch_order, obs_value, obs_variance, obs_owner, obs_cell, jnp.swapaxes(obs_reach, 1, 2), ensemble
        )
    ))
    z, pay, edge = call(
        start_kernel,
        out_shape=(z_shape,) + pay_shapes,
        in_specs=[VMEM] * 2,
        out_specs=(VMEM,) * 3,
        name="start",
    )(own, lax.ppermute(own, "gx", core))
    ranks = []
    state_hbm = pltpu.with_memory_space_constraint(ensemble, pltpu.HBM)
    for k in range(NB):
        last = k + 1 == NB
        far = lax.ppermute(edge, "gx", side_x)
        own_toward, own_level, rank = call(
            functools.partial(own_kernel, k),
            out_shape=(shape(2, M, M), shape(2, M, M), shape(1, OBS)),
            in_specs=[SMEM, VMEM, VMEM],
            out_specs=(VMEM,) * 3,
            name="own",
        )(batch_order, obs_owner, pay)
        far, own_toward = lax.optimization_barrier((far, own_toward))
        sib_far = lax.ppermute(far, "gx", core)
        send = call(send_kernel, out_shape=shape(2, M, M), in_specs=[VMEM] * 3, out_specs=VMEM, name="send")(
            own_toward, far, sib_far
        )
        send, sib_far = lax.optimization_barrier((send, sib_far))
        h = lax.ppermute(send, both, side_y)
        q0 = call(same_kernel, out_shape=shape(2, M, M), in_specs=[VMEM] * 3, out_specs=VMEM, name="same")(
            own_level, far, sib_far
        )
        ranks.append(rank)
        if last:
            across = lax.ppermute(sib_far[ROWS // 2 :], "gx", side_x)
            column = call(
                column_kernel, out_shape=pltpu.VMEM((height, 4 * NB, 128), F32), in_specs=[VMEM] * 4, out_specs=VMEM, name="column"
            )(news, far, sib_far, across)
        if last:
            h, q0, column = lax.optimization_barrier((h, q0, column))
            gathered = lax.all_to_all(column, "gy", 0, 0, tiled=True)
        else:
            turned_shape = jax.ShapeDtypeStruct((TURN * SLAB, 2 * M, TY), BF16)
            come = pltpu.VMEM((TURN, M, SLAB, TY), F32)
            if k + 2 < NB:
                h, q0 = lax.optimization_barrier((h, q0))
            else:
                near = call(
                    functools.partial(turn_kernel, 0),
                    out_shape=turned_shape,
                    in_specs=[HBM],
                    out_specs=VMEM,
                    scratch_shapes=[come, pltpu.SemaphoreType.DMA((TURN,))],
                    name="turn",
                )(state_hbm)
                h, q0, near = lax.optimization_barrier((h, q0, near))
        g = lax.ppermute(h, "gx", core)
        if not last:
            tail = k + 2 == NB
            edge_shape = (shape(ROWS // 2 + 8, 128), shape(8, 128)) if tail else pay_shapes[1:]
            z, pay, edge, *rest = call(
                functools.partial(step_kernel, k + 1),
                out_shape=(z_shape, pay_shapes[0]) + edge_shape,
                in_specs=[VMEM] * 4,
                out_specs=(VMEM,) * (4 if tail else 3),
                name="step",
            )(q0, h, g, z)
            if tail:
                news = rest[0]
    dma = lambda n: pltpu.SemaphoreType.DMA((n,))
    state = call(
        final_kernel,
        out_shape=shape(M, LEV, TX, TY),
        in_specs=[VMEM] * 5 + [HBM],
        out_specs=HBM,
        scratch_shapes=[
            pltpu.VMEM((SLABS - TURN, M, SLAB, TY), F32), pltpu.VMEM((SLABS, M, SLAB, TY), F32),
            dma(SLABS - TURN), dma(SLABS * SLAB // 8),
        ],
        cost_estimate=pl.CostEstimate(flops=6 * M * M * LEV * TX * TY, bytes_accessed=8 * M * LEV * TX * TY, transcendentals=0),
        name="final",
    )(q0, h, g, z, near, state_hbm)
    state, gathered = lax.optimization_barrier((state, gathered))
    innovation = call(
        place_kernel,
        out_shape=shape(NB, OBS),
        in_specs=[SMEM] + [VMEM] * 6,
        out_specs=VMEM,
        name="place",
    )(batch_order, obs_owner, gathered, *ranks)
    return state, innovation


def solution(mesh):
    placed = (P(None, None, "gx", "gy"), P(), P(), P(), P(), P(), P())
    return jax.shard_map(
        local,
        mesh=mesh,
        in_specs=placed,
        out_specs=(P(None, None, "gx", "gy"), P()),
        check_vma=False,
    )
```

```python
import functools

import jax
import jax.numpy as jnp
from jax import lax
from jax.experimental import pallas as pl
from jax.experimental.pallas import tpu as pltpu
from jax.sharding import PartitionSpec as P

M = 80
LEV = 4
NB = 4
TX = 32
TY = 256
CAP = 64
OBS = 2048
TILES = 128
EPS = 1e-05
F32 = jnp.float32
BF16 = jnp.bfloat16
SLAB = 16
PARTS = TX // SLAB
SLABS = LEV * PARTS
TURN = 2

ROW_A = M
ROW_C = M + 1
ROW_W = M + 2
ROW_N = M + 11
ROWS = 96
TAPER = (0.25, 0.5, 0.25, 0.5, 1.0, 0.5, 0.25, 0.5, 0.25)


def split2(x):
    high = x.astype(BF16)
    return high, (x - high.astype(F32)).astype(BF16)


def split3(x):
    high = x.astype(BF16)
    rest = x - high.astype(F32)
    mid = rest.astype(BF16)
    return high, mid, (rest - mid.astype(F32)).astype(BF16)


def iota(shape, dim):
    return lax.broadcasted_iota(jnp.int32, shape, dim)


def dot(a, b, **kw):
    return jnp.dot(a, b, preferred_element_type=F32, **kw)


def dot_t(a, b, **kw):
    return lax.dot_general(a, b, (((1,), (1,)), ((), ())), preferred_element_type=F32, **kw)


def dot3(a, b, product=dot):
    ah, al = split2(a)
    bh, bl = split2(b)
    return product(ah, bh) + (product(ah, bl) + product(al, bh))


def pack(rows):
    return jnp.concatenate([rows[: ROWS // 2], rows[ROWS // 2 :]], axis=1)


def unpack(packed):
    return jnp.concatenate([packed[:, :CAP], packed[:, CAP:]], axis=0)


def make_payload(prior, meta):
    valid = meta[0:1] > 0.5
    value = meta[1:2]
    variance = jnp.where(valid, meta[2:3], 1.0)
    center = jnp.sum(prior, axis=0, keepdims=True) / M
    deviation = prior - center
    spread = jnp.sum(deviation * deviation, axis=0, keepdims=True) / (M - 1)
    total = spread + variance
    miss = value - center
    normed = jnp.where(valid, miss / jnp.sqrt(total), 0.0)
    a = spread / total * miss
    c = jnp.sqrt(variance / total) - 1.0
    d = jnp.where(valid, 1.0 / ((M - 1) * (spread + EPS)), 0.0)
    rows = [deviation, a, c]
    for i in range(9):
        if i == 4:
            rows.append(d)
        else:
            at = 3 + (i if i < 4 else i - 1)
            rows.append(d * (meta[at : at + 1] * TAPER[i]))
    rows.append(jnp.zeros((ROWS - M - 11, CAP), F32))
    return pack(jnp.concatenate(rows, axis=0)), normed


def init_kernel(order_hbm, value_hbm, variance_hbm, owner_hbm, cell_hbm, reach_hbm, x_hbm, out,
                order, value, variance, owner, cell, reach, surface, sems):
    small = [
        pltpu.make_async_copy(source, target, sems.at[i])
        for i, (source, target) in enumerate([
            (order_hbm, order), (owner_hbm, owner), (cell_hbm, cell),
            (value_hbm, value), (variance_hbm, variance), (reach_hbm, reach),
        ])
    ]
    load = pltpu.make_async_copy(x_hbm.at[:, 0], surface, sems.at[6])
    for copy in small:
        copy.start()
    load.start()
    me = lax.axis_index("gx") * lax.axis_size("gy") + lax.axis_index("gy")
    small[0].wait()
    small[1].wait()
    owned = jnp.concatenate([owner[pl.ds(order[k], 1), :] for k in range(NB)], axis=0) == me
    ownf = jnp.where(owned, 1.0, 0.0)
    chunks = OBS // 128
    own64 = jnp.concatenate([ownf[:, 128 * c : 128 * c + 128] for c in range(chunks)], axis=0).astype(BF16)
    upper = jnp.where(iota((128, 128), 0) < iota((128, 128), 1), 1.0, 0.0).astype(BF16)
    rows = NB * chunks
    r0, r1 = iota((rows, rows), 0), iota((rows, rows), 1)
    before = jnp.where((r1 < r0) & (((r0 - r1) & (NB - 1)) == 0), 1.0, 0.0).astype(BF16)
    base = dot(dot(before, own64).astype(BF16), jnp.ones((128, 128), BF16))
    rank64 = dot(own64, upper) + base
    rank = jnp.concatenate([rank64[NB * c : NB * c + NB] for c in range(chunks)], axis=1)
    rank = jnp.where(owned, rank, -1.0)
    slots = iota((CAP, OBS), 0).astype(F32)
    for copy in small[2:]:
        copy.wait()
    metas = []
    for k in range(NB):
        b = order[k]
        hot = jnp.where(rank[k : k + 1] == slots, 1.0, 0.0).astype(BF16)
        where = cell[pl.ds(b, 1), :]
        vh, vm, vl = split3(value[pl.ds(b, 1), :])
        rh, rm, rl = split3(variance[pl.ds(b, 1), :])
        parts = [
            reach[b].astype(F32),
            lax.shift_right_logical(where, 8).astype(F32),
            (where & 255).astype(F32),
            vh.astype(F32), vm.astype(F32), vl.astype(F32),
            rh.astype(F32), rm.astype(F32), rl.astype(F32),
            jnp.ones((1, OBS), F32),
            jnp.zeros((15, OBS), F32),
        ]
        metas.append(dot_t(jnp.concatenate(parts, axis=0).astype(BF16), hot))
    got = jnp.concatenate(metas, axis=1)
    out[M:] = jnp.concatenate(
        [
            got[16:17],
            got[10:11] + got[11:12] + got[12:13],
            got[13:14] + got[14:15] + got[15:16],
            got[:8],
            jnp.zeros((5, NB * CAP), F32),
        ],
        axis=0,
    )
    hot_y = jnp.where(got[9:10] == iota((TY, NB * CAP), 0).astype(F32), 1.0, 0.0).astype(BF16)
    hot_x = jnp.where(got[8:9] == iota((TX, NB * CAP), 0).astype(F32), 1.0, 0.0)
    load.wait()
    group = 16
    for g in range(M // group):
        high, low = split2(surface[group * g : group * g + group].reshape(group * TX, TY))
        picked = dot(high, hot_y) + dot(low, hot_y)
        out[group * g : group * g + group] = jnp.sum(
            picked.reshape(group, TX, NB * CAP) * hot_x[None], axis=1
        )


def core_of():
    return lax.rem(lax.axis_index("gx"), 2)


def edge(index, count):
    return (index == 0) | (index == count - 1)


def upward(index):
    return lax.rem(index + core_of(), 2) == 0


def emit(k, z, z_out, pay_out, edge_out, news_out=None):
    pays = []
    at = slice(CAP * k, CAP * k + CAP)
    news = []
    for t in range(2):
        pay, normed = make_payload(z[t][:M, at], z[t][M:, at])
        pay_out[t] = pay
        z_out[t, ROW_N : ROW_N + 1, at] = normed
        pays.append(pay)
        news.append(normed)
    edge_out[: ROWS // 2] = jnp.where(upward(lax.axis_index("gx") // 2), pays[1], pays[0])
    if news_out is not None:
        rows = [
            jnp.concatenate([z[t][ROW_N : ROW_N + 1, CAP * i : CAP * i + CAP] for t in range(2)], axis=1) for i in range(k)
        ]
        rows.append(jnp.concatenate(news, axis=1))
        rows.append(jnp.zeros((8 - NB, 2 * CAP), F32))
        block = jnp.concatenate(rows, axis=0)
        edge_out[ROWS // 2 :] = block
        news_out[...] = block


def start_kernel(own, sib, z_out, pay_out, edge_out):
    first = core_of() == 0
    mine, other = own[...], sib[...]
    z = [jnp.where(first, mine, other), jnp.where(first, other, mine)]
    unit = jnp.where(iota((ROWS, 128), 0) == iota((ROWS, 128), 1), 1.0, 0.0)
    unit = jnp.where(iota((ROWS, 128), 0) < M, unit, 0.0)
    for t in range(2):
        z_out[t, :, : NB * CAP] = z[t]
        z_out[t, :, NB * CAP :] = unit
    emit(0, z, z_out, pay_out, edge_out)


def right_side(rows):
    return rows[ROW_A : ROW_A + 1] + rows[ROW_C : ROW_C + 1] * rows[:M]


def factor(rows, dx, dy):
    at = ROW_W + 3 * (dx + 1) + dy + 1
    return rows[at : at + 1]


def toward(rows, dx):
    return jnp.where(upward(lax.axis_index("gy")), factor(rows, dx, 1), factor(rows, dx, -1))


def level(rows, dx):
    return factor(rows, dx, 0)


def inner(pay, weight):
    blocks = [unpack(pay[t]) for t in range(2)]
    right = jnp.concatenate([right_side(b) for b in blocks], axis=1)
    return [
        dot3(right, jnp.concatenate([b[:M] * weight(b, t - i) for i, b in enumerate(blocks)], axis=1), dot_t)
        for t in range(2)
    ]


def outer(far, sib_far, weight):
    y, chips = lax.axis_index("gx") // 2, lax.axis_size("gx") // 2
    up = upward(y)
    first = core_of() == 0
    ends = edge(y, chips)
    far = jnp.where(ends & jnp.logical_not(first), 0.0, far[: ROWS // 2])
    sib_far = jnp.where(ends & first, 0.0, sib_far[: ROWS // 2])
    blocks = [unpack(jnp.where(up, sib_far, far)), unpack(jnp.where(up, far, sib_far))]
    return [dot3(right_side(b), b[:M] * weight(b, dx), dot_t) for b, dx in zip(blocks, (1, -1))]


def own_kernel(k, order, owner, pay, toward_out, level_out, rank_out):
    for t, value in enumerate(inner(pay, toward)):
        toward_out[t] = value
    for t, value in enumerate(inner(pay, level)):
        level_out[t] = value
    row = owner[pl.ds(order[k], 1), :]
    upper = jnp.where(iota((128, 128), 0) < iota((128, 128), 1), 1.0, 0.0).astype(BF16)
    tiles = iota((TILES, 128), 0)
    base = jnp.zeros((TILES, 1), F32)
    for c in range(OBS // 128):
        at = slice(128 * c, 128 * c + 128)
        hot = jnp.where(row[:, at] == tiles, 1.0, 0.0)
        rank = dot(hot.astype(BF16), upper) + base
        rank_out[:, at] = jnp.sum(hot * rank, axis=0, keepdims=True)
        base = base + jnp.sum(hot, axis=1, keepdims=True)


def send_kernel(own, far, sib_far, out):
    for t, value in enumerate(outer(far, sib_far, toward)):
        out[t] = own[t] + value


def same_kernel(own, far, sib_far, out):
    for t, value in enumerate(outer(far, sib_far, level)):
        out[t] = own[t] + value


def column_kernel(news, far, sib_far, across, out):
    first = core_of() == 0
    at = slice(ROWS // 2, ROWS // 2 + NB)
    mine, other = far[at], sib_far[at]
    column = jnp.concatenate(
        [news[:NB], jnp.where(first, mine, other), across[:NB], jnp.where(first, other, mine)], axis=0
    )
    out[...] = jnp.broadcast_to(column[None], out.shape)


def advance(z, gain):
    anomaly = z - jnp.sum(z, axis=0, keepdims=True) / M
    return z + dot3(gain, anomaly)


def whole_gain(t, q0, h, g):
    first = core_of() == 0
    ends = edge(lax.axis_index("gy"), lax.axis_size("gy"))
    return q0[t] + jnp.where(ends & jnp.logical_not(first), 0.0, h[t]) + jnp.where(ends & first, 0.0, g[t])


def step_kernel(k, q0, h, g, z, z_out, pay_out, edge_out, news_out=None):
    new = []
    for t in range(2):
        moved = advance(z[t, :M], whole_gain(t, q0, h, g))
        z_out[t, :M] = moved
        z_out[t, M:] = z[t, M:]
        new.append(jnp.concatenate([moved, z[t, M:]], axis=0))
    emit(k, new, z_out, pay_out, edge_out, news_out)


def part(ref, i, at=0, rows=SLAB):
    return ref.at[:, i // PARTS, pl.ds((i % PARTS) * SLAB + at, rows), :]


def turn(block, out, at):
    high, low = split2(jnp.swapaxes(block, 0, 1))
    out[at : at + 8, :M] = high
    out[at : at + 8, M:] = low


def turn_kernel(first, x, out, come, sems):
    loads = [pltpu.make_async_copy(part(x, first + i), come.at[i], sems.at[i]) for i in range(TURN)]
    for load in loads:
        load.start()
    for i in range(TURN):
        loads[i].wait()
        for j in range(0, SLAB, 8):
            turn(come[i, :, j : j + 8, :], out, SLAB * i + j)


def final_kernel(q0, h, g, z, near, x, out, come, go, come_sems, go_sems):
    loads = [pltpu.make_async_copy(part(x, i), come.at[i - TURN], come_sems.at[i - TURN]) for i in range(TURN, SLABS)]
    stores = []
    for load in loads:
        load.start()
    c = core_of()
    t = advance(z[c, :M, NB * CAP :], whole_gain(c, q0, h, g))[:, :M]
    th, tl = split2(t)
    w = jnp.concatenate([th, th, tl], axis=1)
    whole = range(0, SLAB, 8)
    for i, halves in ((0, whole[:1]), *((i, whole) for i in range(TURN, SLABS)), (0, whole[1:]), (1, whole)):
        if i >= TURN:
            loads[i - TURN].wait()
        for j in halves:
            if i >= TURN:
                turned = jnp.swapaxes(come[i - TURN, :, j : j + 8, :], 0, 1)
            rows = []
            for r in range(8):
                if i >= TURN:
                    xh, xl = split2(turned[r])
                    stack = [xh, xl, xh]
                else:
                    both = near[SLAB * i + j + r]
                    stack = [both, both[:M]]
                rows.append(dot(w, jnp.concatenate(stack, axis=0))[None])
            go[i, :, j : j + 8, :] = jnp.swapaxes(jnp.concatenate(rows, axis=0), 0, 1)
            sem = go_sems.at[(SLAB * i + j) // 8]
            stores.append(pltpu.make_async_copy(go.at[i, :, pl.ds(j, 8), :], part(out, i, j, 8), sem))
            stores[-1].start()
    for store in stores:
        store.wait()


def place_kernel(order, owner, gathered, r0, r1, r2, r3, out):
    y = lax.axis_index("gx") // 2
    tiles = iota((TILES, OBS), 0)
    slots = iota((CAP, OBS), 0).astype(F32)
    rows = gathered.reshape(TILES // 2 * NB, 2 * CAP)
    for k, rank in enumerate((r0, r1, r2, r3)):
        b = order[k]
        tile = owner[pl.ds(b, 1), :]
        place = ((tile >> 4) & 1) * (TILES // 2) + (tile & 15) * 4 + ((tile >> 5) ^ y)
        turned = rows[pl.ds(k, TILES // 2, stride=NB), :].T
        table = jnp.concatenate([turned[:CAP], turned[CAP:]], axis=1)
        if k < NB // 2:
            chunks = [slice(at, at + 128) for at in range(0, OBS, 128)]
            got = jnp.concatenate([
                jnp.take_along_axis(table, jnp.broadcast_to(place[:, at], (CAP, 128)), axis=1) for at in chunks
            ], axis=1)
        else:
            hot = jnp.where(place == tiles, 1.0, 0.0).astype(BF16)
            both = dot(jnp.concatenate(split2(table), axis=0), hot)
            got = both[:CAP] + both[CAP:]
        out[pl.ds(b, 1), :] = jnp.sum(jnp.where(rank[...] == slots, got, 0.0), axis=0, keepdims=True)


VMEM = pl.BlockSpec(memory_space=pltpu.VMEM)
SMEM = pl.BlockSpec(memory_space=pltpu.SMEM)
HBM = pl.BlockSpec(memory_space=pltpu.HBM)


def shape(*dims):
    return jax.ShapeDtypeStruct(dims, F32)


def swaps(pairs):
    return pairs + [(high, low) for low, high in pairs]


def local(ensemble, obs_value, obs_variance, obs_owner, obs_cell, obs_reach, batch_order):
    params = pltpu.CompilerParams(vmem_limit_bytes=32 * 2**20)
    call = functools.partial(pl.pallas_call, compiler_params=params)
    width, height = lax.axis_size("gx"), lax.axis_size("gy")
    both = ("gx", "gy")
    core = swaps([(x, x + 1) for x in range(0, width, 2)])
    chips = width // 2
    side_x = swaps([(2 * y + c, 2 * ((y + 1) % chips) + c) for c in range(2) for y in range(c, chips, 2)])
    side_y = swaps([
        (x * height + k, x * height + k + 1) for x in range(width) for k in range(x % 2, height - 1, 2)
    ] + [(x * height + k, (x + 2) * height + k) for x in range(1, width, 4) for k in (0, height - 1)])
    pay_shapes = (shape(2, ROWS // 2, 128), shape(ROWS // 2, 128))
    z_shape = shape(2, ROWS, NB * CAP + 128)
    row = pltpu.VMEM((NB, OBS), F32)
    row_i = pltpu.VMEM((NB, OBS), jnp.int32)
    own = call(
        init_kernel,
        out_shape=shape(ROWS, NB * CAP),
        in_specs=[HBM] * 7,
        out_specs=VMEM,
        scratch_shapes=[
            pltpu.SMEM((NB,), jnp.int32), row, row, row_i, row_i,
            pltpu.VMEM((NB, 8, OBS), jnp.int32), pltpu.VMEM((M, TX, TY), F32), pltpu.SemaphoreType.DMA((7,)),
        ],
        name="init",
    )(*(
        pltpu.with_memory_space_constraint(value, pltpu.HBM)
        for value in (
            batch_order, obs_value, obs_variance, obs_owner, obs_cell, jnp.swapaxes(obs_reach, 1, 2), ensemble
        )
    ))
    z, pay, edge = call(
        start_kernel,
        out_shape=(z_shape,) + pay_shapes,
        in_specs=[VMEM] * 2,
        out_specs=(VMEM,) * 3,
        name="start",
    )(own, lax.ppermute(own, "gx", core))
    ranks = []
    state_hbm = pltpu.with_memory_space_constraint(ensemble, pltpu.HBM)
    for k in range(NB):
        last = k + 1 == NB
        far = lax.ppermute(edge, "gx", side_x)
        own_toward, own_level, rank = call(
            functools.partial(own_kernel, k),
            out_shape=(shape(2, M, M), shape(2, M, M), shape(1, OBS)),
            in_specs=[SMEM, VMEM, VMEM],
            out_specs=(VMEM,) * 3,
            name="own",
        )(batch_order, obs_owner, pay)
        far, own_toward = lax.optimization_barrier((far, own_toward))
        sib_far = lax.ppermute(far, "gx", core)
        send = call(send_kernel, out_shape=shape(2, M, M), in_specs=[VMEM] * 3, out_specs=VMEM, name="send")(
            own_toward, far, sib_far
        )
        send, sib_far = lax.optimization_barrier((send, sib_far))
        h = lax.ppermute(send, both, side_y)
        q0 = call(same_kernel, out_shape=shape(2, M, M), in_specs=[VMEM] * 3, out_specs=VMEM, name="same")(
            own_level, far, sib_far
        )
        ranks.append(rank)
        if last:
            across = lax.ppermute(sib_far[ROWS // 2 :], "gx", side_x)
            column = call(
                column_kernel, out_shape=pltpu.VMEM((height, 4 * NB, 128), F32), in_specs=[VMEM] * 4, out_specs=VMEM, name="column"
            )(news, far, sib_far, across)
        if last:
            h, q0, column = lax.optimization_barrier((h, q0, column))
            gathered = lax.all_to_all(column, "gy", 0, 0, tiled=True)
        else:
            turned_shape = jax.ShapeDtypeStruct((TURN * SLAB, 2 * M, TY), BF16)
            come = pltpu.VMEM((TURN, M, SLAB, TY), F32)
            if k + 2 < NB:
                h, q0 = lax.optimization_barrier((h, q0))
            else:
                near = call(
                    functools.partial(turn_kernel, 0),
                    out_shape=turned_shape,
                    in_specs=[HBM],
                    out_specs=VMEM,
                    scratch_shapes=[come, pltpu.SemaphoreType.DMA((TURN,))],
                    name="turn",
                )(state_hbm)
                h, q0, near = lax.optimization_barrier((h, q0, near))
        g = lax.ppermute(h, "gx", core)
        if not last:
            tail = k + 2 == NB
            edge_shape = (shape(ROWS // 2 + 8, 128), shape(8, 128)) if tail else pay_shapes[1:]
            z, pay, edge, *rest = call(
                functools.partial(step_kernel, k + 1),
                out_shape=(z_shape, pay_shapes[0]) + edge_shape,
                in_specs=[VMEM] * 4,
                out_specs=(VMEM,) * (4 if tail else 3),
                name="step",
            )(q0, h, g, z)
            if tail:
                news = rest[0]
    dma = lambda n: pltpu.SemaphoreType.DMA((n,))
    state = call(
        final_kernel,
        out_shape=shape(M, LEV, TX, TY),
        in_specs=[VMEM] * 5 + [HBM],
        out_specs=HBM,
        scratch_shapes=[
            pltpu.VMEM((SLABS - TURN, M, SLAB, TY), F32), pltpu.VMEM((SLABS, M, SLAB, TY), F32),
            dma(SLABS - TURN), dma(SLABS * SLAB // 8),
        ],
        cost_estimate=pl.CostEstimate(flops=6 * M * M * LEV * TX * TY, bytes_accessed=8 * M * LEV * TX * TY, transcendentals=0),
        name="final",
    )(q0, h, g, z, near, state_hbm)
    state, gathered = lax.optimization_barrier((state, gathered))
    innovation = call(
        place_kernel,
        out_shape=shape(NB, OBS),
        in_specs=[SMEM] + [VMEM] * 6,
        out_specs=VMEM,
        name="place",
    )(batch_order, obs_owner, gathered, *ranks)
    return state, innovation


def solution(mesh):
    placed = (P(None, None, "gx", "gy"), P(), P(), P(), P(), P(), P())
    return jax.shard_map(
        local,
        mesh=mesh,
        in_specs=placed,
        out_specs=(P(None, None, "gx", "gy"), P()),
        check_vma=False,
    )
```
